128 devices in a mesh: dp: 16 (over z_lo, x, core), tensor: 8 (over y, z_hi).
Axes of the slice: x: 4, y: 4, z: 4 (z_hi: 2, z_lo: 2; z = z_hi * 2 + z_lo), core: 2. Of those that a mesh axis runs over, the one named last changes fastest.
Arguments:
- block_input: bfloat16 [16, 1024, 1024], P('dp', 'tensor'), may hold values from -6 to 6
- segments: int32 [16, 1024], P('dp'), may hold values from 0 to 4, as said below
- first_gain: float32 [1024], replicated, may hold values from 0.5 to 1.5
- mamba_gate: bfloat16 [1024, 1536], P('dp', 'tensor'), may hold values from -0.1875 to 0.1875
- mamba_input: bfloat16 [1024, 1536], P('dp', 'tensor'), may hold values from -0.1875 to 0.1875
- step_weight: bfloat16 [1024, 24], P('dp', 'tensor'), may hold values from -0.1875 to 0.1875
- state_weight: bfloat16 [1024, 256], P(('dp', 'tensor')), may hold values from -0.1875 to 0.1875
- conv_inner: float32 [4, 1536], P(None, 'tensor'), may hold values from -2.5 to 2.5
- conv_state: float32 [4, 256], replicated, may hold values from -2.5 to 2.5
- decay_log: float32 [24], P('tensor'), may hold values from -5.3 to 1.1
- step_bias: float32 [24], P('tensor'), may hold values from -5 to -3
- skip_scale: float32 [24], P('tensor'), may hold values from 0.5 to 1.5
- query_weight: bfloat16 [1024, 512], P('dp', 'tensor'), may hold values from -0.1875 to 0.1875
- keyval_weight: bfloat16 [1024, 256], P(('dp', 'tensor')), may hold values from -0.1875 to 0.1875
- mamba_out: bfloat16 [1536, 1024], P('tensor', 'dp'), may hold values from -0.15625 to 0.15625
- attention_out: bfloat16 [512, 1024], P('tensor', 'dp'), may hold values from -2 to 2
- second_gain: float32 [1024], replicated, may hold values from 0.5 to 1.5
- feed_gate: bfloat16 [1024, 2048], P('dp', 'tensor'), may hold values from -0.1875 to 0.1875
- feed_up: bfloat16 [1024, 2048], P('dp', 'tensor'), may hold values from -0.1875 to 0.1875
- feed_down: bfloat16 [2048, 1024], P('tensor', 'dp'), may hold values from -0.125 to 0.125
- cotangent: bfloat16 [16, 1024, 1024], P('dp', 'tensor'), may hold values from -6 to 6
Outputs:
- block_output: bfloat16 [16, 1024, 1024], P('dp', 'tensor')
- input_grad: float32 [16, 1024, 1024], P('dp', 'tensor')
- first_gain_grad: float32 [1024], replicated
- mamba_gate_grad: float32 [1024, 1536], P('dp', 'tensor')
- mamba_input_grad: float32 [1024, 1536], P('dp', 'tensor')
- step_weight_grad: float32 [1024, 24], P('dp', 'tensor')
- state_weight_grad: float32 [1024, 256], P(('dp', 'tensor'))
- conv_inner_grad: float32 [4, 1536], P(None, 'tensor')
- conv_state_grad: float32 [4, 256], replicated
- decay_log_grad: float32 [24], P('tensor')
- step_bias_grad: float32 [24], P('tensor')
- skip_scale_grad: float32 [24], P('tensor')
- query_weight_grad: float32 [1024, 512], P('dp', 'tensor')
- keyval_weight_grad: float32 [1024, 256], P(('dp', 'tensor'))
- mamba_out_grad: float32 [1536, 1024], P('tensor', 'dp')
- attention_out_grad: float32 [512, 1024], P('tensor', 'dp')
- second_gain_grad: float32 [1024], replicated
- feed_gate_grad: float32 [1024, 2048], P('dp', 'tensor')
- feed_up_grad: float32 [1024, 2048], P('dp', 'tensor')
- feed_down_grad: float32 [2048, 1024], P('tensor', 'dp')
The draws below stay inside these ranges and needn't reach their ends.
Inputs may be any that keep to these rules, and one draw needn't show every extreme that they name: `segments`: in each row of 1024 positions the numbers start at 0, never fall and rise by one at four places, and segment 2 holds every position from 64 to 959.
All inputs are finite; a program needn't handle non-finite values.
Results may differ from the reference program's by a relative error of at most 0.028.
Values may be sent and summed in bfloat16 or wider, within the bound.
No kernel may reach another device: no remote copies, remote signals or barrier semaphores. Data moves between devices by JAX's collectives and lax.ppermute only.
A program may use at most 192 MiB of HBM per device.

```python
import jax
import jax.numpy as jnp
from jax import lax

D = 1024
MHEADS = 24
STATE = 128
QHEADS = 8
KVHEADS = 2
AHDIM = 64
FF = 2048
CONV = 4
INNER = 1536
LEN = 1024
SSD_BLOCK = 128
ROWS = 16


def draw_segments(key, part):
    key = jax.random.fold_in(key, 23)
    edge_len = LEN // 16
    step_len = edge_len // 2
    key_list = jax.random.split(key, 4)
    head_one = jax.random.randint(key_list[0], (ROWS, 1), 1, step_len + 1)
    head_two = head_one + jax.random.randint(key_list[1], (ROWS, 1), 1, step_len + 1)
    tail_one = LEN - edge_len + jax.random.randint(key_list[2], (ROWS, 1), 1, step_len + 1)
    tail_two = tail_one + jax.random.randint(key_list[3], (ROWS, 1), 1, step_len)
    cut_points = jnp.concatenate([head_one, head_two, tail_one, tail_two], axis=1).astype(jnp.int32)
    positions = jnp.arange(LEN, dtype=jnp.int32)
    return jnp.sum((positions[None, :, None] >= cut_points[:, None, :]).astype(jnp.int32), axis=-1)


def draw_decay_log(key, part):
    key = jax.random.fold_in(key, 11)
    return jax.random.uniform(key, (MHEADS,), jnp.float32, -5.3, 1.1)


def level_of(stream_key, shape, cuts, least, top_value):
    level, own = 1.0, jax.random.fold_in(stream_key, 6)
    for dim, shards_of in cuts:
        steps = jnp.exp(jax.random.uniform(jax.random.fold_in(own, dim), (shards_of,), jnp.float32, least / len(cuts), top_value / len(cuts)))
        level = level * jnp.repeat(steps, shape[dim] // shards_of).reshape([-1 if axis == dim else 1 for axis in range(len(shape))])
    return level


def gaussian(key, shape, spread, most, cuts=(), held_as=jnp.bfloat16):
    factor_of = level_of(key, shape, cuts, -0.22, 0.18) if cuts else 1.0
    drawn = jax.random.normal(key, shape, jnp.float32) * spread * factor_of
    return jnp.minimum(jnp.maximum(drawn, -most), most).astype(held_as)


def setup_inputs(seed: int = 0) -> dict:
    streams_of = jax.random.split(jax.random.key(seed), 22)
    return {
        "block_input": gaussian(streams_of[0], (ROWS, LEN, D), 1.0, 6.0, ((0, 16), (1, 8))),
        "segments": draw_segments(jax.random.fold_in(streams_of[21], 71), 0),
        "first_gain": jnp.clip(1.0 + 0.1 * jax.random.normal(streams_of[2], (D,), jnp.float32), 0.5, 1.5),
        "mamba_gate": gaussian(streams_of[3], (D, INNER), D ** -0.5, 0.1875, ((0, 16), (1, 8))),
        "mamba_input": gaussian(streams_of[4], (D, INNER), D ** -0.5, 0.1875, ((0, 16), (1, 8))),
        "step_weight": gaussian(streams_of[5], (D, MHEADS), D ** -0.5, 0.1875, ((0, 16), (1, 8))),
        "state_weight": gaussian(streams_of[6], (D, 2 * STATE), D ** -0.5, 0.1875, ((0, 128),)),
        "conv_inner": gaussian(streams_of[7], (CONV, INNER), 0.5, 2.5, ((1, 8),), jnp.float32),
        "conv_state": gaussian(streams_of[8], (CONV, 2 * STATE), 0.5, 2.5, (), jnp.float32),
        "decay_log": draw_decay_log(jax.random.fold_in(streams_of[21], 71), 0),
        "step_bias": jnp.clip(-5.0 + 2.0 * jax.random.uniform(streams_of[10], (MHEADS,), jnp.float32) ** level_of(streams_of[10], (MHEADS,), ((0, 8),), -0.2, 0.2), -5.0, -3.0),
        "skip_scale": jnp.clip(0.5 + 1.0 * jax.random.uniform(streams_of[11], (MHEADS,), jnp.float32) ** level_of(streams_of[11], (MHEADS,), ((0, 8),), -0.2, 0.2), 0.5, 1.5),
        "query_weight": gaussian(streams_of[12], (D, QHEADS * AHDIM), D ** -0.5, 0.1875, ((0, 16), (1, 8))),
        "keyval_weight": gaussian(streams_of[13], (D, 2 * KVHEADS * AHDIM), D ** -0.5, 0.1875, ((0, 128),)),
        "mamba_out": gaussian(streams_of[14], (INNER, D), INNER ** -0.5, 0.15625, ((0, 8), (1, 16))),
        "attention_out": gaussian(streams_of[15], (QHEADS * AHDIM, D), (QHEADS * AHDIM // 64) ** -0.5, 2.0, ((0, 8), (1, 16))),
        "second_gain": jnp.clip(1.0 + 0.1 * jax.random.normal(streams_of[16], (D,), jnp.float32), 0.5, 1.5),
        "feed_gate": gaussian(streams_of[17], (D, FF), D ** -0.5, 0.1875, ((0, 16), (1, 8))),
        "feed_up": gaussian(streams_of[18], (D, FF), D ** -0.5, 0.1875, ((0, 16), (1, 8))),
        "feed_down": gaussian(streams_of[19], (FF, D), FF ** -0.5, 0.125, ((0, 8), (1, 16))),
        "cotangent": gaussian(streams_of[20], (ROWS, LEN, D), 1.0, 6.0, ((0, 16), (1, 8))),
    }


PRECISE = lax.Precision.HIGHEST
NORM_EPS = 1e-05
ROPE_BASE = 10000.0
MASKED_SCORE = -1e+30

@jax.custom_vjp
def low(v):
    return lax.optimization_barrier(v.astype(jnp.bfloat16)).astype(jnp.float32)

@jax.custom_vjp
def low_back(v):
    return v

def low_keep(v):
    return (low(v), None)

def low_pass(kept, grad):
    return (grad,)

def back_keep(v):
    return (v, None)

def back_low(kept, grad):
    return (low(grad),)
low.defvjp(low_keep, low_pass)
low_back.defvjp(back_keep, back_low)

def rms_norm(values, scale_vec):
    return values * lax.rsqrt(lax.optimization_barrier(jnp.mean(values * values, axis=-1, keepdims=True)) + NORM_EPS) * scale_vec

def lag_masks(seg_ids, tap_count):
    length = seg_ids.shape[-1]
    mask_list = [jnp.ones(seg_ids.shape, jnp.float32)]
    for lag_step in range(1, tap_count):
        earlier = jnp.concatenate([jnp.full(seg_ids.shape[:-1] + (lag_step,), -1, jnp.int32), seg_ids[..., :length - lag_step]], axis=-1)
        mask_list.append((earlier == seg_ids).astype(jnp.float32))
    return jnp.stack(mask_list)

def conv_silu(values, taps_weight, lag_mask):
    length = values.shape[-2]
    summed = values * taps_weight[0]
    for lag_step in range(1, taps_weight.shape[0]):
        shifted = jnp.concatenate([jnp.zeros_like(values[..., :lag_step, :]), values[..., :length - lag_step, :]], axis=-2)
        summed = summed + shifted * lag_mask[lag_step][..., None] * taps_weight[lag_step]
    return jax.nn.silu(summed)

def ssd_block(carried, blocks):
    states, last_seg = carried
    conv_x, input_map, output_map, step_size, decay_step, seg_ids = blocks
    decay_sum = jnp.cumsum(decay_step, axis=1)
    places = jnp.arange(seg_ids.shape[1])
    same_seg = (seg_ids[:, :, None] == seg_ids[:, None, :]) & (places[:, None] >= places[None, :])
    keep_mask = same_seg[..., None]
    decay_gap = decay_sum[:, :, None, :] - decay_sum[:, None, :, :]
    decay_mask = jnp.where(keep_mask, jnp.exp(jnp.where(keep_mask, decay_gap, 0.0)), 0.0)
    intersections = jnp.einsum('rthn,rshn->rtsh', output_map, input_map, precision=PRECISE)
    mixing = decay_mask * intersections * step_size[:, None, :, :]
    inside = jnp.einsum('rtsh,rshp->rthp', mixing, conv_x, precision=PRECISE)
    reach_in = (seg_ids == last_seg[:, None]).astype(jnp.float32)[..., None] * jnp.exp(decay_sum)
    incoming = jnp.einsum('rthn,rhpn->rthp', output_map, states, precision=PRECISE) * reach_in[..., None]
    end_seg = seg_ids[:, -1]
    to_end = jnp.exp(decay_sum[:, -1:, :] - decay_sum) * (seg_ids == end_seg[:, None]).astype(jnp.float32)[..., None] * step_size
    through = jnp.exp(decay_sum[:, -1, :]) * (end_seg == last_seg).astype(jnp.float32)[:, None]
    updated = states * through[:, :, None, None] + jnp.einsum('rsh,rshp,rshn->rhpn', to_end, conv_x, input_map, precision=PRECISE)
    return ((updated, end_seg), inside + incoming)

def mamba_core(conv_x, state_maps, gate_raw, step_raw, decay_log, step_bias, skip_scale, seg_ids):
    row_count, length, head_count, map_width = state_maps.shape
    state_size = map_width // 2
    head_dim = conv_x.shape[-1] // head_count
    block_count = length // SSD_BLOCK
    step_size = jax.nn.softplus(step_raw + step_bias)
    decay_step = -step_size * jnp.exp(decay_log)

    def split_blocks(values):
        return jnp.moveaxis(values.reshape((row_count, block_count, SSD_BLOCK) + values.shape[2:]), 1, 0)
    blocks = (split_blocks(conv_x.reshape(row_count, length, head_count, head_dim)), split_blocks(state_maps[..., :state_size]), split_blocks(state_maps[..., state_size:]), split_blocks(step_size), split_blocks(decay_step), split_blocks(seg_ids))
    initial = (jnp.zeros((row_count, head_count, head_dim, state_size), jnp.float32), jnp.full((row_count,), -1, jnp.int32))
    final_state, outputs = lax.scan(jax.checkpoint(ssd_block), initial, blocks)
    result = jnp.moveaxis(outputs, 0, 1).reshape(row_count, length, head_count * head_dim)
    result = result + conv_x * jnp.repeat(skip_scale, head_dim)
    return result * jax.nn.silu(gate_raw)

def rope_tables(length, head_dim):
    half_dim = head_dim // 2
    freq_vec = ROPE_BASE ** (-2.0 * jnp.arange(half_dim, dtype=jnp.float32) / head_dim)
    angles = jnp.arange(length, dtype=jnp.float32)[:, None] * freq_vec[None, :]
    angles = jnp.concatenate([angles, angles], axis=-1)
    return (jnp.cos(angles), jnp.sin(angles))

def rotate(values, cosine, sine_tab):
    half_dim = values.shape[-1] // 2
    turned = jnp.concatenate([-values[..., half_dim:], values[..., :half_dim]], axis=-1)
    return values * cosine + turned * sine_tab

def mamba_row(mamba_x, state_proj, gate_raw, step_raw, seg_ids, conv_inner, conv_state, decay_log, step_bias, skip_scale):
    head_count = decay_log.shape[0]
    length = mamba_x.shape[0]
    copies = low_back(jnp.broadcast_to(state_proj[:, None, :], (length, head_count, state_proj.shape[-1])))
    conv_in = jnp.concatenate([mamba_x, copies.reshape(length, -1)], axis=-1)
    taps_weight = jnp.concatenate([conv_inner, jnp.tile(conv_state, (1, head_count))], axis=-1)
    conv_out = low(conv_silu(conv_in, taps_weight, lag_masks(seg_ids, CONV)))
    inner_width = mamba_x.shape[-1]
    state_maps = conv_out[:, inner_width:].reshape(length, head_count, -1)
    return mamba_core(conv_out[None, :, :inner_width], state_maps[None], gate_raw[None], step_raw[None], decay_log, step_bias, skip_scale, seg_ids[None])[0]

def attention_row(query_raw, keyval, seg_ids):
    length = query_raw.shape[0]
    group_size = QHEADS // KVHEADS
    cosine, sine_tab = rope_tables(length, AHDIM)
    cosine = cosine[:, None]
    sine_tab = sine_tab[:, None]
    key_heads = jnp.repeat(keyval[:, :KVHEADS * AHDIM].reshape(length, KVHEADS, AHDIM), group_size, axis=1)
    value_heads = jnp.repeat(keyval[:, KVHEADS * AHDIM:].reshape(length, KVHEADS, AHDIM), group_size, axis=1)
    keys_low = low(rotate(low_back(key_heads), cosine, sine_tab))
    values_low = low(low_back(value_heads))
    queries = low(rotate(query_raw.reshape(length, QHEADS, AHDIM), cosine, sine_tab))
    scores = low_back(jnp.einsum('the,she->hts', queries, keys_low, precision=PRECISE) * AHDIM ** (-0.5))
    places = jnp.arange(length)
    allowed = (seg_ids[:, None] == seg_ids[None, :]) & (places[None, :] <= places[:, None])
    weights = low(jax.nn.softmax(jnp.where(allowed[None], scores, MASKED_SCORE), axis=-1))
    attended = jnp.einsum('hts,she->the', weights, values_low, precision=PRECISE)
    return low(low_back(attended)).reshape(length, QHEADS * AHDIM)

def project(values, weight):
    return jnp.einsum('rld,de->rle', values, weight, precision=PRECISE)

def forward(block_input, first_gain, mamba_gate, mamba_input, step_weight, state_weight, conv_inner, conv_state, decay_log, step_bias, skip_scale, query_weight, keyval_weight, mamba_out, attention_out, second_gain, feed_gate, feed_up, feed_down, segments):
    normed = low(rms_norm(block_input, first_gain))
    gate_raw = low_back(project(normed, mamba_gate))
    mamba_x = low_back(project(normed, mamba_input))
    step_raw = low_back(project(normed, step_weight))
    state_proj = project(normed, state_weight)
    query_raw = low_back(project(normed, query_weight))
    keyval = project(normed, keyval_weight)

    def mamba_one(row_args):
        return mamba_row(row_args[0], row_args[1], row_args[2], row_args[3], row_args[4], conv_inner, conv_state, decay_log, step_bias, skip_scale)

    def attend_one(row_args):
        return attention_row(row_args[0], row_args[1], row_args[2])
    gated_out = low(lax.map(jax.checkpoint(mamba_one), (mamba_x, state_proj, gate_raw, step_raw, segments)))
    attended = lax.map(jax.checkpoint(attend_one), (query_raw, keyval, segments))
    mixed = low_back(project(gated_out, mamba_out) + project(attended, attention_out))
    hidden = block_input + mixed
    normed_two = low(rms_norm(hidden, second_gain))
    gate_proj = low_back(project(normed_two, feed_gate))
    up_proj = low_back(project(normed_two, feed_up))
    activation = low(jax.nn.silu(gate_proj) * up_proj)
    return hidden + low_back(project(activation, feed_down))

def reference(block_input, segments, first_gain, mamba_gate, mamba_input, step_weight, state_weight, conv_inner, conv_state, decay_log, step_bias, skip_scale, query_weight, keyval_weight, mamba_out, attention_out, second_gain, feed_gate, feed_up, feed_down, cotangent):
    primals = (block_input.astype(jnp.float32), first_gain.astype(jnp.float32), mamba_gate.astype(jnp.float32), mamba_input.astype(jnp.float32), step_weight.astype(jnp.float32), state_weight.astype(jnp.float32), conv_inner.astype(jnp.float32), conv_state.astype(jnp.float32), decay_log.astype(jnp.float32), step_bias.astype(jnp.float32), skip_scale.astype(jnp.float32), query_weight.astype(jnp.float32), keyval_weight.astype(jnp.float32), mamba_out.astype(jnp.float32), attention_out.astype(jnp.float32), second_gain.astype(jnp.float32), feed_gate.astype(jnp.float32), feed_up.astype(jnp.float32), feed_down.astype(jnp.float32))

    def closed(*values_in):
        return forward(*values_in, segments)
    output, pullback = jax.vjp(closed, *primals)
    gradients = pullback(cotangent.astype(jnp.float32))
    return (output.astype(jnp.bfloat16), gradients[0], gradients[1], gradients[2], gradients[3], gradients[4], gradients[5], gradients[6], gradients[7], gradients[8], gradients[9], gradients[10], gradients[11], gradients[12], gradients[13], gradients[14], gradients[15], gradients[16], gradients[17], gradients[18])
```

```python
import jax
import jax.numpy as jnp
from jax import lax
from jax.experimental import pallas as pl
from jax.experimental.pallas import tpu as pltpu
from jax.sharding import PartitionSpec as P

QHEADS = 8
KVHEADS = 2
AHDIM = 64
TOKENS = 1024
WIDTH = 1024
BLOCK = 128
BLOCKS = TOKENS // BLOCK
HEADS = 3
HDIM = 64
INNER = HEADS * HDIM
FEED = 256
QUERY_BLOCK = 256
NORM_EPS = 1e-05
ROPE_BASE = 10000.0
MASKED = -1e30
VMEM_BYTES = 60 * 1024 * 1024

CONV_END = 512
GATE_AT = 512
QK_AT = 768
SV_AT = 896
PACKED = 1024

F32 = jnp.float32
BF16 = jnp.bfloat16


def dot(a, b):
    return lax.dot_general(a, b, (((1,), (0,)), ((), ())), preferred_element_type=F32)


def dot_right(a, b):
    return lax.dot_general(a, b, (((1,), (1,)), ((), ())), preferred_element_type=F32)


def dot_left(a, b):
    return lax.dot_general(a, b, (((0,), (0,)), ((), ())), preferred_element_type=F32)


def parts_of(values, terms):
    parts = []
    for _ in range(terms - 1):
        part = values.astype(BF16)
        parts.append(part)
        values = values - part.astype(F32)
    parts.append(values.astype(BF16))
    return parts


def times_ones(values, ones, terms=2):
    return sum(dot(part, ones) for part in parts_of(values, terms))


def ones_times(ones, values, terms=2):
    return sum(dot(ones, part) for part in parts_of(values, terms))


def iota(shape, dim):
    return lax.broadcasted_iota(jnp.int32, shape, dim)


def softplus(v):
    return jnp.maximum(v, 0.0) + jnp.log1p(jnp.exp(-jnp.abs(v)))


def sigmoid(v):
    return 1.0 / (1.0 + jnp.exp(-v))


def head_matrices():
    lane, channel = (iota((BLOCK, 256), 0), iota((BLOCK, 256), 1))
    spread = ((channel >> 6) == lane) & (channel < INNER)
    lane, channel = (iota((256, BLOCK), 1), iota((256, BLOCK), 0))
    gather = ((channel >> 6) == lane) & (channel < INNER)
    return (spread.astype(BF16), gather.astype(BF16))


def per_head(values):
    of_head = iota(values.shape, 1) >> 6
    return jnp.concatenate(
        [jnp.where(of_head == h, values, jnp.zeros_like(values)) for h in range(HEADS)], axis=0
    )


def conv_parts(proj_ref, taps_ref, aux, start):
    here = proj_ref[pl.ds(start, BLOCK), 0:CONV_END]
    before = proj_ref[pl.ds(pl.multiple_of(jnp.maximum(start - 8, 0), 8), 8), 0:CONV_END]
    both = jnp.concatenate([before, here], axis=0)
    lagged = [here]
    for lag in range(1, 4):
        lagged.append(both[8 - lag : 8 - lag + BLOCK] * aux[:, lag : lag + 1])
    pre = sum(lagged[lag] * taps_ref[lag : lag + 1, :] for lag in range(4))
    return (lagged, pre)


def step_parts(proj_ref, par_ref, aux, lower, start):
    raw = proj_ref[pl.ds(start, BLOCK), SV_AT:PACKED] + par_ref[0:1, 0:128]
    is_head = iota((BLOCK, 128), 1) < HEADS
    step = jnp.where(is_head, softplus(raw), 0.0)
    rate = -step * jnp.exp(par_ref[1:2, 0:128])
    total = ones_times(lower, rate, 3)
    reach = aux[:, 4:5] * jnp.exp(total)
    to_end = aux[:, 5:6] * jnp.exp(total[BLOCK - 1 : BLOCK, :] - total)
    return (raw, is_head, step, rate, total, reach, to_end)


def decay_of(total, total_rows, keep, h):
    gap = total[:, h : h + 1] - total_rows[h : h + 1, :]
    return jnp.exp(jnp.where(keep, gap, MASKED))


def turn_halves(values, rope, back):
    up = pltpu.roll(values, 96, 1) * rope[:, 128:256]
    down = pltpu.roll(values, 32, 1) * rope[:, 256:384]
    here = values * rope[:, 0:128]
    return here - up - down if back else here + up + down


def allowed_keys(aux_ref, segrow_ref, first, count):
    query_seg = aux_ref[first : first + QUERY_BLOCK, 0:1]
    key_seg = segrow_ref[0:1, 0:count]
    shape = (QUERY_BLOCK, count)
    return (query_seg == key_seg) & (iota(shape, 1) <= iota(shape, 0) + first)


def mixer_forward_kernel(
    normed_ref,
    w1_ref,
    w2_ref,
    aux_ref,
    segrow_ref,
    par_ref,
    taps_ref,
    rope_ref,
    mix_ref,
    proj_ref,
    states_ref,
    qkv_ref,
    lse_ref,
    heads_ref,
):
    for first in range(0, TOKENS, 256):
        rows = slice(first, first + 256)
        proj_ref[rows, :] = dot(normed_ref[rows, :], w1_ref[...])
    lane = iota((256, 128), 1)
    for first in range(0, TOKENS, 256):
        rows = slice(first, first + 256)
        turned = turn_halves(proj_ref[rows, QK_AT:SV_AT], rope_ref[rows, :], False)
        qkv_ref[rows, 0:128] = jnp.where(lane < 64, turned * AHDIM**-0.5, 0.0).astype(BF16)
        qkv_ref[rows, 128:256] = jnp.where(lane < 64, pltpu.roll(turned, 64, 1), 0.0).astype(BF16)
        tail = proj_ref[rows, SV_AT:PACKED]
        ones = jnp.where(lane == 0, 1.0, 0.0)
        qkv_ref[rows, 256:384] = jnp.where(lane >= 64, tail, ones).astype(BF16)
    for first in range(0, TOKENS, QUERY_BLOCK):
        rows = slice(first, first + QUERY_BLOCK)
        count = first + QUERY_BLOCK
        scores = dot_right(qkv_ref[rows, 0:128], qkv_ref[0:count, 128:256])
        scores = jnp.where(allowed_keys(aux_ref, segrow_ref, first, count), scores, MASKED)
        top = jnp.max(scores, axis=1, keepdims=True)
        raised = jnp.exp(scores - top)
        summed = dot(raised.astype(BF16), qkv_ref[0:count, 256:384])
        total = summed[:, 0:1]
        heads_ref[rows, 128:256] = jnp.where(lane >= 64, summed / total, 0.0).astype(BF16)
        lse_ref[rows, :] = jnp.broadcast_to(top + jnp.log(total), (QUERY_BLOCK, 128))

    spread, _ = head_matrices()
    causal = iota((BLOCK, BLOCK), 0) >= iota((BLOCK, BLOCK), 1)
    lower = causal.astype(BF16)

    def block_step(index, state):
        start = pl.multiple_of(index * BLOCK, BLOCK)
        rows = pl.ds(start, BLOCK)
        aux = aux_ref[rows, :]
        _, pre = conv_parts(proj_ref, taps_ref, aux, start)
        conv = (pre * sigmoid(pre)).astype(BF16)
        in_map, out_map, inner = (conv[:, 0:128], conv[:, 128:256], conv[:, 256:512].astype(F32))
        _, _, step, _, total, reach, to_end = step_parts(proj_ref, par_ref, aux, lower, start)
        wide = times_ones(jnp.concatenate([step, reach, to_end], axis=0), spread)
        step_wide, reach_wide, end_wide = (wide[0:128], wide[128:256], wide[256:384])
        stepped = inner * step_wide
        keep = causal & (aux[:, 0:1] == segrow_ref[0:1, pl.ds(start, BLOCK)])
        total_rows = jnp.transpose(total)
        shared = dot_right(out_map, in_map)
        mixing = jnp.concatenate(
            [(decay_of(total, total_rows, keep, h) * shared).astype(BF16) for h in range(HEADS)],
            axis=1,
        )
        states_ref[rows, :] = state
        result = dot(mixing, per_head(stepped).astype(BF16))
        result = result + dot(out_map, state.astype(BF16)) * reach_wide
        result = result + inner * par_ref[2:3, :]
        gate = proj_ref[rows, GATE_AT:QK_AT]
        gated = (result * (gate * sigmoid(gate))).astype(BF16)
        heads_ref[rows, 0:128] = gated[:, 0:128]
        heads_ref[rows, 128:256] = heads_ref[rows, 128:256] + gated[:, 128:256]
        added = dot_left(in_map, (stepped * end_wide).astype(BF16))
        return state * reach_wide[BLOCK - 1 : BLOCK, :] + added

    lax.fori_loop(0, BLOCKS, block_step, jnp.zeros((BLOCK, 256), F32))
    for first in range(0, TOKENS, 256):
        rows = slice(first, first + 256)
        mix_ref[rows, :] = dot_right(heads_ref[rows, :], w2_ref[...]).astype(BF16)


def mixer_backward_kernel(
    mixgrad_ref,
    w2_ref,
    w1_ref,
    normed_ref,
    aux_ref,
    segrow_ref,
    par_ref,
    taps_ref,
    rope_ref,
    proj_ref,
    states_ref,
    qkv_ref,
    lse_ref,
    dproj_ref,
    ngrad_ref,
    small_ref,
    gain_ref,
    d_ref,
    dkv_ref,
):
    for first in range(0, TOKENS, 256):
        rows = slice(first, first + 256)
        d_ref[rows, :] = dot(mixgrad_ref[rows, :], w2_ref[...])
    lane = iota((QUERY_BLOCK, 128), 1)
    dkv_ref[...] = jnp.zeros_like(dkv_ref)
    for first in range(0, TOKENS, QUERY_BLOCK):
        rows = slice(first, first + QUERY_BLOCK)
        count = first + QUERY_BLOCK
        queries, keys = (qkv_ref[rows, 0:128], qkv_ref[0:count, 128:256])
        out_grad = jnp.where(lane >= 64, d_ref[rows, 128:256], 0.0).astype(BF16)
        scores = dot_right(queries, keys) - lse_ref[rows, 0:1]
        weights = jnp.exp(
            jnp.where(allowed_keys(aux_ref, segrow_ref, first, count), scores, MASKED)
        )
        weight_grad = dot_right(out_grad, qkv_ref[0:count, 256:384])
        mean = jnp.sum(weights * weight_grad, axis=1, keepdims=True)
        score_grad = (weights * (weight_grad - mean)).astype(BF16)
        query_grad = dot(score_grad, keys) * AHDIM**-0.5
        d_ref[rows, 128:256] = jnp.where(
            lane < 64, d_ref[rows, 128:256], pltpu.roll(query_grad, 64, 1)
        )
        dkv_ref[0:count, 0:128] += dot_left(score_grad, queries)
        dkv_ref[0:count, 128:256] += dot_left(weights.astype(BF16), out_grad)
    for first in range(0, TOKENS, 256):
        rows = slice(first, first + 256)
        query_grad = pltpu.roll(d_ref[rows, 128:256], 64, 1)
        both = jnp.where(lane < 64, query_grad, pltpu.roll(dkv_ref[rows, 0:128], 64, 1))
        dproj_ref[rows, QK_AT:SV_AT] = turn_halves(both, rope_ref[rows, :], True).astype(BF16)
        dproj_ref[rows, SV_AT:PACKED] = jnp.where(lane >= 64, dkv_ref[rows, 128:256], 0.0).astype(
            BF16
        )

    spread, gather = head_matrices()
    row, column = (iota((BLOCK, BLOCK), 0), iota((BLOCK, BLOCK), 1))
    causal = row >= column
    lower = causal.astype(BF16)
    upper = (row <= column).astype(BF16)
    strict = (row > column).astype(BF16)
    real = iota((BLOCK, 256), 1) < INNER
    head_lane = iota((BLOCK, 128), 1)

    def block_step(turn, carried):
        state_grad, later, taps_sum, head_sum, skip_sum = carried
        start = pl.multiple_of((BLOCKS - 1 - turn) * BLOCK, BLOCK)
        rows = pl.ds(start, BLOCK)
        aux = aux_ref[rows, :]
        lagged, pre = conv_parts(proj_ref, taps_ref, aux, start)
        sig = sigmoid(pre)
        conv = (pre * sig).astype(BF16)
        in_map, out_map, inner = (conv[:, 0:128], conv[:, 128:256], conv[:, 256:512].astype(F32))
        raw, is_head, step, rate, total, reach, to_end = step_parts(
            proj_ref, par_ref, aux, lower, start
        )
        wide = times_ones(jnp.concatenate([step, reach, to_end], axis=0), spread)
        step_wide, reach_wide, end_wide = (wide[0:128], wide[128:256], wide[256:384])
        stepped = inner * step_wide
        stepped_low = stepped.astype(BF16)
        keep = causal & (aux[:, 0:1] == segrow_ref[0:1, pl.ds(start, BLOCK)])
        total_rows = jnp.transpose(total)
        shared = dot_right(out_map, in_map)
        decays = [decay_of(total, total_rows, keep, h) for h in range(HEADS)]
        mixing = [(decay * shared).astype(BF16) for decay in decays]
        state = states_ref[rows, :]
        state_low = state.astype(BF16)
        incoming = dot(out_map, state_low) * reach_wide
        result = dot(jnp.concatenate(mixing, axis=1), per_head(stepped).astype(BF16)) + incoming
        result = result + inner * par_ref[2:3, :]

        gate = proj_ref[rows, GATE_AT:QK_AT]
        gate_sig = sigmoid(gate)
        gated_grad = jnp.where(real, d_ref[rows, :], 0.0)
        gate_grad = gated_grad * result * (gate_sig * (1.0 + gate * (1.0 - gate_sig)))
        dproj_ref[rows, GATE_AT:QK_AT] = gate_grad.astype(BF16)
        out_grad = gated_grad * (gate * gate_sig)
        by_head = per_head(out_grad).astype(BF16)

        mixing_grad = dot_right(by_head, stepped_low)
        shared_grad = jnp.zeros((BLOCK, BLOCK), F32)
        edges = []
        for h in range(HEADS):
            decayed = mixing_grad[h * BLOCK : (h + 1) * BLOCK] * decays[h]
            shared_grad = shared_grad + decayed
            edges.append((decayed * shared).astype(BF16))
        crossing = dot(upper, jnp.concatenate(edges, axis=1))
        rate_grad = jnp.zeros((BLOCK, 128), F32)
        for h in range(HEADS):
            part = jnp.where(row > column, crossing[:, h * BLOCK : (h + 1) * BLOCK], 0.0)
            part = jnp.sum(part, axis=1, keepdims=True)
            rate_grad = rate_grad + jnp.where(head_lane == h, part, 0.0)

        reached = (out_grad * reach_wide).astype(BF16)
        state_grad_low = state_grad.astype(BF16)
        ended = dot(in_map, state_grad_low) * end_wide
        mapped = dot_left(jnp.concatenate(mixing, axis=0), by_head) + ended
        inner_grad = mapped * step_wide + out_grad * par_ref[2:3, :]
        kept = jnp.sum(state_grad * state, axis=0, keepdims=True)
        kept = jnp.broadcast_to(kept * reach_wide[BLOCK - 1 : BLOCK, :], (8, 256))
        sums = times_ones(
            jnp.concatenate([inner * mapped, out_grad * incoming, stepped * ended, kept], axis=0),
            gather,
        )
        flows = ones_times(
            jnp.concatenate([upper, strict], axis=1), sums[128:384]
        )
        rate_grad = rate_grad + flows + sums[384:385]
        step_grad = sums[0:128] - jnp.exp(par_ref[1:2, 0:128]) * rate_grad
        step_grad = jnp.where(is_head, step_grad * sigmoid(raw), 0.0)
        dproj_ref[rows, SV_AT:PACKED] = dproj_ref[rows, SV_AT:PACKED] + step_grad.astype(BF16)
        head_sum = head_sum + jnp.concatenate(
            [
                jnp.sum(jnp.where(is_head, rate_grad * rate, 0.0), axis=0, keepdims=True),
                jnp.sum(step_grad, axis=0, keepdims=True),
                jnp.zeros((6, 128), F32),
            ],
            axis=0,
        )
        skip_sum = skip_sum + jnp.sum(inner * out_grad, axis=0, keepdims=True)

        shared_low = shared_grad.astype(BF16)
        out_map_grad = dot(shared_low, in_map) + dot_right(reached, state_low)
        in_map_grad = dot_left(shared_low, out_map) + dot_right(
            (stepped * end_wide).astype(BF16), state_grad_low
        )
        conv_grad = jnp.concatenate([in_map_grad, out_map_grad, inner_grad], axis=1)
        pre_grad = conv_grad * (sig * (1.0 + pre * (1.0 - sig)))
        taps_sum = taps_sum + jnp.concatenate(
            [jnp.sum(pre_grad * lagged[lag], axis=0, keepdims=True) for lag in range(4)]
            + [jnp.zeros((4, CONV_END), F32)],
            axis=0,
        )
        both = jnp.concatenate([pre_grad, later], axis=0)
        masks = aux_ref[pl.ds(start, BLOCK + 8), :]
        u_grad = pre_grad * taps_ref[0:1, :]
        for lag in range(1, 4):
            shifted = (both * masks[:, lag : lag + 1])[lag : lag + BLOCK]
            u_grad = u_grad + shifted * taps_ref[lag : lag + 1, :]
        dproj_ref[rows, 0:CONV_END] = u_grad.astype(BF16)
        state_grad = state_grad * reach_wide[BLOCK - 1 : BLOCK, :] + dot_left(out_map, reached)
        return (state_grad, pre_grad[0:8], taps_sum, head_sum, skip_sum)

    carried = (
        jnp.zeros((BLOCK, 256), F32),
        jnp.zeros((8, CONV_END), F32),
        jnp.zeros((8, CONV_END), F32),
        jnp.zeros((8, 128), F32),
        jnp.zeros((1, 256), F32),
    )
    _, _, taps_sum, head_sum, skip_sum = lax.fori_loop(0, BLOCKS, block_step, carried)
    small_ref[0:8, :] = taps_sum
    small_ref[8:16, 0:128] = head_sum
    small_ref[8:16, 128:256] = jnp.zeros((8, 128), F32)
    small_ref[8:16, 256:512] = jnp.broadcast_to(skip_sum, (8, 256))

    gain = jnp.zeros((1, WIDTH), F32)
    for first in range(0, TOKENS, 256):
        rows = slice(first, first + 256)
        grad = dot_right(dproj_ref[rows, :], w1_ref[...])
        ngrad_ref[rows, :] = grad.astype(BF16)
        gain = gain + jnp.sum(grad * normed_ref[rows, :].astype(F32), axis=0, keepdims=True)
    gain_ref[...] = jnp.broadcast_to(gain, (8, WIDTH))


def feed_kernel(
    normed_ref, cot_ref, w_ref, out_ref, ngrad_ref, act_ref, grads_ref, gain_ref
):
    both = dot(normed_ref[...], w_ref[:, 256:768])
    gate, up = (both[:, 0:FEED], both[:, FEED:])
    sig = sigmoid(gate)
    silu = gate * sig
    act = (silu * up).astype(BF16)
    act_ref[...] = act
    out_ref[...] = dot_right(act, w_ref[:, 768:1024]).astype(BF16)
    act_grad = dot(cot_ref[...], w_ref[:, 768:1024])
    gate_grad = (act_grad * up * (sig + silu * (1.0 - sig))).astype(BF16)
    up_grad = (act_grad * silu).astype(BF16)
    grads = jnp.concatenate([gate_grad, up_grad], axis=1)
    grads_ref[...] = grads
    normed_grad = dot_right(grads, w_ref[:, 256:768])
    ngrad_ref[...] = normed_grad.astype(BF16)
    gain = jnp.sum(normed_grad * normed_ref[...].astype(F32), axis=0, keepdims=True)

    @pl.when(pl.program_id(0) == 0)
    def _():
        gain_ref[...] = jnp.zeros_like(gain_ref)

    gain_ref[...] += jnp.broadcast_to(gain, (8, WIDTH))


def shape_of(rows, columns, dtype):
    return jax.ShapeDtypeStruct((rows, columns), dtype)


def whole(rows, columns):
    return pl.BlockSpec((rows, columns), lambda i: (0, 0))


def mixer_forward(normed, w1, w2, aux, segrow, par, taps, rope):
    return pl.pallas_call(
        mixer_forward_kernel,
        grid=(1,),
        in_specs=[
            whole(TOKENS, WIDTH),
            whole(WIDTH, PACKED),
            whole(WIDTH, 256),
            whole(TOKENS + 8, 128),
            whole(8, TOKENS),
            whole(8, 256),
            whole(8, CONV_END),
            whole(TOKENS, 384),
        ],
        out_specs=[
            whole(TOKENS, WIDTH),
            whole(TOKENS, PACKED),
            whole(TOKENS, 256),
            whole(TOKENS, 384),
            whole(TOKENS, 128),
            whole(TOKENS, 256),
        ],
        out_shape=[
            shape_of(TOKENS, WIDTH, BF16),
            shape_of(TOKENS, PACKED, F32),
            shape_of(TOKENS, 256, F32),
            shape_of(TOKENS, 384, BF16),
            shape_of(TOKENS, 128, F32),
            shape_of(TOKENS, 256, BF16),
        ],
        compiler_params=pltpu.CompilerParams(vmem_limit_bytes=VMEM_BYTES),
        name="mixer_forward",
    )(normed, w1, w2, aux, segrow, par, taps, rope)


def mixer_backward(
    mixgrad, w2, w1, normed, aux, segrow, par, taps, rope, proj, states, qkv, lse
):
    return pl.pallas_call(
        mixer_backward_kernel,
        grid=(1,),
        in_specs=[
            whole(TOKENS, WIDTH),
            whole(WIDTH, 256),
            whole(WIDTH, PACKED),
            whole(TOKENS, WIDTH),
            whole(TOKENS + 8, 128),
            whole(8, TOKENS),
            whole(8, 256),
            whole(8, CONV_END),
            whole(TOKENS, 384),
            whole(TOKENS, PACKED),
            whole(TOKENS, 256),
            whole(TOKENS, 384),
            whole(TOKENS, 128),
        ],
        out_specs=[
            whole(TOKENS, PACKED),
            whole(TOKENS, WIDTH),
            whole(16, CONV_END),
            whole(8, WIDTH),
        ],
        out_shape=[
            shape_of(TOKENS, PACKED, BF16),
            shape_of(TOKENS, WIDTH, BF16),
            shape_of(16, CONV_END, F32),
            shape_of(8, WIDTH, F32),
        ],
        scratch_shapes=[pltpu.VMEM((TOKENS, 256), F32), pltpu.VMEM((TOKENS, 256), F32)],
        compiler_params=pltpu.CompilerParams(vmem_limit_bytes=VMEM_BYTES),
        name="mixer_backward",
    )(mixgrad, w2, w1, normed, aux, segrow, par, taps, rope, proj, states, qkv, lse)


def feed_forward_backward(normed, cot, w2):
    def rows(columns):
        return pl.BlockSpec((256, columns), lambda i: (i, 0))

    return pl.pallas_call(
        feed_kernel,
        grid=(TOKENS // 256,),
        in_specs=[rows(WIDTH), rows(WIDTH), whole(WIDTH, 1024)],
        out_specs=[rows(WIDTH), rows(WIDTH), rows(FEED), rows(2 * FEED), whole(8, WIDTH)],
        out_shape=[
            shape_of(TOKENS, WIDTH, BF16),
            shape_of(TOKENS, WIDTH, BF16),
            shape_of(TOKENS, FEED, BF16),
            shape_of(TOKENS, 2 * FEED, BF16),
            shape_of(8, WIDTH, F32),
        ],
        compiler_params=pltpu.CompilerParams(vmem_limit_bytes=VMEM_BYTES),
        name="feed",
    )(normed, cot, w2)


def aux_arrays(segments):
    seg = segments.reshape(TOKENS)
    columns = [seg.astype(F32)]
    for lag in range(1, 4):
        earlier = jnp.concatenate([jnp.full((lag,), -1, jnp.int32), seg[: TOKENS - lag]])
        columns.append((earlier == seg).astype(F32))
    ends = seg.reshape(BLOCKS, BLOCK)[:, -1]
    before = jnp.concatenate([jnp.full((1,), -1, jnp.int32), ends[:-1]])
    columns.append((seg == jnp.repeat(before, BLOCK)).astype(F32))
    columns.append((seg == jnp.repeat(ends, BLOCK)).astype(F32))
    aux = jnp.pad(jnp.stack(columns, axis=1), ((0, 8), (0, 128 - len(columns))))
    return (aux, jnp.broadcast_to(seg.astype(F32), (8, TOKENS)))


def rope_arrays():
    half = AHDIM // 2
    freq = ROPE_BASE ** (-2.0 * jnp.arange(half, dtype=F32) / AHDIM)
    angles = jnp.arange(TOKENS, dtype=F32)[:, None] * freq[None, :]
    cosine, sine = (jnp.cos(angles), jnp.sin(angles))
    none = jnp.zeros_like(sine)
    return jnp.concatenate([cosine] * 4 + [-sine, none] * 2 + [none, sine] * 2, axis=1)


def pad_columns(values, width):
    return jnp.pad(values, ((0, 0), (0, width - values.shape[1])))


def row_norm(values):
    return lax.rsqrt(jnp.mean(values * values, axis=-1, keepdims=True) + NORM_EPS)


def norm_back(values, gain, grad):
    scale = row_norm(values)
    scaled = grad * gain
    return scale * scaled - values * (
        scale**3 * jnp.mean(scaled * values, axis=-1, keepdims=True)
    )


def spread_rows(shard, axis):
    copies = jnp.broadcast_to(shard, (lax.axis_size(axis), *shard.shape))
    blocks = lax.all_to_all(copies, axis, split_axis=0, concat_axis=0, tiled=True)
    return blocks.reshape(-1, *shard.shape[1:])


def sum_rows(values, axis):
    size = lax.axis_size(axis)
    blocks = values.reshape(size, -1, values.shape[-1])
    blocks = lax.all_to_all(blocks, axis, split_axis=0, concat_axis=0, tiled=True)
    return jnp.sum(blocks.astype(F32), axis=0)


def body(
    block_input,
    segments,
    first_gain,
    mamba_gate,
    mamba_input,
    step_weight,
    state_weight,
    conv_inner,
    conv_state,
    decay_log,
    step_bias,
    skip_scale,
    query_weight,
    keyval_weight,
    mamba_out,
    attention_out,
    second_gain,
    feed_gate,
    feed_up,
    feed_down,
    cotangent,
):
    tensor_index = lax.axis_index("tensor")
    kv_head = tensor_index // (QHEADS // KVHEADS)
    aux, segrow = aux_arrays(segments)
    rope = rope_arrays()
    par = jnp.concatenate(
        [
            pad_columns(step_bias[None], 256),
            pad_columns(decay_log[None], 256),
            pad_columns(jnp.repeat(skip_scale, HDIM)[None], 256),
            jnp.zeros((5, 256), F32),
        ],
        axis=0,
    )
    taps = jnp.pad(jnp.concatenate([conv_state, pad_columns(conv_inner, 256)], axis=1), ((0, 4), (0, 0)))

    x = block_input[0].astype(F32)
    normed_here = (x * row_norm(x) * first_gain).astype(BF16)
    normed = spread_rows(normed_here, "tensor")
    shared = spread_rows(jnp.concatenate([state_weight, keyval_weight], axis=1), "tensor")
    share_rows = shared.shape[0]
    key_part = lax.dynamic_slice(shared, (0, 256 + kv_head * AHDIM), (share_rows, AHDIM))
    value_part = lax.dynamic_slice(
        shared, (0, 256 + (KVHEADS + kv_head) * AHDIM), (share_rows, AHDIM)
    )
    w1_here = jnp.concatenate(
        [
            shared[:, 0:256],
            pad_columns(mamba_input, 256),
            pad_columns(mamba_gate, 256),
            query_weight,
            key_part,
            pad_columns(step_weight, 64),
            value_part,
        ],
        axis=1,
    )
    w2_here = jnp.concatenate(
        [mamba_out.T, attention_out.T, feed_gate, feed_up, feed_down.T], axis=1
    )
    w1 = lax.all_gather(w1_here, "dp", axis=0, tiled=True)
    w2 = lax.all_gather(w2_here, "dp", axis=0, tiled=True)

    mix, proj, states, qkv, lse, heads = mixer_forward(
        normed, w1, w2, aux, segrow, par, taps, rope
    )
    hidden = x + sum_rows(mix, "tensor")
    normed_two = spread_rows((hidden * row_norm(hidden) * second_gain).astype(BF16), "tensor")
    cot_all = spread_rows(cotangent[0], "tensor")
    out_part, normed_two_grad, act, feed_grads, second_part = feed_forward_backward(
        normed_two, cot_all, w2
    )
    block_out = hidden + sum_rows(out_part, "tensor")
    hidden_grad = cotangent[0].astype(F32) + norm_back(
        hidden, second_gain, sum_rows(normed_two_grad, "tensor")
    )
    mix_grad = spread_rows(hidden_grad.astype(BF16), "tensor")
    dproj, normed_grad, small, first_part = mixer_backward(
        mix_grad, w2, w1, normed, aux, segrow, par, taps, rope, proj, states, qkv, lse
    )
    w2_grad = jnp.concatenate(
        [
            dot_left(mix_grad, heads).astype(BF16),
            dot_left(normed_two, feed_grads).astype(BF16),
            dot_left(cot_all, act).astype(BF16),
        ],
        axis=1,
    )
    w1_grad = dot_left(normed, dproj).astype(BF16)
    input_grad = hidden_grad + norm_back(x, first_gain, sum_rows(normed_grad, "tensor"))

    w2_sum = sum_rows(w2_grad, "dp")
    w1_sum = sum_rows(w1_grad, "dp")
    shared_sum = jnp.zeros((share_rows, 512), F32)
    shared_sum = lax.dynamic_update_slice(shared_sum, w1_sum[:, 0:256], (0, 0))
    shared_sum = lax.dynamic_update_slice(
        shared_sum, w1_sum[:, 832:896], (0, 256 + kv_head * AHDIM)
    )
    shared_sum = lax.dynamic_update_slice(
        shared_sum, w1_sum[:, 960:1024], (0, 256 + (KVHEADS + kv_head) * AHDIM)
    )
    shared_sum = sum_rows(shared_sum, "tensor")

    tensor_count = lax.axis_size("tensor")
    own = jnp.concatenate(
        [
            small[0:4, 256 : 256 + INNER].reshape(-1),
            small[8, 0:HEADS],
            small[9, 0:HEADS],
            jnp.sum(small[8, 256 : 256 + INNER].reshape(HEADS, HDIM), axis=1),
        ]
    )
    own_all = lax.dynamic_update_slice(
        jnp.zeros((tensor_count, own.shape[0]), F32), own[None], (tensor_index, 0)
    )
    first_sum, second_sum, state_taps_sum, own_sum = lax.psum(
        (first_part[0] / first_gain, second_part[0] / second_gain, small[0:4, 0:256], own_all),
        ("dp", "tensor"),
    )
    own = lax.dynamic_slice(own_sum, (tensor_index, 0), (1, own.shape[0]))[0]
    taps_end = 4 * INNER
    return (
        block_out.astype(BF16)[None],
        input_grad[None],
        first_sum,
        w1_sum[:, GATE_AT : GATE_AT + INNER],
        w1_sum[:, 256 : 256 + INNER],
        w1_sum[:, SV_AT : SV_AT + HEADS],
        shared_sum[:, 0:256],
        own[0:taps_end].reshape(4, INNER),
        state_taps_sum,
        own[taps_end : taps_end + HEADS],
        own[taps_end + HEADS : taps_end + 2 * HEADS],
        own[taps_end + 2 * HEADS :],
        w1_sum[:, QK_AT : QK_AT + AHDIM],
        shared_sum[:, 256:512],
        w2_sum[:, 0:INNER].T,
        w2_sum[:, INNER:256].T,
        second_sum,
        w2_sum[:, 256:512],
        w2_sum[:, 512:768],
        w2_sum[:, 768:1024].T,
    )


def solution(mesh):
    in_specs = (
        P("dp", "tensor", None),
        P("dp", None),
        P(),
        P("dp", "tensor"),
        P("dp", "tensor"),
        P("dp", "tensor"),
        P(("dp", "tensor"), None),
        P(None, "tensor"),
        P(),
        P("tensor"),
        P("tensor"),
        P("tensor"),
        P("dp", "tensor"),
        P(("dp", "tensor"), None),
        P("tensor", "dp"),
        P("tensor", "dp"),
        P(),
        P("dp", "tensor"),
        P("dp", "tensor"),
        P("tensor", "dp"),
        P("dp", "tensor", None),
    )
    out_specs = (
        P("dp", "tensor", None),
        P("dp", "tensor", None),
        P(),
        P("dp", "tensor"),
        P("dp", "tensor"),
        P("dp", "tensor"),
        P(("dp", "tensor"), None),
        P(None, "tensor"),
        P(),
        P("tensor"),
        P("tensor"),
        P("tensor"),
        P("dp", "tensor"),
        P(("dp", "tensor"), None),
        P("tensor", "dp"),
        P("tensor", "dp"),
        P(),
        P("dp", "tensor"),
        P("dp", "tensor"),
        P("tensor", "dp"),
    )
    return jax.shard_map(body, mesh=mesh, in_specs=in_specs, out_specs=out_specs, check_vma=False)
```

```python
import jax
import jax.numpy as jnp
from jax import lax
from jax.experimental import pallas as pl
from jax.experimental.pallas import tpu as pltpu
from jax.sharding import PartitionSpec as P

QHEADS = 8
KVHEADS = 2
AHDIM = 64
TOKENS = 1024
WIDTH = 1024
BLOCK = 128
BLOCKS = TOKENS // BLOCK
HEADS = 3
HDIM = 64
INNER = HEADS * HDIM
FEED = 256
QUERY_BLOCK = 256
NORM_EPS = 1e-05
ROPE_BASE = 10000.0
MASKED = -1e30
VMEM_BYTES = 60 * 1024 * 1024

KV_AT = 0
CONV_AT = 128
GATE_AT = 640
QS_AT = 896
PACKED = 1024
EARLY = 384
SENT = 896
PAYLOAD = 32
CONV_WIDTH = 512
STEP_LANE = 64

ROWS16 = ("zlo", "xh", "xl", "yl")
FEED32 = ("yh", *ROWS16)
TENSOR = ("yh", "yl", "zhi")
FINE_SIZES = (2,) * 7
MIX = ("c", "yh", "yl", "zhi")

F32 = jnp.float32
BF16 = jnp.bfloat16


def dot(a, b):
    return lax.dot_general(a, b, (((1,), (0,)), ((), ())), preferred_element_type=F32)


def dot_right(a, b):
    return lax.dot_general(a, b, (((1,), (1,)), ((), ())), preferred_element_type=F32)


def dot_left(a, b):
    return lax.dot_general(a, b, (((0,), (0,)), ((), ())), preferred_element_type=F32)


def parts_of(values, terms):
    parts = []
    for _ in range(terms - 1):
        part = values.astype(BF16)
        parts.append(part)
        values = values - part.astype(F32)
    parts.append(values.astype(BF16))
    return parts


def times_ones(values, ones, terms=2):
    return sum(dot(part, ones) for part in parts_of(values, terms))


def ones_times(ones, values, terms=2):
    return sum(dot(ones, part) for part in parts_of(values, terms))


def iota(shape, dim):
    return lax.broadcasted_iota(jnp.int32, shape, dim)


def softplus(v):
    return jnp.maximum(v, 0.0) + jnp.log1p(jnp.exp(-jnp.abs(v)))


def sigmoid(v):
    return 1.0 / (1.0 + jnp.exp(-v))


def head_matrices():
    lane, channel = (iota((BLOCK, 256), 0), iota((BLOCK, 256), 1))
    spread = ((channel >> 6) + STEP_LANE == lane) & (channel < INNER)
    lane, channel = (iota((256, BLOCK), 1), iota((256, BLOCK), 0))
    gather = ((channel >> 6) + STEP_LANE == lane) & (channel < INNER)
    return (spread.astype(BF16), gather.astype(BF16))


def per_head(values):
    of_head = iota(values.shape, 1) >> 6
    return jnp.concatenate(
        [jnp.where(of_head == h, values, jnp.zeros_like(values)) for h in range(HEADS)], axis=0
    )


def conv_parts(proj_ref, par_ref, aux, start):
    here = proj_ref[pl.ds(start, BLOCK), CONV_AT:GATE_AT]
    before = proj_ref[pl.ds(pl.multiple_of(jnp.maximum(start - 8, 0), 8), 8), CONV_AT:GATE_AT]
    both = jnp.concatenate([before, here], axis=0)
    lagged = [here]
    for lag in range(1, 4):
        lagged.append(both[8 - lag : 8 - lag + BLOCK] * aux[:, lag : lag + 1])
    pre = sum(lagged[lag] * par_ref[lag : lag + 1, :] for lag in range(4))
    return (lagged, pre)


def step_parts(proj_ref, par_ref, aux, lower, start):
    raw = proj_ref[pl.ds(start, BLOCK), QS_AT:PACKED] + par_ref[8:9, 0:128]
    lane = iota((BLOCK, 128), 1)
    is_head = (lane >= STEP_LANE) & (lane < STEP_LANE + HEADS)
    step = jnp.where(is_head, softplus(raw), 0.0)
    rate = -step * jnp.exp(par_ref[9:10, 0:128])
    total = ones_times(lower, rate, 3)
    reach = aux[:, 4:5] * jnp.exp(total)
    to_end = aux[:, 5:6] * jnp.exp(total[BLOCK - 1 : BLOCK, :] - total)
    return (raw, is_head, step, rate, total, reach, to_end)


def decay_of(total, total_rows, keep, h):
    at = STEP_LANE + h
    gap = total[:, at : at + 1] - total_rows[at : at + 1, :]
    return jnp.exp(jnp.where(keep, gap, MASKED))


def turn_halves(values, rope, back):
    up = pltpu.roll(values, 96, 1) * rope[:, 128:256]
    down = pltpu.roll(values, 32, 1) * rope[:, 256:384]
    here = values * rope[:, 0:128]
    return here - up - down if back else here + up + down


def allowed_keys(aux_ref, segrow_ref, first, count):
    query_seg = aux_ref[first : first + QUERY_BLOCK, 0:1]
    key_seg = segrow_ref[0:1, 0:count]
    shape = (QUERY_BLOCK, count)
    return (query_seg == key_seg) & (iota(shape, 1) <= iota(shape, 0) + first)


def fold(line):
    return jnp.concatenate([line[:, 128 * i : 128 * i + 128] for i in range(8)], axis=0)


def place_pieces(place_ref, pieces, whole_ref, sems):
    copies = []
    for mate in range(2):
        for k in range(4):
            near = place_ref[1] ^ k
            block = 4 * (near >> 1) + 2 * (place_ref[0] ^ mate) + (near & 1)
            rows = pl.ds(pl.multiple_of(block * BLOCK, BLOCK), BLOCK)
            at = 4 * mate + k
            piece = pieces[at].at[pl.ds(0, BLOCK), :]
            copies.append(pltpu.make_async_copy(piece, whole_ref.at[rows, :], sems.at[at]))
    for copy in copies:
        copy.start()
    for copy in copies:
        copy.wait()


def write_halves(place_ref, keep_ref, send_ref, index, value):
    at = index & 2

    @pl.when(place_ref[0] == (index & 1))
    def _():
        keep_ref[at] = value[0:BLOCK]
        keep_ref[at + 1] = value[BLOCK:]

    @pl.when(place_ref[0] != (index & 1))
    def _():
        send_ref[at] = value[0:BLOCK]
        send_ref[at + 1] = value[BLOCK:]


def mixer_forward_kernel(
    place_ref,
    p0,
    p1,
    p2,
    p3,
    p4,
    p5,
    p6,
    p7,
    w_ref,
    aux_ref,
    segrow_ref,
    par_ref,
    rope_ref,
    keep_ref,
    send_ref,
    normed_ref,
    proj_ref,
    states_ref,
    qkv_ref,
    lse_ref,
    heads_ref,
    sems,
):
    place_pieces(place_ref, (p0, p1, p2, p3, p4, p5, p6, p7), normed_ref, sems)
    for first in range(0, TOKENS, 256):
        rows = slice(first, first + 256)
        state = dot(normed_ref[rows, :], w_ref[:, 0:512])
        proj_ref[rows, CONV_AT : CONV_AT + 256] = state[:, 0:256]
        proj_ref[rows, KV_AT:CONV_AT] = state[:, 256:384]
        proj_ref[rows, QS_AT:PACKED] = state[:, 384:512]
        inner = dot(normed_ref[rows, :], w_ref[:, 512:SENT])
        real = iota((256, 256), 1) < INNER
        gate = jnp.concatenate([inner[:, INNER:], inner[:, 0:64]], axis=1)
        proj_ref[rows, CONV_AT + 256 : GATE_AT] = jnp.where(real, inner[:, 0:256], 0.0)
        proj_ref[rows, GATE_AT:QS_AT] = jnp.where(real, gate, 0.0)
    lane = iota((256, 128), 1)
    for first in range(0, TOKENS, 256):
        rows = slice(first, first + 256)
        rope = rope_ref[rows, :]
        keyval = proj_ref[rows, KV_AT:CONV_AT]
        turned = turn_halves(proj_ref[rows, QS_AT:PACKED], rope, False)
        qkv_ref[rows, 0:128] = (turned * AHDIM**-0.5).astype(BF16)
        qkv_ref[rows, 128:256] = turn_halves(keyval, rope, False).astype(BF16)
        ones = jnp.where(lane == 0, 1.0, 0.0)
        qkv_ref[rows, 256:384] = jnp.where(lane >= 64, keyval, ones).astype(BF16)
    for first in range(0, TOKENS, QUERY_BLOCK):
        rows = slice(first, first + QUERY_BLOCK)
        count = first + QUERY_BLOCK
        scores = dot_right(qkv_ref[rows, 0:128], qkv_ref[0:count, 128:256])
        scores = jnp.where(allowed_keys(aux_ref, segrow_ref, first, count), scores, MASKED)
        top = jnp.max(scores, axis=1, keepdims=True)
        raised = jnp.exp(scores - top)
        summed = dot(raised.astype(BF16), qkv_ref[0:count, 256:384])
        total = summed[:, 0:1]
        heads_ref[rows, 128:256] = jnp.where(lane >= 64, summed / total, 0.0).astype(BF16)
        lse_ref[rows, :] = jnp.broadcast_to(top + jnp.log(total), (QUERY_BLOCK, 128))

    spread, _ = head_matrices()
    causal = iota((BLOCK, BLOCK), 0) >= iota((BLOCK, BLOCK), 1)
    lower = causal.astype(BF16)

    def block_step(index, state):
        start = pl.multiple_of(index * BLOCK, BLOCK)
        rows = pl.ds(start, BLOCK)
        aux = aux_ref[rows, :]
        _, pre = conv_parts(proj_ref, par_ref, aux, start)
        conv = (pre * sigmoid(pre)).astype(BF16)
        in_map, out_map, inner = (conv[:, 0:128], conv[:, 128:256], conv[:, 256:512].astype(F32))
        _, _, step, _, total, reach, to_end = step_parts(proj_ref, par_ref, aux, lower, start)
        wide = times_ones(jnp.concatenate([step, reach, to_end], axis=0), spread)
        step_wide, reach_wide, end_wide = (wide[0:128], wide[128:256], wide[256:384])
        stepped = inner * step_wide
        keep = causal & (aux[:, 0:1] == segrow_ref[0:1, pl.ds(start, BLOCK)])
        total_rows = jnp.transpose(total)
        shared = dot_right(out_map, in_map)
        mixing = jnp.concatenate(
            [(decay_of(total, total_rows, keep, h) * shared).astype(BF16) for h in range(HEADS)],
            axis=1,
        )
        states_ref[rows, :] = state
        result = dot(mixing, per_head(stepped).astype(BF16))
        result = result + dot(out_map, state.astype(BF16)) * reach_wide
        result = result + inner * par_ref[10:11, 0:256]
        gate = proj_ref[rows, GATE_AT:QS_AT]
        gated = (result * (gate * sigmoid(gate))).astype(BF16)
        heads_ref[rows, 0:128] = gated[:, 0:128]
        heads_ref[rows, 128:256] = heads_ref[rows, 128:256] + gated[:, 128:256]
        added = dot_left(in_map, (stepped * end_wide).astype(BF16))
        return state * reach_wide[BLOCK - 1 : BLOCK, :] + added

    lax.fori_loop(0, BLOCKS, block_step, jnp.zeros((BLOCK, 256), F32))
    for first in range(0, TOKENS, 256):
        rows = slice(first, first + 256)
        mix = dot_right(heads_ref[rows, :], w_ref[:, SENT:]).astype(BF16)
        write_halves(place_ref, keep_ref, send_ref, first // 256, mix)


def mixer_backward_kernel(
    place_ref,
    p0,
    p1,
    p2,
    p3,
    p4,
    p5,
    p6,
    p7,
    w_ref,
    normed_ref,
    aux_ref,
    segrow_ref,
    par_ref,
    rope_ref,
    proj_ref,
    states_ref,
    qkv_ref,
    lse_ref,
    second_ref,
    keep_ref,
    send_ref,
    mixgrad_ref,
    dproj_ref,
    small_ref,
    d_ref,
    dkv_ref,
    sems,
):
    place_pieces(place_ref, (p0, p1, p2, p3, p4, p5, p6, p7), mixgrad_ref, sems)
    for first in range(0, TOKENS, 256):
        rows = slice(first, first + 256)
        d_ref[rows, :] = dot(mixgrad_ref[rows, :], w_ref[:, SENT:])
    lane = iota((QUERY_BLOCK, 128), 1)
    dkv_ref[...] = jnp.zeros_like(dkv_ref)
    for first in range(0, TOKENS, QUERY_BLOCK):
        rows = slice(first, first + QUERY_BLOCK)
        count = first + QUERY_BLOCK
        queries, keys = (qkv_ref[rows, 0:128], qkv_ref[0:count, 128:256])
        out_grad = jnp.where(lane >= 64, d_ref[rows, 128:256], 0.0).astype(BF16)
        scores = dot_right(queries, keys) - lse_ref[rows, 0:1]
        weights = jnp.exp(
            jnp.where(allowed_keys(aux_ref, segrow_ref, first, count), scores, MASKED)
        )
        weight_grad = dot_right(out_grad, qkv_ref[0:count, 256:384])
        mean = jnp.sum(weights * weight_grad, axis=1, keepdims=True)
        score_grad = (weights * (weight_grad - mean)).astype(BF16)
        query_grad = dot(score_grad, keys) * AHDIM**-0.5
        d_ref[rows, 128:256] = jnp.where(
            lane < 64, d_ref[rows, 128:256], pltpu.roll(query_grad, 64, 1)
        )
        dkv_ref[0:count, 0:128] += dot_left(score_grad, queries)
        dkv_ref[0:count, 128:256] += dot_left(weights.astype(BF16), out_grad)
    for first in range(0, TOKENS, 256):
        rows = slice(first, first + 256)
        rope = rope_ref[rows, :]
        query_grad = turn_halves(pltpu.roll(d_ref[rows, 128:256], 64, 1), rope, True)
        dproj_ref[rows, 384:512] = query_grad.astype(BF16)
        key_grad = turn_halves(dkv_ref[rows, 0:128], rope, True)
        keyval_grad = jnp.where(lane < 64, key_grad, dkv_ref[rows, 128:256])
        dproj_ref[rows, 256:384] = keyval_grad.astype(BF16)

    spread, gather = head_matrices()
    row, column = (iota((BLOCK, BLOCK), 0), iota((BLOCK, BLOCK), 1))
    causal = row >= column
    lower = causal.astype(BF16)
    upper = (row <= column).astype(BF16)
    strict = (row > column).astype(BF16)
    real = iota((BLOCK, 256), 1) < INNER
    head_lane = iota((BLOCK, 128), 1)

    def block_step(turn, carried):
        state_grad, later, taps_sum, head_sum, skip_sum = carried
        start = pl.multiple_of((BLOCKS - 1 - turn) * BLOCK, BLOCK)
        rows = pl.ds(start, BLOCK)
        aux = aux_ref[rows, :]
        lagged, pre = conv_parts(proj_ref, par_ref, aux, start)
        sig = sigmoid(pre)
        conv = (pre * sig).astype(BF16)
        in_map, out_map, inner = (conv[:, 0:128], conv[:, 128:256], conv[:, 256:512].astype(F32))
        raw, is_head, step, rate, total, reach, to_end = step_parts(
            proj_ref, par_ref, aux, lower, start
        )
        wide = times_ones(jnp.concatenate([step, reach, to_end], axis=0), spread)
        step_wide, reach_wide, end_wide = (wide[0:128], wide[128:256], wide[256:384])
        stepped = inner * step_wide
        stepped_low = stepped.astype(BF16)
        keep = causal & (aux[:, 0:1] == segrow_ref[0:1, pl.ds(start, BLOCK)])
        total_rows = jnp.transpose(total)
        shared = dot_right(out_map, in_map)
        decays = [decay_of(total, total_rows, keep, h) for h in range(HEADS)]
        mixing = [(decay * shared).astype(BF16) for decay in decays]
        state = states_ref[rows, :]
        state_low = state.astype(BF16)
        incoming = dot(out_map, state_low) * reach_wide
        result = dot(jnp.concatenate(mixing, axis=1), per_head(stepped).astype(BF16)) + incoming
        result = result + inner * par_ref[10:11, 0:256]

        gate = proj_ref[rows, GATE_AT:QS_AT]
        gate_sig = sigmoid(gate)
        gated_grad = jnp.where(real, d_ref[rows, :], 0.0)
        gate_grad = gated_grad * result * (gate_sig * (1.0 + gate * (1.0 - gate_sig)))
        out_grad = gated_grad * (gate * gate_sig)
        by_head = per_head(out_grad).astype(BF16)

        mixing_grad = dot_right(by_head, stepped_low)
        shared_grad = jnp.zeros((BLOCK, BLOCK), F32)
        edges = []
        for h in range(HEADS):
            decayed = mixing_grad[h * BLOCK : (h + 1) * BLOCK] * decays[h]
            shared_grad = shared_grad + decayed
            edges.append((decayed * shared).astype(BF16))
        crossing = dot(upper, jnp.concatenate(edges, axis=1))
        rate_grad = jnp.zeros((BLOCK, 128), F32)
        for h in range(HEADS):
            part = jnp.where(row > column, crossing[:, h * BLOCK : (h + 1) * BLOCK], 0.0)
            part = jnp.sum(part, axis=1, keepdims=True)
            rate_grad = rate_grad + jnp.where(head_lane == STEP_LANE + h, part, 0.0)

        reached = (out_grad * reach_wide).astype(BF16)
        state_grad_low = state_grad.astype(BF16)
        ended = dot(in_map, state_grad_low) * end_wide
        mapped = dot_left(jnp.concatenate(mixing, axis=0), by_head) + ended
        inner_grad = mapped * step_wide + out_grad * par_ref[10:11, 0:256]
        kept = jnp.sum(state_grad * state, axis=0, keepdims=True)
        kept = jnp.broadcast_to(kept * reach_wide[BLOCK - 1 : BLOCK, :], (8, 256))
        sums = times_ones(
            jnp.concatenate([inner * mapped, out_grad * incoming, stepped * ended, kept], axis=0),
            gather,
        )
        flows = ones_times(
            jnp.concatenate([upper, strict], axis=1), sums[128:384]
        )
        rate_grad = rate_grad + flows + sums[384:385]
        step_grad = sums[0:128] - jnp.exp(par_ref[9:10, 0:128]) * rate_grad
        step_grad = jnp.where(is_head, step_grad * sigmoid(raw), 0.0)
        dproj_ref[rows, 384:512] = dproj_ref[rows, 384:512] + step_grad.astype(BF16)
        head_sum = head_sum + jnp.concatenate(
            [
                jnp.sum(jnp.where(is_head, rate_grad * rate, 0.0), axis=0, keepdims=True),
                jnp.sum(step_grad, axis=0, keepdims=True),
                jnp.zeros((6, 128), F32),
            ],
            axis=0,
        )
        skip_sum = skip_sum + jnp.sum(inner * out_grad, axis=0, keepdims=True)

        shared_low = shared_grad.astype(BF16)
        out_map_grad = dot(shared_low, in_map) + dot_right(reached, state_low)
        in_map_grad = dot_left(shared_low, out_map) + dot_right(
            (stepped * end_wide).astype(BF16), state_grad_low
        )
        conv_grad = jnp.concatenate([in_map_grad, out_map_grad, inner_grad], axis=1)
        pre_grad = conv_grad * (sig * (1.0 + pre * (1.0 - sig)))
        taps_sum = taps_sum + jnp.concatenate(
            [jnp.sum(pre_grad * lagged[lag], axis=0, keepdims=True) for lag in range(4)]
            + [jnp.zeros((4, CONV_WIDTH), F32)],
            axis=0,
        )
        both = jnp.concatenate([pre_grad, later], axis=0)
        masks = aux_ref[pl.ds(start, BLOCK + 8), :]
        u_grad = pre_grad * par_ref[0:1, :]
        for lag in range(1, 4):
            shifted = (both * masks[:, lag : lag + 1])[lag : lag + BLOCK]
            u_grad = u_grad + shifted * par_ref[lag : lag + 1, :]
        dproj_ref[rows, 0:256] = u_grad[:, 0:256].astype(BF16)
        inner = jnp.concatenate([u_grad[:, 256 : 256 + INNER], gate_grad[:, 0:INNER]], axis=1)
        dproj_ref[rows, 512:SENT] = inner.astype(BF16)
        state_grad = state_grad * reach_wide[BLOCK - 1 : BLOCK, :] + dot_left(out_map, reached)
        return (state_grad, pre_grad[0:8], taps_sum, head_sum, skip_sum)

    carried = (
        jnp.zeros((BLOCK, 256), F32),
        jnp.zeros((8, CONV_WIDTH), F32),
        jnp.zeros((8, CONV_WIDTH), F32),
        jnp.zeros((8, 128), F32),
        jnp.zeros((1, 256), F32),
    )
    _, _, taps_sum, head_sum, skip_sum = lax.fori_loop(0, BLOCKS, block_step, carried)
    gain = jnp.zeros((1, WIDTH), F32)
    for first in range(0, TOKENS, 256):
        rows = slice(first, first + 256)
        grad = dot_right(dproj_ref[rows, :], w_ref[:, 0:SENT])
        write_halves(place_ref, keep_ref, send_ref, first // 256, grad.astype(BF16))
        gain = gain + jnp.sum(grad * normed_ref[rows, :].astype(F32), axis=0, keepdims=True)
    upper_rows = jnp.concatenate([taps_sum[0:4, 0:256], taps_sum[0:4, 256:512]], axis=0)
    upper_rows = jnp.concatenate([upper_rows, fold(gain)], axis=1)
    skip_rows = jnp.concatenate([skip_sum, jnp.zeros((7, 256), F32)], axis=0)
    lower_rows = jnp.concatenate([fold(second_ref[0:1, :]), head_sum[:, 64:128], skip_rows[:, 0:INNER]], axis=1)
    small = jnp.concatenate([upper_rows, lower_rows], axis=0)
    high = small.astype(BF16)
    small_ref[0:16, :] = high
    small_ref[16:32, :] = (small - high.astype(F32)).astype(BF16)


def feed_kernel(
    a0, a1, m0, m1, ca0, ca1, cm0, cm1, w_ref,
    out_keep0, out_keep1, out_send0, out_send1, grad_keep0, grad_keep1, grad_send0, grad_send1,
    act_ref, grads_ref, gain_ref,
):
    gain = jnp.zeros((1, WIDTH), F32)
    outs = ((out_keep0, out_send0), (out_keep1, out_send1))
    grad_outs = ((grad_keep0, grad_send0), (grad_keep1, grad_send1))
    inputs = ((a0, m0, ca0, cm0), (a1, m1, ca1, cm1))
    for j in range(2):
        own, mate, own_cot, mate_cot = inputs[j]
        rows = slice(256 * j, 256 * j + 256)
        normed = jnp.concatenate([own[...], mate[...]], axis=0)
        cot = jnp.concatenate([own_cot[...], mate_cot[...]], axis=0)
        out_sum, grad_sum = (0.0, 0.0)
        for h in range(2):
            both = dot(normed, w_ref[h, :, 0:512])
            gate, up = (both[:, 0:FEED], both[:, FEED:])
            sig = sigmoid(gate)
            silu = gate * sig
            act = (silu * up).astype(BF16)
            act_ref[rows, h * FEED : (h + 1) * FEED] = act
            out_sum = out_sum + dot_right(act, w_ref[h, :, 512:768])
            act_grad = dot(cot, w_ref[h, :, 512:768])
            gate_grad = (act_grad * up * (sig + silu * (1.0 - sig))).astype(BF16)
            up_grad = (act_grad * silu).astype(BF16)
            grads = jnp.concatenate([gate_grad, up_grad], axis=1)
            grads_ref[rows, h * 512 : (h + 1) * 512] = grads
            grad_sum = grad_sum + dot_right(grads, w_ref[h, :, 0:512])
        gain = gain + jnp.sum(grad_sum * normed.astype(F32), axis=0, keepdims=True)
        out_low, grad_low = (out_sum.astype(BF16), grad_sum.astype(BF16))
        for half in range(2):
            outs[j][half][...] = out_low[half * BLOCK : (half + 1) * BLOCK]
            grad_outs[j][half][...] = grad_low[half * BLOCK : (half + 1) * BLOCK]
    gain_ref[...] = jnp.broadcast_to(gain, (8, WIDTH))


def feed_weights_kernel(a0, a1, m0, m1, ca0, ca1, cm0, cm1, act_ref, grads_ref, out_ref):
    normed = jnp.concatenate([r[...] for r in (a0, m0, a1, m1)], axis=0)
    cot = jnp.concatenate([r[...] for r in (ca0, cm0, ca1, cm1)], axis=0)
    up = dot_left(normed, grads_ref[...]).astype(BF16)
    down = dot_left(cot, act_ref[...]).astype(BF16)
    for h in range(2):
        out_ref[h, :, 0:512] = up[:, h * 512 : (h + 1) * 512]
        out_ref[h, :, 512:768] = down[:, h * FEED : (h + 1) * FEED]


def early_weights_kernel(normed_ref, dproj_ref, small_ref, out_ref):
    grad = dot_left(normed_ref[...], dproj_ref[:, 0:EARLY]).astype(BF16)
    for i in range(16):
        out_ref[i, 0:64, :] = grad[64 * i : 64 * i + 64]
        out_ref[i, 64:, :] = small_ref[...]


def main_weights_kernel(normed_ref, dproj_ref, mixgrad_ref, heads_ref, out_ref):
    out_ref[:, 0:512] = dot_left(normed_ref[...], dproj_ref[:, EARLY:SENT]).astype(BF16)
    out_ref[:, 512:] = dot_left(mixgrad_ref[...], heads_ref[...]).astype(BF16)


def pair_kernel(turn_ref, keep_ref, come_ref, o0, o1, o2, o3):
    for k, out in enumerate((o0, o1, o2, o3)):
        at = turn_ref[0] ^ k
        out[...] = (keep_ref[at].astype(F32) + come_ref[at].astype(F32)).astype(BF16)


def total_of(pieces):
    return sum(piece[...].astype(F32) for piece in pieces)


def row_norm(values):
    return lax.rsqrt(jnp.mean(values * values, axis=-1, keepdims=True) + NORM_EPS)


def norm_back(values, gain, grad):
    scale = row_norm(values)
    scaled = grad * gain
    return scale * scaled - values * (
        scale**3 * jnp.mean(scaled * values, axis=-1, keepdims=True)
    )


def first_norm_kernel(x_ref, gain_ref, normed_ref):
    x = x_ref[...].astype(F32)
    normed_ref[...] = (x * row_norm(x) * gain_ref[...]).astype(BF16)


def add_kernel(a_ref, b_ref, out_ref):
    out_ref[...] = (a_ref[...].astype(F32) + b_ref[...].astype(F32)).astype(BF16)


def second_norm_kernel(x_ref, gain_ref, s0, s1, s2, s3, hidden_ref, normed_ref):
    hidden = x_ref[...].astype(F32) + total_of((s0, s1, s2, s3))
    hidden_ref[...] = hidden
    normed_ref[...] = (hidden * row_norm(hidden) * gain_ref[...]).astype(BF16)


def hidden_grad_kernel(hidden_ref, gain_ref, cot_ref, s0, s1, s2, grad_ref, low_ref):
    back = norm_back(hidden_ref[...], gain_ref[...], total_of((s0, s1, s2)))
    grad = cot_ref[...].astype(F32) + back
    grad_ref[...] = grad
    low_ref[...] = grad.astype(BF16)


def input_grad_kernel(x_ref, gain_ref, hidden_grad_ref, s0, s1, s2, s3, grad_ref):
    x = x_ref[...].astype(F32)
    back = norm_back(x, gain_ref[...], total_of((s0, s1, s2, s3)))
    grad_ref[...] = hidden_grad_ref[...] + back


def output_kernel(hidden_ref, s0, s1, s2, out_ref):
    out_ref[...] = (hidden_ref[...] + total_of((s0, s1, s2))).astype(BF16)


def like(dtype, *shape):
    return jax.ShapeDtypeStruct(shape, dtype)


VMEM = pl.BlockSpec(memory_space=pltpu.VMEM)
SMEM = pl.BlockSpec(memory_space=pltpu.SMEM)
ANY = pl.BlockSpec(memory_space=pl.ANY)


def run(kernel, name, outs, args, specs=None, scratch=(), us=0.05):
    return pl.pallas_call(
        kernel,
        in_specs=specs or [VMEM] * len(args),
        out_specs=[VMEM] * len(outs),
        out_shape=list(outs),
        scratch_shapes=list(scratch),
        compiler_params=pltpu.CompilerParams(vmem_limit_bytes=VMEM_BYTES),
        cost_estimate=pl.CostEstimate(
            flops=int(us * 1e9), transcendentals=0, bytes_accessed=int(us * 2e6)
        ),
        name=name,
    )(*args)


HERE = (BLOCK, WIDTH)
FORWARD_US = 20
BACKWARD_US = 33
SLAB = (4, BLOCK, WIDTH)


def mixer_forward(place, pieces, weights, aux, segrow, pack, rope):
    return run(
        mixer_forward_kernel,
        "mixer_forward",
        (
            like(BF16, *SLAB),
            like(BF16, *SLAB),
            like(BF16, TOKENS, WIDTH),
            like(F32, TOKENS, PACKED),
            like(F32, TOKENS, 256),
            like(BF16, TOKENS, 384),
            like(F32, TOKENS, 128),
            like(BF16, TOKENS, 256),
        ),
        (place, *pieces, weights, aux, segrow, pack, rope),
        [SMEM] + [ANY] * 8 + [VMEM] * 5,
        [pltpu.SemaphoreType.DMA((8,))],
        FORWARD_US,
    )


def mixer_backward(
    place, pieces, weights, normed, aux, segrow, pack, rope, proj, states, qkv, lse, second
):
    return run(
        mixer_backward_kernel,
        "mixer_backward",
        (
            like(BF16, *SLAB),
            like(BF16, *SLAB),
            like(BF16, TOKENS, WIDTH),
            like(BF16, TOKENS, SENT),
            like(BF16, PAYLOAD, EARLY),
        ),
        (place, *pieces, weights, normed, aux, segrow, pack, rope, proj, states, qkv, lse, second),
        [SMEM] + [ANY] * 8 + [VMEM] * 11,
        [
            pltpu.VMEM((TOKENS, 256), F32),
            pltpu.VMEM((TOKENS, 256), F32),
            pltpu.SemaphoreType.DMA((8,)),
        ],
        BACKWARD_US,
    )


def feed_forward_backward(normed, cot, weights):
    return run(
        feed_kernel,
        "feed",
        [like(BF16, *HERE)] * 8
        + [like(BF16, 512, 2 * FEED), like(BF16, 512, 4 * FEED), like(F32, 8, WIDTH)],
        (*normed, *cot, weights),
        us=0.1,
    )


def aux_arrays(seg):
    columns = [seg]
    for lag in range(1, 4):
        earlier = jnp.concatenate([jnp.full((lag,), -1.0, F32), seg[: TOKENS - lag]])
        columns.append((earlier == seg).astype(F32))
    ends = seg.reshape(BLOCKS, BLOCK)[:, -1]
    before = jnp.concatenate([jnp.full((1,), -1.0, F32), ends[:-1]])
    columns.append((seg == jnp.repeat(before, BLOCK)).astype(F32))
    columns.append((seg == jnp.repeat(ends, BLOCK)).astype(F32))
    aux = jnp.pad(jnp.stack(columns, axis=1), ((0, 8), (0, 128 - len(columns))))
    return (aux, jnp.broadcast_to(seg, (8, TOKENS)))


def rope_arrays():
    half = AHDIM // 2
    freq = ROPE_BASE ** (-2.0 * jnp.arange(half, dtype=F32) / AHDIM)
    angles = jnp.arange(TOKENS, dtype=F32)[:, None] * freq[None, :]
    cosine, sine = (jnp.cos(angles), jnp.sin(angles))
    none = jnp.zeros_like(sine)
    parts = [cosine, cosine, none, none, -sine, none, none, none, none, sine, none, none]
    return jnp.concatenate(parts, axis=1)


def pad_columns(values, width, before=0):
    return jnp.pad(values, ((0, 0), (before, width - before - values.shape[1])))


def index_of(axes):
    return lax.axis_index(axes)


def exchange(values, axes, turn):
    size = 2 ** len(axes)
    return lax.ppermute(values, axes, [(i, turn(i)) for i in range(size)])


def other_core(values):
    return exchange(values, ("c",), lambda i: i ^ 1)


def mixer_turn(k):
    def turn(i):
        core, high, low, z = (i >> 3, (i >> 2) & 1, (i >> 1) & 1, i & 1)
        return (low << 3) | ((high ^ (k >> 1)) << 2) | (core << 1) | (z ^ (k & 1))

    return turn


def swap_weights(values):
    return exchange(values, ("c", "yl"), lambda i: ((i & 1) << 1) | (i >> 1))


def mixer_gather(shard):
    own = [exchange(shard, MIX, mixer_turn(k)) for k in range(4)]
    return own + [other_core(piece) for piece in own]


def mixer_sum(keep, send, turn):
    pairs = run(pair_kernel, "pair", [like(BF16, *HERE)] * 4, (turn, keep, other_core(send)),
                [SMEM, VMEM, VMEM])
    return [exchange(pairs[k], MIX, mixer_turn(k)) for k in range(4)]


def z_partner(values):
    return exchange(values, ("zhi",), lambda i: i ^ 1)


def feed_gather(shard):
    near = z_partner(shard)
    return (shard, near, other_core(shard), other_core(near))


def add_near(keep, send):
    return run(add_kernel, "add", [like(BF16, *HERE)], (keep, other_core(send)))[0]


def feed_sum(keep0, keep1, send0, send1):
    return (keep0, other_core(send0), z_partner(add_near(keep1, send1)))


def exact_parts(values):
    first = lax.reduce_precision(values, 8, 7)
    second = lax.reduce_precision(values - first, 8, 7)
    return jnp.concatenate([first, second, values - first - second], axis=0).astype(BF16)


def spread_blocks(shard, axes):
    copies = jnp.broadcast_to(shard, (2 ** len(axes), *shard.shape))
    return lax.all_to_all(copies, axes, split_axis=0, concat_axis=0, tiled=True)


def spread_rows(shard, axes):
    return spread_blocks(shard, axes).reshape(-1, *shard.shape[1:])


def turn_blocks(blocks, axes):
    return lax.all_to_all(blocks, axes, split_axis=0, concat_axis=0, tiled=True)


def sum_blocks(blocks):
    return jnp.sum(blocks.astype(F32), axis=0)


def body(
    block_input,
    segments,
    first_gain,
    mamba_gate,
    mamba_input,
    step_weight,
    state_weight,
    conv_inner,
    conv_state,
    decay_log,
    step_bias,
    skip_scale,
    query_weight,
    keyval_weight,
    mamba_out,
    attention_out,
    second_gain,
    feed_gate,
    feed_up,
    feed_down,
    cotangent,
):
    kv_head = lax.axis_index("yh")
    core = lax.axis_index("c")
    near = index_of(("yh", "zhi"))
    place = jnp.stack([core, near]).astype(jnp.int32)
    turn = near.astype(jnp.int32)[None]

    params = jnp.concatenate(
        [
            jnp.concatenate([conv_inner, jnp.zeros((4, INNER), F32)], axis=0),
            jnp.zeros((8, 256 - INNER), F32),
            jnp.concatenate(
                [
                    pad_columns(step_bias[None], 512, STEP_LANE),
                    pad_columns(decay_log[None], 512, STEP_LANE),
                    pad_columns(jnp.repeat(skip_scale, HDIM)[None], 512),
                    jnp.zeros((1, 512), F32),
                    segments.reshape(2, 512).astype(F32),
                    jnp.zeros((2, 512), F32),
                ],
                axis=0,
            ),
        ],
        axis=1,
    )
    x, cot = (block_input[0], cotangent[0])
    gain_one, gain_two = (first_gain[None], second_gain[None])
    shared = turn_blocks(
        jnp.broadcast_to(jnp.concatenate([state_weight, keyval_weight], axis=1), (8, 8, 512)), TENSOR
    ).reshape(-1, 512)
    (normed_here,) = run(first_norm_kernel, "first_norm", [like(BF16, *HERE)], (x, gain_one))
    normed_pieces = mixer_gather(normed_here)
    share_rows = shared.shape[0]
    key_part = lax.dynamic_slice(shared, (0, 256 + kv_head * AHDIM), (share_rows, AHDIM))
    value_part = lax.dynamic_slice(
        shared, (0, 256 + (KVHEADS + kv_head) * AHDIM), (share_rows, AHDIM)
    )
    main_here = jnp.concatenate(
        [
            shared[:, 0:256],
            key_part,
            value_part,
            query_weight,
            pad_columns(step_weight, 64),
            mamba_input,
            mamba_gate,
            mamba_out.T,
            attention_out.T,
        ],
        axis=1,
    )
    feed_here = jnp.concatenate([feed_gate, feed_up, feed_down.T], axis=1)
    feed_here = jnp.concatenate([feed_here, exact_parts(params)], axis=0)
    main_here = jnp.pad(main_here, ((0, 24), (0, 0)))
    swapped = swap_weights(jnp.concatenate([main_here, feed_here], axis=1))
    weights = spread_rows(swapped[0:share_rows, 0:1152], ROWS16)
    feed_here = swapped[0:share_rows, 1152:]
    params = swapped[share_rows:, 1152:].astype(F32).reshape(3, 8, -1)
    params = params[0] + params[1] + params[2]

    pack = jnp.concatenate(
        [
            jnp.concatenate([conv_state, params[0:4, 0:256]], axis=1),
            jnp.zeros((4, 512), F32),
            params[0:3, 256:768],
            jnp.zeros((5, 512), F32),
        ],
        axis=0,
    )
    aux, segrow = aux_arrays(params[4:6, 256:768].reshape(TOKENS))
    rope = rope_arrays()

    feed_here, weights = lax.optimization_barrier((feed_here, weights))
    feed_weights = spread_rows(feed_here, FEED32).reshape(2, WIDTH, 768)
    cot_pieces = feed_gather(cot)

    keep, send, normed, proj, states, qkv, lse, heads = mixer_forward(
        place, normed_pieces, weights, aux, segrow, pack, rope
    )
    hidden, normed_two_here = run(
        second_norm_kernel,
        "second_norm",
        [like(F32, *HERE), like(BF16, *HERE)],
        (x, gain_two, *mixer_sum(keep, send, turn)),
    )
    normed_two = feed_gather(normed_two_here)
    *parts, act, feed_grads, second_part = feed_forward_backward(
        normed_two, cot_pieces, feed_weights
    )
    (feed_grad,) = run(
        feed_weights_kernel,
        "feed_weights",
        [like(BF16, 2, WIDTH, 768)],
        (*normed_two, *cot_pieces, act, feed_grads),
        us=0.1,
    )
    out_near, out_mate = (add_near(parts[1], parts[3]), other_core(parts[2]))
    sums = feed_sum(*parts[4:8])
    hidden, feed_grad, out_near, *sums = lax.optimization_barrier(
        (hidden, feed_grad, out_near, *sums)
    )
    hidden_grad, mix_grad_here = run(
        hidden_grad_kernel,
        "hidden_grad",
        [like(F32, *HERE), like(BF16, *HERE)],
        (hidden, gain_two, cot, *sums),
    )
    mix_grad_pieces = mixer_gather(mix_grad_here)
    feed_blocks = turn_blocks(feed_grad.reshape(32, share_rows, 768), FEED32)
    (block_out,) = run(
        output_kernel,
        "output",
        [like(BF16, *HERE)],
        (hidden, parts[0], out_mate, z_partner(out_near)),
    )

    keep, send, mix_grad, dproj, small = mixer_backward(
        place, mix_grad_pieces, weights, normed, aux, segrow, pack, rope, proj, states, qkv, lse,
        second_part,
    )
    (early_grad,) = run(
        early_weights_kernel,
        "early_weights",
        [like(BF16, 16, share_rows + PAYLOAD, EARLY)],
        (normed, dproj, small),
        us=0.1,
    )
    (main_grad,) = run(
        main_weights_kernel,
        "main_weights",
        [like(BF16, WIDTH, 768)],
        (normed, dproj, mix_grad, heads),
        us=0.1,
    )
    early_grad, feed_blocks = lax.optimization_barrier((early_grad, feed_blocks))
    both = turn_blocks(early_grad, ROWS16)
    main_grad, keep = lax.optimization_barrier((main_grad, keep))
    main_grad, both = lax.optimization_barrier((main_grad, both))
    main_blocks = turn_blocks(main_grad.reshape(16, share_rows, -1), ROWS16)

    both = sum_blocks(both)
    early_sum = both[0:share_rows]
    vector = both[share_rows : share_rows + 16] + both[share_rows + 16 :]
    shared_sum = jnp.zeros((share_rows, 512), F32)
    shared_sum = lax.dynamic_update_slice(shared_sum, early_sum[:, 0:256], (0, 0))
    shared_sum = lax.dynamic_update_slice(
        shared_sum, early_sum[:, 256 : 256 + AHDIM], (0, 256 + kv_head * AHDIM)
    )
    shared_sum = lax.dynamic_update_slice(
        shared_sum, early_sum[:, 256 + AHDIM :], (0, 256 + (KVHEADS + kv_head) * AHDIM)
    )
    shared_sum = shared_sum.reshape(2, 2, 2, 8, 512)
    sent = lax.dynamic_index_in_dim(shared_sum, 1 - core, 1, keepdims=False)
    lines = pad_columns(vector, 512)
    come = other_core(jnp.concatenate([sent.reshape(32, 512), lines], axis=0))
    held = lax.dynamic_index_in_dim(shared_sum, core, 1, keepdims=False)
    held = held.reshape(4, 8, 512) + come[0:32].reshape(4, 8, 512)
    own = jnp.where(core == lax.axis_index("yl"), lines, come[32:])
    lines = lines + come[32:]

    def for_row(k):
        part = lax.dynamic_index_in_dim(held, near ^ k, 0, keepdims=False)
        return jnp.concatenate([part, lines], axis=0)

    come = [exchange(for_row(k), ("yh", "zhi"), lambda i, k=k: i ^ k) for k in range(1, 4)]
    summed = (for_row(0) + come[0]) + (come[1] + come[2])
    all_sum = summed[8:]

    main_blocks, *sums = lax.optimization_barrier((main_blocks, *mixer_sum(keep, send, turn)))
    (input_grad,) = run(
        input_grad_kernel,
        "input_grad",
        [like(F32, *HERE)],
        (x, gain_one, hidden_grad, *sums),
    )
    total = [sum_blocks(main_blocks), pad_columns(summed[0:8], 768), sum_blocks(feed_blocks)]
    total = swap_weights(jnp.concatenate(total, axis=0).astype(BF16)).astype(F32)
    shared_sum = total[share_rows : share_rows + 8, 0:512]
    feed_total = total[share_rows + 8 :]
    total = total[0:share_rows]
    return (
        block_out[None],
        input_grad[None],
        all_sum[0:8, 256:384].reshape(-1) / first_gain,
        total[:, 128 + INNER : 128 + 2 * INNER],
        total[:, 128 : 128 + INNER],
        total[:, STEP_LANE : STEP_LANE + HEADS],
        shared_sum[:, 0:256],
        own[4:8, 0:INNER],
        all_sum[0:4, 0:256],
        own[8, 128 : 128 + HEADS],
        own[9, 128 : 128 + HEADS],
        jnp.sum(own[8, INNER : 2 * INNER].reshape(HEADS, HDIM), axis=1),
        total[:, 0:AHDIM],
        shared_sum[:, 256:512],
        total[:, 512 : 512 + INNER].T,
        total[:, 512 + INNER :].T,
        all_sum[8:16, 0:128].reshape(-1) / second_gain,
        feed_total[:, 0:256],
        feed_total[:, 256:512],
        feed_total[:, 512:768].T,
    )


def solution(mesh):
    DP, TP = (("zlo", "xh", "xl", "c"), ("yh", "yl", "zhi"))
    fine = jax.sharding.Mesh(mesh.devices.reshape(FINE_SIZES), (*DP, *TP))
    in_specs = (
        P(DP, TP, None),
        P(DP, None),
        P(),
        P(DP, TP),
        P(DP, TP),
        P(DP, TP),
        P((*DP, *TP), None),
        P(None, TP),
        P(),
        P(TP),
        P(TP),
        P(TP),
        P(DP, TP),
        P((*DP, *TP), None),
        P(TP, DP),
        P(TP, DP),
        P(),
        P(DP, TP),
        P(DP, TP),
        P(TP, DP),
        P(DP, TP, None),
    )
    out_specs = (
        P(DP, TP, None),
        P(DP, TP, None),
        P(),
        P(DP, TP),
        P(DP, TP),
        P(DP, TP),
        P((*DP, *TP), None),
        P(None, TP),
        P(),
        P(TP),
        P(TP),
        P(TP),
        P(DP, TP),
        P((*DP, *TP), None),
        P(TP, DP),
        P(TP, DP),
        P(),
        P(DP, TP),
        P(DP, TP),
        P(TP, DP),
    )
    return jax.shard_map(body, mesh=fine, in_specs=in_specs, out_specs=out_specs, check_vma=False)
```

```python
import jax
import jax.numpy as jnp
import numpy as np
from jax import lax
from jax.experimental import pallas as pl
from jax.experimental.pallas import tpu as pltpu
from jax.sharding import PartitionSpec as P

QHEADS = 8
KVHEADS = 2
AHDIM = 64
TOKENS = 1024
WIDTH = 1024
BLOCK = 128
BLOCKS = TOKENS // BLOCK
HEADS = 3
HDIM = 64
INNER = HEADS * HDIM
FEED = 256
QUERY_BLOCK = 256
NORM_EPS = 1e-05
ROPE_BASE = 10000.0
MASKED = -1e30
VMEM_BYTES = 60 * 1024 * 1024

KV_AT = 0
CONV_AT = 128
GATE_AT = 640
QS_AT = 896
PACKED = 1024
EARLY = 384
SENT = 896
PAYLOAD = 32
CONV_WIDTH = 512
STEP_LANE = 64

CHIPS = ("zlo", "xh", "xl")
FEED16 = ("yh", *CHIPS)
TENSOR = ("yh", "yl", "zhi")
NEAR = ("yl", "zhi")
PIECE = BLOCK + 16
WIDE = 1152
FINE_SIZES = (2,) * 7

F32 = jnp.float32
BF16 = jnp.bfloat16


def dot(a, b):
    return lax.dot_general(a, b, (((1,), (0,)), ((), ())), preferred_element_type=F32)


def dot_right(a, b):
    return lax.dot_general(a, b, (((1,), (1,)), ((), ())), preferred_element_type=F32)


def dot_left(a, b):
    return lax.dot_general(a, b, (((0,), (0,)), ((), ())), preferred_element_type=F32)


def parts_of(values, terms):
    parts = []
    for _ in range(terms - 1):
        part = values.astype(BF16)
        parts.append(part)
        values = values - part.astype(F32)
    parts.append(values.astype(BF16))
    return parts


def times_ones(values, ones, terms=2):
    return sum(dot(part, ones) for part in parts_of(values, terms))


def ones_times(ones, values, terms=2):
    return sum(dot(ones, part) for part in parts_of(values, terms))


def iota(shape, dim):
    return lax.broadcasted_iota(jnp.int32, shape, dim)


def softplus(v):
    return jnp.maximum(v, 0.0) + jnp.log1p(jnp.exp(-jnp.abs(v)))


def sigmoid(v):
    return 1.0 / (1.0 + jnp.exp(-v))


def head_matrices():
    lane, channel = (iota((BLOCK, 256), 0), iota((BLOCK, 256), 1))
    spread = ((channel >> 6) + STEP_LANE == lane) & (channel < INNER)
    lane, channel = (iota((256, BLOCK), 1), iota((256, BLOCK), 0))
    gather = ((channel >> 6) + STEP_LANE == lane) & (channel < INNER)
    return (spread.astype(BF16), gather.astype(BF16))


def per_head(values):
    of_head = iota(values.shape, 1) >> 6
    return jnp.concatenate(
        [jnp.where(of_head == h, values, jnp.zeros_like(values)) for h in range(HEADS)], axis=0
    )


def conv_parts(proj_ref, par_ref, aux, start):
    here = proj_ref[pl.ds(start, BLOCK), CONV_AT:GATE_AT]
    before = proj_ref[pl.ds(pl.multiple_of(jnp.maximum(start - 8, 0), 8), 8), CONV_AT:GATE_AT]
    both = jnp.concatenate([before, here], axis=0)
    lagged = [here]
    for lag in range(1, 4):
        lagged.append(both[8 - lag : 8 - lag + BLOCK] * aux[:, lag : lag + 1])
    pre = sum(lagged[lag] * par_ref[lag : lag + 1, :] for lag in range(4))
    return (lagged, pre)


def step_parts(proj_ref, par_ref, aux, lower, start):
    raw = proj_ref[pl.ds(start, BLOCK), QS_AT:PACKED] + par_ref[8:9, 0:128]
    lane = iota((BLOCK, 128), 1)
    is_head = (lane >= STEP_LANE) & (lane < STEP_LANE + HEADS)
    step = jnp.where(is_head, softplus(raw), 0.0)
    rate = -step * jnp.exp(par_ref[9:10, 0:128])
    total = ones_times(lower, rate, 3)
    reach = aux[:, 4:5] * jnp.exp(total)
    to_end = aux[:, 5:6] * jnp.exp(total[BLOCK - 1 : BLOCK, :] - total)
    return (raw, is_head, step, rate, total, reach, to_end)


def decay_of(total, total_rows, keep, h):
    at = STEP_LANE + h
    gap = total[:, at : at + 1] - total_rows[at : at + 1, :]
    return jnp.exp(jnp.where(keep, gap, MASKED))


def turn_halves(values, rope, back):
    up = pltpu.roll(values, 96, 1) * rope[:, 128:256]
    down = pltpu.roll(values, 32, 1) * rope[:, 256:384]
    here = values * rope[:, 0:128]
    return here - up - down if back else here + up + down


def allowed_keys(aux_ref, segrow_ref, first, count):
    query_seg = aux_ref[first : first + QUERY_BLOCK, 0:1]
    key_seg = segrow_ref[0:1, 0:count]
    shape = (QUERY_BLOCK, count)
    return (query_seg == key_seg) & (iota(shape, 1) <= iota(shape, 0) + first)


def fold(line):
    return jnp.concatenate([line[:, 128 * i : 128 * i + 128] for i in range(8)], axis=0)


def begin(pairs, sems, first=0):
    copies = [
        pltpu.make_async_copy(source, target, sems.at[first + at])
        for at, (source, target) in enumerate(pairs)
    ]
    for copy in copies:
        copy.start()
    return copies


def finish(*copies):
    for copy in copies:
        copy.wait()


def join_cores(core, own, mate, whole, sems, first):
    lead = (slice(None),) * (len(whole.shape) - 3)
    pairs = [(own, whole.at[(*lead, core)]), (mate, whole.at[(*lead, 1 - core)])]
    return begin(pairs, sems, first)


def split_cores(core, whole, keep, send, sems, first):
    lead = (slice(None),) * (len(whole.shape) - 3)
    pairs = [(whole.at[(*lead, core)], keep), (whole.at[(*lead, 1 - core)], send)]
    return begin(pairs, sems, first)


def columns(ref, first, last):
    return ref[:, :, :, first:last].reshape(WIDTH, last - first)


def mixer_forward_kernel(
    core_ref,
    p0,
    p1,
    p2,
    p3,
    p4,
    p5,
    p6,
    p7,
    own_hbm,
    mate_hbm,
    rope_hbm,
    aux_hbm,
    segrow_ref,
    par_ref,
    normed_hbm,
    mix_hbm,
    proj_hbm,
    states_hbm,
    qkv_hbm,
    lse_hbm,
    heads_hbm,
    normed_ref,
    w_ref,
    rope_ref,
    aux_ref,
    mix_ref,
    proj_ref,
    states_ref,
    qkv_ref,
    lse_ref,
    heads_ref,
    in_sems,
    out_sems,
):
    pieces = [
        (piece, normed_ref.at[core_ref[2] ^ k])
        for k, piece in enumerate((p0, p1, p2, p3, p4, p5, p6, p7))
    ]
    first_come = begin(pieces, in_sems, 0)
    first_come += join_cores(core_ref[0], own_hbm, mate_hbm, w_ref, in_sems, 8)
    come = begin([(rope_hbm, rope_ref), (aux_hbm, aux_ref)], in_sems, 10)
    finish(*first_come)
    gone = begin([(normed_ref, normed_hbm)], out_sems, 10)
    for chunk in range(4):
        rows = slice(256 * chunk, 256 * chunk + 256)
        normed = normed_ref[2 * chunk : 2 * chunk + 2].reshape(256, WIDTH)
        state = dot(normed, columns(w_ref, 0, 512))
        proj_ref[rows, CONV_AT : CONV_AT + 256] = state[:, 0:256]
        proj_ref[rows, KV_AT:CONV_AT] = state[:, 256:384]
        proj_ref[rows, QS_AT:PACKED] = state[:, 384:512]
        inner = dot(normed, columns(w_ref, 512, SENT))
        real = iota((256, 256), 1) < INNER
        gate = jnp.concatenate([inner[:, INNER:], inner[:, 0:64]], axis=1)
        proj_ref[rows, CONV_AT + 256 : GATE_AT] = jnp.where(real, inner[:, 0:256], 0.0)
        proj_ref[rows, GATE_AT:QS_AT] = jnp.where(real, gate, 0.0)
    gone += begin([(proj_ref, proj_hbm)], out_sems, 1)
    finish(*come)
    lane = iota((256, 128), 1)
    for first in range(0, TOKENS, 256):
        rows = slice(first, first + 256)
        rope = rope_ref[rows, :]
        keyval = proj_ref[rows, KV_AT:CONV_AT]
        turned = turn_halves(proj_ref[rows, QS_AT:PACKED], rope, False)
        qkv_ref[rows, 0:128] = (turned * AHDIM**-0.5).astype(BF16)
        qkv_ref[rows, 128:256] = turn_halves(keyval, rope, False).astype(BF16)
        ones = jnp.where(lane == 0, 1.0, 0.0)
        qkv_ref[rows, 256:384] = jnp.where(lane >= 64, keyval, ones).astype(BF16)
    gone += begin([(qkv_ref, qkv_hbm)], out_sems, 2)
    for first in range(0, TOKENS, QUERY_BLOCK):
        rows = slice(first, first + QUERY_BLOCK)
        count = first + QUERY_BLOCK
        scores = dot_right(qkv_ref[rows, 0:128], qkv_ref[0:count, 128:256])
        scores = jnp.where(allowed_keys(aux_ref, segrow_ref, first, count), scores, MASKED)
        top = jnp.max(scores, axis=1, keepdims=True)
        raised = jnp.exp(scores - top)
        summed = dot(raised.astype(BF16), qkv_ref[0:count, 256:384])
        total = summed[:, 0:1]
        heads_ref[rows, 128:256] = jnp.where(lane >= 64, summed / total, 0.0).astype(BF16)
        lse_ref[rows, :] = jnp.broadcast_to(top + jnp.log(total), (QUERY_BLOCK, 128))

    gone += begin([(lse_ref, lse_hbm)], out_sems, 3)

    spread, _ = head_matrices()
    causal = iota((BLOCK, BLOCK), 0) >= iota((BLOCK, BLOCK), 1)
    lower = causal.astype(BF16)

    def block_step(index, state):
        start = pl.multiple_of(index * BLOCK, BLOCK)
        rows = pl.ds(start, BLOCK)
        aux = aux_ref[rows, :]
        _, pre = conv_parts(proj_ref, par_ref, aux, start)
        conv = (pre * sigmoid(pre)).astype(BF16)
        in_map, out_map, inner = (conv[:, 0:128], conv[:, 128:256], conv[:, 256:512].astype(F32))
        _, _, step, _, total, reach, to_end = step_parts(proj_ref, par_ref, aux, lower, start)
        wide = times_ones(jnp.concatenate([step, reach, to_end], axis=0), spread)
        step_wide, reach_wide, end_wide = (wide[0:128], wide[128:256], wide[256:384])
        stepped = inner * step_wide
        keep = causal & (aux[:, 0:1] == segrow_ref[0:1, pl.ds(start, BLOCK)])
        total_rows = jnp.transpose(total)
        shared = dot_right(out_map, in_map)
        mixing = jnp.concatenate(
            [(decay_of(total, total_rows, keep, h) * shared).astype(BF16) for h in range(HEADS)],
            axis=1,
        )
        states_ref[rows, :] = state
        result = dot(mixing, per_head(stepped).astype(BF16))
        result = result + dot(out_map, state.astype(BF16)) * reach_wide
        result = result + inner * par_ref[10:11, 0:256]
        gate = proj_ref[rows, GATE_AT:QS_AT]
        gated = (result * (gate * sigmoid(gate))).astype(BF16)
        heads_ref[rows, 0:128] = gated[:, 0:128]
        heads_ref[rows, 128:256] = heads_ref[rows, 128:256] + gated[:, 128:256]
        added = dot_left(in_map, (stepped * end_wide).astype(BF16))
        return state * reach_wide[BLOCK - 1 : BLOCK, :] + added

    lax.fori_loop(0, BLOCKS, block_step, jnp.zeros((BLOCK, 256), F32), unroll=UNROLL)
    gone += begin([(states_ref, states_hbm), (heads_ref, heads_hbm)], out_sems, 4)
    w2 = columns(w_ref, SENT, WIDE)
    for chunk in range(4):
        rows = slice(256 * chunk, 256 * chunk + 256)
        mix_ref[rows, :] = dot_right(heads_ref[rows, :], w2).astype(BF16)
        gone += begin([(mix_ref.at[rows, :], mix_hbm.at[rows, :])], out_sems, 6 + chunk)
    finish(*gone)


def mixer_backward_kernel(
    core_ref,
    mixgrad_hbm,
    own_hbm,
    mate_hbm,
    qkv_hbm,
    lse_hbm,
    aux_hbm,
    rope_hbm,
    proj_hbm,
    states_hbm,
    normed_hbm,
    segrow_ref,
    par_ref,
    second_ref,
    ngrad_hbm,
    dproj_hbm,
    small_ref,
    mixgrad_ref,
    w_ref,
    qkv_ref,
    lse_ref,
    aux_ref,
    rope_ref,
    proj_ref,
    states_ref,
    normed_ref,
    mix_ref,
    dproj_ref,
    d_ref,
    dkv_ref,
    in_sems,
    out_sems,
):
    first_come = begin([(mixgrad_hbm, mixgrad_ref)], in_sems, 0)
    first_come += join_cores(core_ref[0], own_hbm, mate_hbm, w_ref, in_sems, 1)
    come = begin(
        [
            (qkv_hbm, qkv_ref),
            (lse_hbm, lse_ref),
            (aux_hbm, aux_ref),
            (rope_hbm, rope_ref),
            (proj_hbm, proj_ref),
            (states_hbm, states_ref),
            (normed_hbm, normed_ref),
        ],
        in_sems,
        3,
    )
    finish(*first_come)
    gone = []
    w2 = columns(w_ref, SENT, WIDE)
    for first in range(0, TOKENS, 256):
        rows = slice(first, first + 256)
        d_ref[rows, :] = dot(mixgrad_ref[rows, :], w2)
    lane = iota((QUERY_BLOCK, 128), 1)
    dkv_ref[...] = jnp.zeros_like(dkv_ref)
    finish(*come[0:3])
    for first in range(0, TOKENS, QUERY_BLOCK):
        rows = slice(first, first + QUERY_BLOCK)
        count = first + QUERY_BLOCK
        queries, keys = (qkv_ref[rows, 0:128], qkv_ref[0:count, 128:256])
        out_grad = jnp.where(lane >= 64, d_ref[rows, 128:256], 0.0).astype(BF16)
        scores = dot_right(queries, keys) - lse_ref[rows, 0:1]
        weights = jnp.exp(
            jnp.where(allowed_keys(aux_ref, segrow_ref, first, count), scores, MASKED)
        )
        weight_grad = dot_right(out_grad, qkv_ref[0:count, 256:384])
        mean = jnp.sum(weights * weight_grad, axis=1, keepdims=True)
        score_grad = (weights * (weight_grad - mean)).astype(BF16)
        query_grad = dot(score_grad, keys) * AHDIM**-0.5
        d_ref[rows, 128:256] = jnp.where(
            lane < 64, d_ref[rows, 128:256], pltpu.roll(query_grad, 64, 1)
        )
        dkv_ref[0:count, 0:128] += dot_left(score_grad, queries)
        dkv_ref[0:count, 128:256] += dot_left(weights.astype(BF16), out_grad)
    finish(come[3])
    for first in range(0, TOKENS, 256):
        rows = slice(first, first + 256)
        rope = rope_ref[rows, :]
        query_grad = turn_halves(pltpu.roll(d_ref[rows, 128:256], 64, 1), rope, True)
        dproj_ref[rows, 384:512] = query_grad.astype(BF16)
        key_grad = turn_halves(dkv_ref[rows, 0:128], rope, True)
        keyval_grad = jnp.where(lane < 64, key_grad, dkv_ref[rows, 128:256])
        dproj_ref[rows, 256:384] = keyval_grad.astype(BF16)

    spread, gather = head_matrices()
    row, column = (iota((BLOCK, BLOCK), 0), iota((BLOCK, BLOCK), 1))
    causal = row >= column
    lower = causal.astype(BF16)
    upper = (row <= column).astype(BF16)
    strict = (row > column).astype(BF16)
    real = iota((BLOCK, 256), 1) < INNER
    head_lane = iota((BLOCK, 128), 1)

    def block_step(turn, carried):
        state_grad, later, taps_sum, head_sum, skip_sum = carried
        start = pl.multiple_of((BLOCKS - 1 - turn) * BLOCK, BLOCK)
        rows = pl.ds(start, BLOCK)
        aux = aux_ref[rows, :]
        lagged, pre = conv_parts(proj_ref, par_ref, aux, start)
        sig = sigmoid(pre)
        conv = (pre * sig).astype(BF16)
        in_map, out_map, inner = (conv[:, 0:128], conv[:, 128:256], conv[:, 256:512].astype(F32))
        raw, is_head, step, rate, total, reach, to_end = step_parts(
            proj_ref, par_ref, aux, lower, start
        )
        wide = times_ones(jnp.concatenate([step, reach, to_end], axis=0), spread)
        step_wide, reach_wide, end_wide = (wide[0:128], wide[128:256], wide[256:384])
        stepped = inner * step_wide
        stepped_low = stepped.astype(BF16)
        keep = causal & (aux[:, 0:1] == segrow_ref[0:1, pl.ds(start, BLOCK)])
        total_rows = jnp.transpose(total)
        shared = dot_right(out_map, in_map)
        decays = [decay_of(total, total_rows, keep, h) for h in range(HEADS)]
        mixing = [(decay * shared).astype(BF16) for decay in decays]
        state = states_ref[rows, :]
        state_low = state.astype(BF16)
        incoming = dot(out_map, state_low) * reach_wide
        result = dot(jnp.concatenate(mixing, axis=1), per_head(stepped).astype(BF16)) + incoming
        result = result + inner * par_ref[10:11, 0:256]

        gate = proj_ref[rows, GATE_AT:QS_AT]
        gate_sig = sigmoid(gate)
        gated_grad = jnp.where(real, d_ref[rows, :], 0.0)
        gate_grad = gated_grad * result * (gate_sig * (1.0 + gate * (1.0 - gate_sig)))
        out_grad = gated_grad * (gate * gate_sig)
        by_head = per_head(out_grad).astype(BF16)

        mixing_grad = dot_right(by_head, stepped_low)
        shared_grad = jnp.zeros((BLOCK, BLOCK), F32)
        edges = []
        for h in range(HEADS):
            decayed = mixing_grad[h * BLOCK : (h + 1) * BLOCK] * decays[h]
            shared_grad = shared_grad + decayed
            edges.append((decayed * shared).astype(BF16))
        crossing = dot(upper, jnp.concatenate(edges, axis=1))
        rate_grad = jnp.zeros((BLOCK, 128), F32)
        for h in range(HEADS):
            part = jnp.where(row > column, crossing[:, h * BLOCK : (h + 1) * BLOCK], 0.0)
            part = jnp.sum(part, axis=1, keepdims=True)
            rate_grad = rate_grad + jnp.where(head_lane == STEP_LANE + h, part, 0.0)

        reached = (out_grad * reach_wide).astype(BF16)
        state_grad_low = state_grad.astype(BF16)
        ended = dot(in_map, state_grad_low) * end_wide
        mapped = dot_left(jnp.concatenate(mixing, axis=0), by_head) + ended
        inner_grad = mapped * step_wide + out_grad * par_ref[10:11, 0:256]
        kept = jnp.sum(state_grad * state, axis=0, keepdims=True)
        kept = jnp.broadcast_to(kept * reach_wide[BLOCK - 1 : BLOCK, :], (8, 256))
        sums = times_ones(
            jnp.concatenate([inner * mapped, out_grad * incoming, stepped * ended, kept], axis=0),
            gather,
        )
        flows = ones_times(
            jnp.concatenate([upper, strict], axis=1), sums[128:384]
        )
        rate_grad = rate_grad + flows + sums[384:385]
        step_grad = sums[0:128] - jnp.exp(par_ref[9:10, 0:128]) * rate_grad
        step_grad = jnp.where(is_head, step_grad * sigmoid(raw), 0.0)
        dproj_ref[rows, 384:512] = dproj_ref[rows, 384:512] + step_grad.astype(BF16)
        head_sum = head_sum + jnp.concatenate(
            [
                jnp.sum(jnp.where(is_head, rate_grad * rate, 0.0), axis=0, keepdims=True),
                jnp.sum(step_grad, axis=0, keepdims=True),
                jnp.zeros((6, 128), F32),
            ],
            axis=0,
        )
        skip_sum = skip_sum + jnp.sum(inner * out_grad, axis=0, keepdims=True)

        shared_low = shared_grad.astype(BF16)
        out_map_grad = dot(shared_low, in_map) + dot_right(reached, state_low)
        in_map_grad = dot_left(shared_low, out_map) + dot_right(
            (stepped * end_wide).astype(BF16), state_grad_low
        )
        conv_grad = jnp.concatenate([in_map_grad, out_map_grad, inner_grad], axis=1)
        pre_grad = conv_grad * (sig * (1.0 + pre * (1.0 - sig)))
        taps_sum = taps_sum + jnp.concatenate(
            [jnp.sum(pre_grad * lagged[lag], axis=0, keepdims=True) for lag in range(4)]
            + [jnp.zeros((4, CONV_WIDTH), F32)],
            axis=0,
        )
        both = jnp.concatenate([pre_grad, later], axis=0)
        masks = aux_ref[pl.ds(start, BLOCK + 8), :]
        u_grad = pre_grad * par_ref[0:1, :]
        for lag in range(1, 4):
            shifted = (both * masks[:, lag : lag + 1])[lag : lag + BLOCK]
            u_grad = u_grad + shifted * par_ref[lag : lag + 1, :]
        dproj_ref[rows, 0:256] = u_grad[:, 0:256].astype(BF16)
        inner = jnp.concatenate([u_grad[:, 256 : 256 + INNER], gate_grad[:, 0:INNER]], axis=1)
        dproj_ref[rows, 512:SENT] = inner.astype(BF16)
        state_grad = state_grad * reach_wide[BLOCK - 1 : BLOCK, :] + dot_left(out_map, reached)
        return (state_grad, pre_grad[0:8], taps_sum, head_sum, skip_sum)

    carried = (
        jnp.zeros((BLOCK, 256), F32),
        jnp.zeros((8, CONV_WIDTH), F32),
        jnp.zeros((8, CONV_WIDTH), F32),
        jnp.zeros((8, 128), F32),
        jnp.zeros((1, 256), F32),
    )
    finish(*come[4:6])
    _, _, taps_sum, head_sum, skip_sum = lax.fori_loop(
        0, BLOCKS, block_step, carried, unroll=UNROLL
    )
    gone += begin([(dproj_ref, dproj_hbm)], out_sems, 0)
    finish(come[6])
    gain = jnp.zeros((1, WIDTH), F32)
    w1 = columns(w_ref, 0, SENT)
    for chunk in range(4):
        rows = slice(256 * chunk, 256 * chunk + 256)
        grad = dot_right(dproj_ref[rows, :], w1)
        mix_ref[rows, :] = grad.astype(BF16)
        gone += begin([(mix_ref.at[rows, :], ngrad_hbm.at[rows, :])], out_sems, 1 + chunk)
        normed = normed_ref[2 * chunk : 2 * chunk + 2].reshape(256, WIDTH)
        gain = gain + jnp.sum(grad * normed.astype(F32), axis=0, keepdims=True)
    upper_rows = jnp.concatenate([taps_sum[0:4, 0:256], taps_sum[0:4, 256:512]], axis=0)
    upper_rows = jnp.concatenate([upper_rows, fold(gain)], axis=1)
    skip_rows = jnp.concatenate([skip_sum, jnp.zeros((7, 256), F32)], axis=0)
    lower_rows = jnp.concatenate([fold(second_ref[0:1, :]), head_sum[:, 64:128], skip_rows[:, 0:INNER]], axis=1)
    small = jnp.concatenate([upper_rows, lower_rows], axis=0)
    small_ref[...] = small
    finish(*gone)


def feed_kernel(
    core_ref, n0, n1, n2, n3, c0, c1, c2, c3, own_hbm, mate_hbm,
    o0, o1, o2, o3, g0, g1, g2, g3, act_ref, grads_ref, gain_ref, w_ref, sems,
):
    finish(*join_cores(core_ref[0], own_hbm, mate_hbm, w_ref, sems, 0))
    inputs = ((n0, n1, c0, c1), (n2, n3, c2, c3))
    outs = (((o0, g0), (o1, g1)), ((o2, g2), (o3, g3)))
    gain = jnp.zeros((1, WIDTH), F32)
    for j in range(2):
        rows = slice(256 * j, 256 * j + 256)
        normed = jnp.concatenate([inputs[j][0][...], inputs[j][1][...]], axis=0)
        cot = jnp.concatenate([inputs[j][2][...], inputs[j][3][...]], axis=0)
        out_sum, grad_sum = (0.0, 0.0)
        for h in range(2):
            up_weights = columns(w_ref.at[h], 0, 512)
            down = columns(w_ref.at[h], 512, 768)
            both = dot(normed, up_weights)
            gate, up = (both[:, 0:FEED], both[:, FEED:])
            sig = sigmoid(gate)
            silu = gate * sig
            act = (silu * up).astype(BF16)
            act_ref[rows, h * FEED : (h + 1) * FEED] = act
            out_sum = out_sum + dot_right(act, down)
            act_grad = dot(cot, down)
            gate_grad = (act_grad * up * (sig + silu * (1.0 - sig))).astype(BF16)
            up_grad = (act_grad * silu).astype(BF16)
            grads = jnp.concatenate([gate_grad, up_grad], axis=1)
            grads_ref[rows, h * 512 : (h + 1) * 512] = grads
            grad_sum = grad_sum + dot_right(grads, up_weights)
        gain = gain + jnp.sum(grad_sum * normed.astype(F32), axis=0, keepdims=True)
        out_low, grad_low = (out_sum.astype(BF16), grad_sum.astype(BF16))
        for half in range(2):
            part = slice(half * BLOCK, (half + 1) * BLOCK)
            outs[j][half][0][...] = out_low[part]
            outs[j][half][1][...] = grad_low[part]
    gain_ref[...] = jnp.broadcast_to(gain, (8, WIDTH))


def feed_weights_kernel(
    core_ref, n0, n1, n2, n3, c0, c1, c2, c3, act_ref, grads_ref, keep_hbm, send_hbm, out_ref, sems
):
    normed = jnp.concatenate([r[...] for r in (n0, n1, n2, n3)], axis=0)
    cot = jnp.concatenate([r[...] for r in (c0, c1, c2, c3)], axis=0)
    up = dot_left(normed, grads_ref[...]).astype(BF16)
    down = dot_left(cot, act_ref[...]).astype(BF16)
    for h in range(2):
        up_here = up[:, h * 512 : (h + 1) * 512].reshape(8, 2, 64, 512)
        down_here = down[:, h * FEED : (h + 1) * FEED].reshape(8, 2, 64, FEED)
        out_ref[h, :, :, :, 0:512] = up_here
        out_ref[h, :, :, :, 512:768] = down_here
    finish(*split_cores(core_ref[0], out_ref, keep_hbm, send_hbm, sems, 0))


def mixer_weights_kernel(
    core_ref, normed_ref, dproj_ref, mixgrad_ref, heads_ref, keep_hbm, send_hbm, out_ref, sems
):
    normed = normed_ref[...].reshape(TOKENS, WIDTH)
    for first, last in ((0, 512), (512, SENT)):
        grad = dot_left(normed, dproj_ref[:, first:last]).astype(BF16)
        out_ref[:, :, :, first:last] = grad.reshape(8, 2, 64, last - first)
    grad = dot_left(mixgrad_ref[...], heads_ref[...]).astype(BF16)
    out_ref[:, :, :, SENT:WIDE] = grad.reshape(8, 2, 64, WIDE - SENT)
    finish(*split_cores(core_ref[0], out_ref, keep_hbm, send_hbm, sems, 0))


def mixer_pair_kernel(keep_ref, come_ref, small_ref, small_come_ref, out_ref):
    total = keep_ref[...].astype(F32) + come_ref[...].astype(F32)
    small = small_ref[...] + small_come_ref[...]
    high = small.astype(BF16)
    low = (small - high.astype(F32)).astype(BF16)
    tail = jnp.concatenate([high, low, jnp.zeros_like(high)], axis=1)
    for i in range(8):
        out_ref[i, 0:64, :] = total[i].astype(BF16)
        out_ref[i, 64:, :] = tail


def feed_pair_kernel(keep_ref, come_ref, out_ref):
    out_ref[...] = (keep_ref[...].astype(F32) + come_ref[...].astype(F32)).astype(BF16)


def collect_kernel(
    core_ref, blocks_ref, lines_ref, gate_ref, input_ref, step_ref, query_ref, mamba_ref, attend_ref,
    own_ref,
):
    total = total_rows(blocks_ref)
    own = total[64:, 0:EARLY] + total[64:, EARLY : 2 * EARLY]
    total = total[0:64]
    keyval = total[:, 256:384]
    turned = pltpu.roll(keyval, AHDIM, 1)
    low = iota(keyval.shape, 1) < AHDIM
    first = core_ref[1] == 0
    keys = jnp.where(first, jnp.where(low, keyval, 0.0), jnp.where(low, 0.0, turned))
    values = jnp.where(first, jnp.where(low, turned, 0.0), jnp.where(low, 0.0, keyval))
    shared = jnp.concatenate([total[:, 0:256], keys, values], axis=1)
    for t in range(8):
        lines_ref[t, 0:8, :] = shared[8 * t : 8 * t + 8]
        lines_ref[t, 8:24, 0:EARLY] = own
        lines_ref[t, 8:24, EARLY:] = jnp.zeros((16, 512 - EARLY), F32)
    own_ref[...] = own
    query_ref[...] = total[:, EARLY : EARLY + AHDIM]
    step_ref[...] = total[:, EARLY + STEP_LANE : EARLY + STEP_LANE + HEADS]
    input_ref[...] = total[:, 512 : 512 + INNER]
    gate_ref[...] = total[:, 512 + INNER : SENT]
    turned = jnp.transpose(total[:, SENT:WIDE])
    mamba_ref[...] = turned[0:INNER]
    attend_ref[...] = turned[INNER:]


def last_kernel(
    lines_ref, gain_one_ref, gain_two_ref, state_ref, keyval_ref, taps_ref, first_ref, second_ref
):
    pairs = [lines_ref[2 * t] + lines_ref[2 * t + 1] for t in range(4)]
    total = (pairs[0] + pairs[1]) + (pairs[2] + pairs[3])
    state_ref[...] = total[0:8, 0:256]
    keyval_ref[...] = total[0:8, 256:512]
    taps_ref[...] = total[8:12, 0:256]
    first_ref[...] = total[8:16, 256:384] / gain_one_ref[...]
    second_ref[...] = total[16:24, 0:128] / gain_two_ref[...]


def total_of(pieces):
    return sum(piece[...].astype(F32) for piece in pieces)


def total_rows(blocks_ref):
    return sum(blocks_ref[i].astype(F32) for i in range(8))


def row_norm(values):
    return lax.rsqrt(jnp.mean(values * values, axis=-1, keepdims=True) + NORM_EPS)


def norm_back(values, gain, grad):
    scale = row_norm(values)
    scaled = grad * gain
    return scale * scaled - values * (
        scale**3 * jnp.mean(scaled * values, axis=-1, keepdims=True)
    )


def first_norm_kernel(x_ref, gain_ref, normed_ref):
    x = x_ref[...].astype(F32)
    normed_ref[...] = (x * row_norm(x) * gain_ref[...]).astype(BF16)


def second_norm_kernel(x_ref, gain_ref, blocks_ref, hidden_ref, normed_ref):
    hidden = x_ref[...].astype(F32) + total_rows(blocks_ref)
    hidden_ref[...] = hidden
    normed_ref[...] = (hidden * row_norm(hidden) * gain_ref[...]).astype(BF16)


def hidden_grad_kernel(hidden_ref, gain_ref, cot_ref, s0, s1, s2, s3, grad_ref, low_ref):
    back = norm_back(hidden_ref[...], gain_ref[...], total_of((s0, s1, s2, s3)))
    grad = cot_ref[...].astype(F32) + back
    grad_ref[...] = grad
    low = grad.astype(BF16)
    for i in range(8):
        low_ref[i] = low


def input_grad_kernel(x_ref, gain_ref, hidden_grad_ref, blocks_ref, grad_ref):
    x = x_ref[...].astype(F32)
    back = norm_back(x, gain_ref[...], total_rows(blocks_ref))
    grad_ref[...] = hidden_grad_ref[...] + back


def output_kernel(hidden_ref, s0, s1, s2, s3, out_ref):
    out_ref[...] = (hidden_ref[...] + total_of((s0, s1, s2, s3))).astype(BF16)


def like(dtype, *shape):
    return jax.ShapeDtypeStruct(shape, dtype)


VMEM = pl.BlockSpec(memory_space=pltpu.VMEM)
SMEM = pl.BlockSpec(memory_space=pltpu.SMEM)
ANY = pl.BlockSpec(memory_space=pl.ANY)


def run(kernel, name, outs, args, specs=None, scratch=(), us=0.05, out_specs=None):
    return pl.pallas_call(
        kernel,
        in_specs=specs or [VMEM] * len(args),
        out_specs=out_specs or [VMEM] * len(outs),
        out_shape=list(outs),
        scratch_shapes=list(scratch),
        compiler_params=pltpu.CompilerParams(vmem_limit_bytes=VMEM_BYTES),
        cost_estimate=pl.CostEstimate(
            flops=int(us * 1e9), transcendentals=0, bytes_accessed=int(us * 2e6)
        ),
        name=name,
    )(*args)


def held(array):
    return pltpu.VMEM(array.shape, array.dtype)


HERE = (BLOCK, WIDTH)
UNROLL = 2
FORWARD_US = 20
BACKWARD_US = 33
ROW = (8, BLOCK, WIDTH)


def mixer_forward(core, pieces, own, mate, aux, segrow, pack, rope):
    outs = (
        like(BF16, *ROW),
        like(BF16, TOKENS, WIDTH),
        like(F32, TOKENS, PACKED),
        like(F32, TOKENS, 256),
        like(BF16, TOKENS, 384),
        like(F32, TOKENS, 128),
        like(BF16, TOKENS, 256),
    )
    return run(
        mixer_forward_kernel,
        "mixer_forward",
        outs,
        (core, *pieces, own, mate, rope, aux, segrow, pack),
        [SMEM] + [ANY] * 12 + [VMEM] * 2,
        [pltpu.VMEM(ROW, BF16), pltpu.VMEM((8, 2, 64, WIDE), BF16), held(rope), held(aux)]
        + [held(a) for a in outs[1:]]
        + [pltpu.SemaphoreType.DMA((n,)) for n in (12, 11)],
        FORWARD_US,
        [ANY] * 7,
    )


def mixer_backward(
    core, mix_grad, own, mate, normed, aux, segrow, pack, rope, proj, states, qkv, lse, second
):
    outs = (like(BF16, TOKENS, WIDTH), like(BF16, TOKENS, SENT), like(F32, 16, EARLY))
    moved = (qkv, lse, aux, rope, proj, states)
    return run(
        mixer_backward_kernel,
        "mixer_backward",
        outs,
        (core, mix_grad, own, mate, *moved, normed, segrow, pack, second),
        [SMEM] + [ANY] * 10 + [VMEM] * 3,
        [held(mix_grad), pltpu.VMEM((8, 2, 64, WIDE), BF16)]
        + [held(a) for a in moved]
        + [pltpu.VMEM(ROW, BF16)]
        + [held(a) for a in outs[0:2]]
        + [pltpu.VMEM((TOKENS, 256), F32), pltpu.VMEM((TOKENS, 256), F32)]
        + [pltpu.SemaphoreType.DMA((n,)) for n in (10, 5)],
        BACKWARD_US,
        [ANY] * 2 + [VMEM],
    )


def feed_forward_backward(core, normed, cot, weights):
    return run(
        feed_kernel,
        "feed",
        [like(BF16, *HERE)] * 8
        + [like(BF16, 512, 2 * FEED), like(BF16, 512, 4 * FEED), like(F32, 8, WIDTH)],
        (core, *normed, *cot, *weights),
        [SMEM] + [VMEM] * 8 + [ANY] * 2,
        [pltpu.VMEM((2, 8, 2, 64, 768), BF16), pltpu.SemaphoreType.DMA((2,))],
    )


def aux_arrays(seg):
    columns = [seg]
    for lag in range(1, 4):
        earlier = jnp.concatenate([jnp.full((lag,), -1.0, F32), seg[: TOKENS - lag]])
        columns.append((earlier == seg).astype(F32))
    ends = seg.reshape(BLOCKS, BLOCK)[:, -1]
    before = jnp.concatenate([jnp.full((1,), -1.0, F32), ends[:-1]])
    columns.append((seg == jnp.repeat(before, BLOCK)).astype(F32))
    columns.append((seg == jnp.repeat(ends, BLOCK)).astype(F32))
    aux = jnp.pad(jnp.stack(columns, axis=1), ((0, 8), (0, 128 - len(columns))))
    return (aux, jnp.broadcast_to(seg, (8, TOKENS)))


def rope_arrays():
    half = AHDIM // 2
    freq = (ROPE_BASE ** (-2.0 * np.arange(half) / AHDIM)).astype(np.float32)
    angles = np.arange(TOKENS, dtype=np.float32)[:, None] * freq[None, :]
    cosine, sine = (np.cos(angles.astype(np.float64)), np.sin(angles.astype(np.float64)))
    none = np.zeros_like(sine)
    parts = [cosine, cosine, none, none, -sine, none, none, none, none, sine, none, none]
    return jnp.asarray(np.concatenate(parts, axis=1).astype(np.float32))


def pad_columns(values, width, before=0):
    return jnp.pad(values, ((0, 0), (before, width - before - values.shape[1])))


def index_of(axes):
    return lax.axis_index(axes)


def exchange(values, axes, turn):
    size = 2 ** len(axes)
    return lax.ppermute(values, axes, [(i, turn(i)) for i in range(size)])


def other_core(values):
    return exchange(values, ("c",), lambda i: i ^ 1)


def near_gather(shard):
    return [shard] + near_return([shard] * 4)


def near_return(pieces):
    return [exchange(pieces[j], NEAR, lambda i, j=j: i ^ j) for j in range(1, 4)]


def spread_blocks(shard, axes):
    copies = jnp.broadcast_to(shard, (2 ** len(axes), *shard.shape))
    return turn_blocks(copies, axes)


def turn_blocks(blocks, axes):
    return lax.all_to_all(blocks, axes, split_axis=0, concat_axis=0, tiled=True)


def sum_blocks(blocks):
    return jnp.sum(blocks.astype(F32), axis=0)


def body(
    block_input,
    segments,
    first_gain,
    mamba_gate,
    mamba_input,
    step_weight,
    state_weight,
    conv_inner,
    conv_state,
    decay_log,
    step_bias,
    skip_scale,
    query_weight,
    keyval_weight,
    mamba_out,
    attention_out,
    second_gain,
    feed_gate,
    feed_up,
    feed_down,
    cotangent,
):
    kv_head = lax.axis_index("yh")
    core = jnp.stack([lax.axis_index("c"), kv_head, lax.axis_index(TENSOR)]).astype(jnp.int32)
    x, cot = (block_input[0], cotangent[0])
    gain_one, gain_two = (first_gain[None], second_gain[None])
    shared = spread_blocks(jnp.concatenate([state_weight, keyval_weight], axis=1), TENSOR)
    shared = shared.reshape(-1, 512)
    (normed_here,) = run(first_norm_kernel, "first_norm", [like(BF16, *HERE)], (x, gain_one))
    normed_pieces = [normed_here] + [
        exchange(normed_here, TENSOR, lambda i, k=k: i ^ k) for k in range(1, 8)
    ]
    pack = jnp.concatenate(
        [
            jnp.concatenate([conv_state, pad_columns(conv_inner, 256)], axis=1),
            jnp.zeros((4, 512), F32),
            pad_columns(step_bias[None], 512, STEP_LANE),
            pad_columns(decay_log[None], 512, STEP_LANE),
            pad_columns(jnp.repeat(skip_scale, HDIM)[None], 512),
            jnp.zeros((5, 512), F32),
        ],
        axis=0,
    )
    aux, segrow = aux_arrays(segments.reshape(TOKENS).astype(F32))
    rope = rope_arrays()

    feed_here = jnp.concatenate([feed_gate, feed_up, feed_down.T], axis=1)
    feed_copies = jnp.broadcast_to(feed_here, (16, *feed_here.shape))
    share_rows = shared.shape[0]
    key_part = lax.dynamic_slice(shared, (0, 256 + kv_head * AHDIM), (share_rows, AHDIM))
    value_part = lax.dynamic_slice(
        shared, (0, 256 + (KVHEADS + kv_head) * AHDIM), (share_rows, AHDIM)
    )
    main_here = jnp.concatenate(
        [
            shared[:, 0:256],
            key_part,
            value_part,
            query_weight,
            pad_columns(step_weight, 64),
            mamba_input,
            mamba_gate,
            mamba_out.T,
            attention_out.T,
        ],
        axis=1,
    )
    own = spread_blocks(main_here, CHIPS)
    mate = other_core(own)

    own, feed_copies, aux, segrow, pack = lax.optimization_barrier(
        (own, feed_copies, aux, segrow, pack)
    )
    feed_own = turn_blocks(feed_copies, FEED16).reshape(2, 8, share_rows, 768)

    normed, mix, proj, states, qkv, lse, heads = mixer_forward(
        core, normed_pieces, own, mate, aux, segrow, pack, rope
    )
    mix, feed_own, cot_here = lax.optimization_barrier((mix, feed_own, cot))
    feed_weights = (feed_own, other_core(feed_own))
    mix_blocks, *cot_pieces = lax.optimization_barrier(
        (turn_blocks(mix.reshape(ROW), TENSOR), *near_gather(cot_here))
    )
    hidden, normed_two_here = run(
        second_norm_kernel,
        "second_norm",
        [like(F32, *HERE), like(BF16, *HERE)],
        (x, gain_two, mix_blocks),
    )
    normed_two = near_gather(normed_two_here)
    *parts, act, feed_grads, second_part = feed_forward_backward(
        core, normed_two, cot_pieces, feed_weights
    )
    feed_keep, feed_send = run(
        feed_weights_kernel,
        "feed_weights",
        [like(BF16, 2, 8, share_rows, 768)] * 2,
        (core, *normed_two, *cot_pieces, act, feed_grads),
        [SMEM] + [VMEM] * 10,
        [pltpu.VMEM((2, 8, 2, 64, 768), BF16), pltpu.SemaphoreType.DMA((2,))],
        out_specs=[ANY] * 2,
    )
    sums = near_return(parts[4:8])
    hidden, feed_keep, feed_send, *sums = lax.optimization_barrier(
        (hidden, feed_keep, feed_send, *sums)
    )
    hidden_grad, mix_grad_copies = run(
        hidden_grad_kernel,
        "hidden_grad",
        [like(F32, *HERE), like(BF16, *ROW)],
        (hidden, gain_two, cot, parts[4], *sums),
    )
    (feed_pair,) = run(
        feed_pair_kernel,
        "feed_pair",
        [like(BF16, 2, 8, share_rows, 768)],
        (feed_keep, other_core(feed_send)),
    )
    mix_grad = turn_blocks(mix_grad_copies, TENSOR).reshape(TOKENS, WIDTH)
    feed_pair, mix_grad = lax.optimization_barrier((feed_pair, mix_grad))
    feed_blocks = turn_blocks(feed_pair.reshape(16, share_rows, 768), FEED16)

    normed_grad, dproj, small = mixer_backward(
        core, mix_grad, own, mate, normed, aux, segrow, pack, rope, proj, states, qkv, lse,
        second_part,
    )
    normed_grad, feed_blocks, *out_sums = lax.optimization_barrier(
        (normed_grad, feed_blocks, *near_return(parts[0:4]))
    )
    input_blocks = turn_blocks(normed_grad.reshape(ROW), TENSOR)
    keep, send = run(
        mixer_weights_kernel,
        "mixer_weights",
        [like(BF16, 8, share_rows, WIDE)] * 2,
        (core, normed, dproj, mix_grad, heads),
        [SMEM] + [VMEM] * 4,
        [pltpu.VMEM((8, 2, 64, WIDE), BF16), pltpu.SemaphoreType.DMA((2,))],
        out_specs=[ANY] * 2,
    )
    (pair,) = run(
        mixer_pair_kernel,
        "mixer_pair",
        [like(BF16, 8, share_rows + 16, WIDE)],
        (keep, other_core(send), small, other_core(small)),
    )
    pair, input_blocks = lax.optimization_barrier((pair, input_blocks))
    (block_out,) = run(
        output_kernel, "output", [like(BF16, *HERE)], (hidden, parts[0], *out_sums)
    )
    blocks = turn_blocks(pair, CHIPS)
    (input_grad,) = run(
        input_grad_kernel,
        "input_grad",
        [like(F32, *HERE)],
        (x, gain_one, hidden_grad, input_blocks),
    )
    feed_total = sum_blocks(feed_blocks)
    lines, gate_sum, input_sum, step_sum, query_sum, mamba_sum, attend_sum, own = run(
        collect_kernel,
        "collect",
        [
            like(F32, 8, 24, 512),
            like(F32, share_rows, INNER),
            like(F32, share_rows, INNER),
            like(F32, share_rows, HEADS),
            like(F32, share_rows, AHDIM),
            like(F32, INNER, share_rows),
            like(F32, AHDIM, share_rows),
            like(F32, 16, EARLY),
        ],
        (core, blocks),
        [SMEM, VMEM],
    )
    state_sum, keyval_sum, state_taps, first_sum, second_sum = run(
        last_kernel,
        "last",
        [
            like(F32, 8, 256),
            like(F32, 8, 256),
            like(F32, 4, 256),
            like(F32, 8, 128),
            like(F32, 8, 128),
        ],
        (turn_blocks(lines, TENSOR), first_gain.reshape(8, 128), second_gain.reshape(8, 128)),
    )
    return (
        block_out[None],
        input_grad[None],
        first_sum.reshape(-1),
        gate_sum,
        input_sum,
        step_sum,
        state_sum,
        own[4:8, 0:INNER],
        state_taps,
        own[8, 128 : 128 + HEADS],
        own[9, 128 : 128 + HEADS],
        jnp.sum(own[8, INNER : 2 * INNER].reshape(HEADS, HDIM), axis=1),
        query_sum,
        keyval_sum,
        mamba_sum,
        attend_sum,
        second_sum.reshape(-1),
        feed_total[:, 0:256],
        feed_total[:, 256:512],
        feed_total[:, 512:768].T,
    )


def solution(mesh):
    DP, TP = (("zlo", "xh", "xl", "c"), ("yh", "yl", "zhi"))
    fine = jax.sharding.Mesh(mesh.devices.reshape(FINE_SIZES), (*DP, *TP))
    in_specs = (
        P(DP, TP, None),
        P(DP, None),
        P(),
        P(DP, TP),
        P(DP, TP),
        P(DP, TP),
        P((*DP, *TP), None),
        P(None, TP),
        P(),
        P(TP),
        P(TP),
        P(TP),
        P(DP, TP),
        P((*DP, *TP), None),
        P(TP, DP),
        P(TP, DP),
        P(),
        P(DP, TP),
        P(DP, TP),
        P(TP, DP),
        P(DP, TP, None),
    )
    out_specs = (
        P(DP, TP, None),
        P(DP, TP, None),
        P(),
        P(DP, TP),
        P(DP, TP),
        P(DP, TP),
        P((*DP, *TP), None),
        P(None, TP),
        P(),
        P(TP),
        P(TP),
        P(TP),
        P(DP, TP),
        P((*DP, *TP), None),
        P(TP, DP),
        P(TP, DP),
        P(),
        P(DP, TP),
        P(DP, TP),
        P(TP, DP),
    )
    return jax.shard_map(body, mesh=fine, in_specs=in_specs, out_specs=out_specs, check_vma=False)
```

```python
import jax
import jax.numpy as jnp
import numpy as np
from jax import lax
from jax.experimental import pallas as pl
from jax.experimental.pallas import tpu as pltpu
from jax.sharding import PartitionSpec as P

QHEADS = 8
KVHEADS = 2
AHDIM = 64
TOKENS = 1024
WIDTH = 1024
BLOCK = 128
BLOCKS = TOKENS // BLOCK
HEADS = 3
HDIM = 64
INNER = HEADS * HDIM
FEED = 256
QUERY_BLOCK = 256
NORM_EPS = 1e-05
ROPE_BASE = 10000.0
MASKED = -1e30
VMEM_BYTES = 60 * 1024 * 1024

KV_AT = 0
CONV_AT = 128
GATE_AT = 640
QS_AT = 896
PACKED = 1024
EARLY = 384
SENT = 896
PAYLOAD = 32
CONV_WIDTH = 512
STEP_LANE = 64

CHIPS = ("zlo", "xh", "xl")
FEED16 = ("yh", *CHIPS)
TENSOR = ("yh", "yl", "zhi")
NEAR = ("yl", "zhi")
PIECE = BLOCK + 16
WIDE = 1152
FINE_SIZES = (2,) * 7

F32 = jnp.float32
BF16 = jnp.bfloat16


def dot(a, b):
    return lax.dot_general(a, b, (((1,), (0,)), ((), ())), preferred_element_type=F32)


def dot_right(a, b):
    return lax.dot_general(a, b, (((1,), (1,)), ((), ())), preferred_element_type=F32)


def dot_left(a, b):
    return lax.dot_general(a, b, (((0,), (0,)), ((), ())), preferred_element_type=F32)


def parts_of(values, terms):
    parts = []
    for _ in range(terms - 1):
        part = values.astype(BF16)
        parts.append(part)
        values = values - part.astype(F32)
    parts.append(values.astype(BF16))
    return parts


def times_ones(values, ones, terms=2):
    return sum(dot(part, ones) for part in parts_of(values, terms))


def ones_times(ones, values, terms=2):
    return sum(dot(ones, part) for part in parts_of(values, terms))


def iota(shape, dim):
    return lax.broadcasted_iota(jnp.int32, shape, dim)


def softplus(v):
    return jnp.maximum(v, 0.0) + jnp.log1p(jnp.exp(-jnp.abs(v)))


def sigmoid(v):
    return 1.0 / (1.0 + jnp.exp(-v))


def head_matrices():
    lane, channel = (iota((BLOCK, 256), 0), iota((BLOCK, 256), 1))
    spread = ((channel >> 6) + STEP_LANE == lane) & (channel < INNER)
    lane, channel = (iota((256, BLOCK), 1), iota((256, BLOCK), 0))
    gather = ((channel >> 6) + STEP_LANE == lane) & (channel < INNER)
    return (spread.astype(BF16), gather.astype(BF16))


def per_head(values):
    of_head = iota(values.shape, 1) >> 6
    return jnp.concatenate(
        [jnp.where(of_head == h, values, jnp.zeros_like(values)) for h in range(HEADS)], axis=0
    )


def conv_parts(proj_ref, par_ref, aux, start):
    here = proj_ref[pl.ds(start, BLOCK), CONV_AT:GATE_AT]
    before = proj_ref[pl.ds(pl.multiple_of(jnp.maximum(start - 8, 0), 8), 8), CONV_AT:GATE_AT]
    both = jnp.concatenate([before, here], axis=0)
    lagged = [here]
    for lag in range(1, 4):
        lagged.append(both[8 - lag : 8 - lag + BLOCK] * aux[:, lag : lag + 1])
    pre = sum(lagged[lag] * par_ref[lag : lag + 1, :] for lag in range(4))
    return (lagged, pre)


def step_parts(proj_ref, par_ref, aux, lower, start):
    raw = proj_ref[pl.ds(start, BLOCK), QS_AT:PACKED] + par_ref[8:9, 0:128]
    lane = iota((BLOCK, 128), 1)
    is_head = (lane >= STEP_LANE) & (lane < STEP_LANE + HEADS)
    step = jnp.where(is_head, softplus(raw), 0.0)
    rate = -step * jnp.exp(par_ref[9:10, 0:128])
    total = ones_times(lower, rate, 3)
    reach = aux[:, 4:5] * jnp.exp(total)
    to_end = aux[:, 5:6] * jnp.exp(total[BLOCK - 1 : BLOCK, :] - total)
    return (raw, is_head, step, rate, total, reach, to_end)


def decay_of(total, total_rows, keep, h):
    at = STEP_LANE + h
    gap = total[:, at : at + 1] - total_rows[at : at + 1, :]
    return jnp.exp(jnp.where(keep, gap, MASKED))


def turn_halves(values, rope, back):
    up = pltpu.roll(values, 96, 1) * rope[:, 128:256]
    down = pltpu.roll(values, 32, 1) * rope[:, 256:384]
    here = values * rope[:, 0:128]
    return here - up - down if back else here + up + down


def allowed_keys(aux_ref, segrow_ref, first, count):
    query_seg = aux_ref[first : first + QUERY_BLOCK, 0:1]
    key_seg = segrow_ref[0:1, 0:count]
    shape = (QUERY_BLOCK, count)
    return (query_seg == key_seg) & (iota(shape, 1) <= iota(shape, 0) + first)


def fold(line):
    return jnp.concatenate([line[:, 128 * i : 128 * i + 128] for i in range(8)], axis=0)


def begin(pairs, sems, first=0):
    copies = [
        pltpu.make_async_copy(source, target, sems.at[first + at])
        for at, (source, target) in enumerate(pairs)
    ]
    for copy in copies:
        copy.start()
    return copies


def finish(*copies):
    for copy in copies:
        copy.wait()


def join_cores(core, own, mate, whole, sems, first):
    lead = (slice(None),) * (len(whole.shape) - 3)
    pairs = [(own, whole.at[(*lead, core)]), (mate, whole.at[(*lead, 1 - core)])]
    return begin(pairs, sems, first)


def split_cores(core, whole, keep, send, sems, first):
    lead = (slice(None),) * (len(whole.shape) - 3)
    pairs = [(whole.at[(*lead, core)], keep), (whole.at[(*lead, 1 - core)], send)]
    return begin(pairs, sems, first)


def columns(ref, first, last):
    return ref[:, :, :, first:last].reshape(WIDTH, last - first)


def mixer_forward_kernel(
    core_ref,
    p0,
    p1,
    p2,
    p3,
    p4,
    p5,
    p6,
    p7,
    own_hbm,
    mate_hbm,
    rope_hbm,
    aux_hbm,
    segrow_ref,
    par_ref,
    normed_hbm,
    mix_hbm,
    proj_hbm,
    states_hbm,
    qkv_hbm,
    lse_hbm,
    heads_hbm,
    normed_ref,
    w_ref,
    rope_ref,
    aux_ref,
    mix_ref,
    proj_ref,
    states_ref,
    qkv_ref,
    lse_ref,
    heads_ref,
    in_sems,
    out_sems,
):
    pieces = [
        (piece, normed_ref.at[core_ref[2] ^ k])
        for k, piece in enumerate((p0, p1, p2, p3, p4, p5, p6, p7))
    ]
    first_come = begin(pieces, in_sems, 0)
    first_come += join_cores(core_ref[0], own_hbm, mate_hbm, w_ref, in_sems, 8)
    come = begin([(rope_hbm, rope_ref), (aux_hbm, aux_ref)], in_sems, 10)
    finish(*first_come)
    gone = begin([(normed_ref, normed_hbm)], out_sems, 10)
    for chunk in range(4):
        rows = slice(256 * chunk, 256 * chunk + 256)
        normed = normed_ref[2 * chunk : 2 * chunk + 2].reshape(256, WIDTH)
        state = dot(normed, columns(w_ref, 0, 512))
        proj_ref[rows, CONV_AT : CONV_AT + 256] = state[:, 0:256]
        proj_ref[rows, KV_AT:CONV_AT] = state[:, 256:384]
        proj_ref[rows, QS_AT:PACKED] = state[:, 384:512]
        inner = dot(normed, columns(w_ref, 512, SENT))
        real = iota((256, 256), 1) < INNER
        gate = jnp.concatenate([inner[:, INNER:], inner[:, 0:64]], axis=1)
        proj_ref[rows, CONV_AT + 256 : GATE_AT] = jnp.where(real, inner[:, 0:256], 0.0)
        proj_ref[rows, GATE_AT:QS_AT] = jnp.where(real, gate, 0.0)
    gone += begin([(proj_ref, proj_hbm)], out_sems, 1)
    finish(*come)
    lane = iota((256, 128), 1)
    for first in range(0, TOKENS, 256):
        rows = slice(first, first + 256)
        rope = rope_ref[rows, :]
        keyval = proj_ref[rows, KV_AT:CONV_AT]
        turned = turn_halves(proj_ref[rows, QS_AT:PACKED], rope, False)
        qkv_ref[rows, 0:128] = (turned * AHDIM**-0.5).astype(BF16)
        qkv_ref[rows, 128:256] = turn_halves(keyval, rope, False).astype(BF16)
        ones = jnp.where(lane == 0, 1.0, 0.0)
        qkv_ref[rows, 256:384] = jnp.where(lane >= 64, keyval, ones).astype(BF16)
    gone += begin([(qkv_ref, qkv_hbm)], out_sems, 2)
    for first in range(0, TOKENS, QUERY_BLOCK):
        rows = slice(first, first + QUERY_BLOCK)
        count = first + QUERY_BLOCK
        scores = dot_right(qkv_ref[rows, 0:128], qkv_ref[0:count, 128:256])
        scores = jnp.where(allowed_keys(aux_ref, segrow_ref, first, count), scores, MASKED)
        top = jnp.max(scores, axis=1, keepdims=True)
        raised = jnp.exp(scores - top)
        summed = dot(raised.astype(BF16), qkv_ref[0:count, 256:384])
        total = summed[:, 0:1]
        heads_ref[rows, 128:256] = jnp.where(lane >= 64, summed / total, 0.0).astype(BF16)
        lse_ref[rows, :] = jnp.broadcast_to(top + jnp.log(total), (QUERY_BLOCK, 128))

    gone += begin([(lse_ref, lse_hbm)], out_sems, 3)

    spread, _ = head_matrices()
    causal = iota((BLOCK, BLOCK), 0) >= iota((BLOCK, BLOCK), 1)
    lower = causal.astype(BF16)

    def block_step(index, state):
        start = pl.multiple_of(index * BLOCK, BLOCK)
        rows = pl.ds(start, BLOCK)
        aux = aux_ref[rows, :]
        _, pre = conv_parts(proj_ref, par_ref, aux, start)
        conv = (pre * sigmoid(pre)).astype(BF16)
        in_map, out_map, inner = (conv[:, 0:128], conv[:, 128:256], conv[:, 256:512].astype(F32))
        _, _, step, _, total, reach, to_end = step_parts(proj_ref, par_ref, aux, lower, start)
        wide = times_ones(jnp.concatenate([step, reach, to_end], axis=0), spread)
        step_wide, reach_wide, end_wide = (wide[0:128], wide[128:256], wide[256:384])
        stepped = inner * step_wide
        keep = causal & (aux[:, 0:1] == segrow_ref[0:1, pl.ds(start, BLOCK)])
        total_rows = jnp.transpose(total)
        shared = dot_right(out_map, in_map)
        mixing = jnp.concatenate(
            [(decay_of(total, total_rows, keep, h) * shared).astype(BF16) for h in range(HEADS)],
            axis=1,
        )
        states_ref[rows, :] = state
        result = dot(mixing, per_head(stepped).astype(BF16))
        result = result + dot(out_map, state.astype(BF16)) * reach_wide
        result = result + inner * par_ref[10:11, 0:256]
        gate = proj_ref[rows, GATE_AT:QS_AT]
        gated = (result * (gate * sigmoid(gate))).astype(BF16)
        heads_ref[rows, 0:128] = gated[:, 0:128]
        heads_ref[rows, 128:256] = heads_ref[rows, 128:256] + gated[:, 128:256]
        added = dot_left(in_map, (stepped * end_wide).astype(BF16))
        return state * reach_wide[BLOCK - 1 : BLOCK, :] + added

    lax.fori_loop(0, BLOCKS, block_step, jnp.zeros((BLOCK, 256), F32), unroll=UNROLL)
    gone += begin([(states_ref, states_hbm), (heads_ref, heads_hbm)], out_sems, 4)
    w2 = columns(w_ref, SENT, WIDE)
    for chunk in range(4):
        rows = slice(256 * chunk, 256 * chunk + 256)
        mix_ref[rows, :] = dot_right(heads_ref[rows, :], w2).astype(BF16)
        gone += begin([(mix_ref.at[rows, :], mix_hbm.at[rows, :])], out_sems, 6 + chunk)
    finish(*gone)


def mixer_backward_kernel(
    core_ref,
    mixgrad_hbm,
    own_hbm,
    mate_hbm,
    qkv_hbm,
    lse_hbm,
    aux_hbm,
    rope_hbm,
    proj_hbm,
    states_hbm,
    normed_hbm,
    segrow_ref,
    par_ref,
    second_ref,
    ngrad_hbm,
    dproj_hbm,
    small_ref,
    mixgrad_ref,
    w_ref,
    qkv_ref,
    lse_ref,
    aux_ref,
    rope_ref,
    proj_ref,
    states_ref,
    normed_ref,
    mix_ref,
    dproj_ref,
    d_ref,
    dkv_ref,
    in_sems,
    out_sems,
):
    first_come = begin([(mixgrad_hbm, mixgrad_ref)], in_sems, 0)
    first_come += join_cores(core_ref[0], own_hbm, mate_hbm, w_ref, in_sems, 1)
    come = begin(
        [
            (qkv_hbm, qkv_ref),
            (lse_hbm, lse_ref),
            (aux_hbm, aux_ref),
            (rope_hbm, rope_ref),
            (proj_hbm, proj_ref),
            (states_hbm, states_ref),
            (normed_hbm, normed_ref),
        ],
        in_sems,
        3,
    )
    finish(*first_come)
    gone = []
    w2 = columns(w_ref, SENT, WIDE)
    for first in range(0, TOKENS, 256):
        rows = slice(first, first + 256)
        d_ref[rows, :] = dot(mixgrad_ref[rows, :], w2)
    lane = iota((QUERY_BLOCK, 128), 1)
    dkv_ref[...] = jnp.zeros_like(dkv_ref)
    finish(*come[0:3])
    for first in range(0, TOKENS, QUERY_BLOCK):
        rows = slice(first, first + QUERY_BLOCK)
        count = first + QUERY_BLOCK
        queries, keys = (qkv_ref[rows, 0:128], qkv_ref[0:count, 128:256])
        out_grad = jnp.where(lane >= 64, d_ref[rows, 128:256], 0.0).astype(BF16)
        scores = dot_right(queries, keys) - lse_ref[rows, 0:1]
        weights = jnp.exp(
            jnp.where(allowed_keys(aux_ref, segrow_ref, first, count), scores, MASKED)
        )
        weight_grad = dot_right(out_grad, qkv_ref[0:count, 256:384])
        mean = jnp.sum(weights * weight_grad, axis=1, keepdims=True)
        score_grad = (weights * (weight_grad - mean)).astype(BF16)
        query_grad = dot(score_grad, keys) * AHDIM**-0.5
        d_ref[rows, 128:256] = jnp.where(
            lane < 64, d_ref[rows, 128:256], pltpu.roll(query_grad, 64, 1)
        )
        dkv_ref[0:count, 0:128] += dot_left(score_grad, queries)
        dkv_ref[0:count, 128:256] += dot_left(weights.astype(BF16), out_grad)
    finish(come[3])
    for first in range(0, TOKENS, 256):
        rows = slice(first, first + 256)
        rope = rope_ref[rows, :]
        query_grad = turn_halves(pltpu.roll(d_ref[rows, 128:256], 64, 1), rope, True)
        dproj_ref[rows, 384:512] = query_grad.astype(BF16)
        key_grad = turn_halves(dkv_ref[rows, 0:128], rope, True)
        keyval_grad = jnp.where(lane < 64, key_grad, dkv_ref[rows, 128:256])
        dproj_ref[rows, 256:384] = keyval_grad.astype(BF16)

    spread, gather = head_matrices()
    row, column = (iota((BLOCK, BLOCK), 0), iota((BLOCK, BLOCK), 1))
    causal = row >= column
    lower = causal.astype(BF16)
    upper = (row <= column).astype(BF16)
    strict = (row > column).astype(BF16)
    real = iota((BLOCK, 256), 1) < INNER
    head_lane = iota((BLOCK, 128), 1)

    def block_step(turn, carried):
        state_grad, later, taps_sum, head_sum, skip_sum = carried
        start = pl.multiple_of((BLOCKS - 1 - turn) * BLOCK, BLOCK)
        rows = pl.ds(start, BLOCK)
        aux = aux_ref[rows, :]
        lagged, pre = conv_parts(proj_ref, par_ref, aux, start)
        sig = sigmoid(pre)
        conv = (pre * sig).astype(BF16)
        in_map, out_map, inner = (conv[:, 0:128], conv[:, 128:256], conv[:, 256:512].astype(F32))
        raw, is_head, step, rate, total, reach, to_end = step_parts(
            proj_ref, par_ref, aux, lower, start
        )
        wide = times_ones(jnp.concatenate([step, reach, to_end], axis=0), spread)
        step_wide, reach_wide, end_wide = (wide[0:128], wide[128:256], wide[256:384])
        stepped = inner * step_wide
        stepped_low = stepped.astype(BF16)
        keep = causal & (aux[:, 0:1] == segrow_ref[0:1, pl.ds(start, BLOCK)])
        total_rows = jnp.transpose(total)
        shared = dot_right(out_map, in_map)
        decays = [decay_of(total, total_rows, keep, h) for h in range(HEADS)]
        mixing = [(decay * shared).astype(BF16) for decay in decays]
        state = states_ref[rows, :]
        state_low = state.astype(BF16)
        incoming = dot(out_map, state_low) * reach_wide
        result = dot(jnp.concatenate(mixing, axis=1), per_head(stepped).astype(BF16)) + incoming
        result = result + inner * par_ref[10:11, 0:256]

        gate = proj_ref[rows, GATE_AT:QS_AT]
        gate_sig = sigmoid(gate)
        gated_grad = jnp.where(real, d_ref[rows, :], 0.0)
        gate_grad = gated_grad * result * (gate_sig * (1.0 + gate * (1.0 - gate_sig)))
        out_grad = gated_grad * (gate * gate_sig)
        by_head = per_head(out_grad).astype(BF16)

        mixing_grad = dot_right(by_head, stepped_low)
        shared_grad = jnp.zeros((BLOCK, BLOCK), F32)
        edges = []
        for h in range(HEADS):
            decayed = mixing_grad[h * BLOCK : (h + 1) * BLOCK] * decays[h]
            shared_grad = shared_grad + decayed
            edges.append((decayed * shared).astype(BF16))
        crossing = dot(upper, jnp.concatenate(edges, axis=1))
        rate_grad = jnp.zeros((BLOCK, 128), F32)
        for h in range(HEADS):
            part = jnp.where(row > column, crossing[:, h * BLOCK : (h + 1) * BLOCK], 0.0)
            part = jnp.sum(part, axis=1, keepdims=True)
            rate_grad = rate_grad + jnp.where(head_lane == STEP_LANE + h, part, 0.0)

        reached = (out_grad * reach_wide).astype(BF16)
        state_grad_low = state_grad.astype(BF16)
        ended = dot(in_map, state_grad_low) * end_wide
        mapped = dot_left(jnp.concatenate(mixing, axis=0), by_head) + ended
        inner_grad = mapped * step_wide + out_grad * par_ref[10:11, 0:256]
        kept = jnp.sum(state_grad * state, axis=0, keepdims=True)
        kept = jnp.broadcast_to(kept * reach_wide[BLOCK - 1 : BLOCK, :], (8, 256))
        sums = times_ones(
            jnp.concatenate([inner * mapped, out_grad * incoming, stepped * ended, kept], axis=0),
            gather,
        )
        flows = ones_times(
            jnp.concatenate([upper, strict], axis=1), sums[128:384]
        )
        rate_grad = rate_grad + flows + sums[384:385]
        step_grad = sums[0:128] - jnp.exp(par_ref[9:10, 0:128]) * rate_grad
        step_grad = jnp.where(is_head, step_grad * sigmoid(raw), 0.0)
        dproj_ref[rows, 384:512] = dproj_ref[rows, 384:512] + step_grad.astype(BF16)
        head_sum = head_sum + jnp.concatenate(
            [
                jnp.sum(jnp.where(is_head, rate_grad * rate, 0.0), axis=0, keepdims=True),
                jnp.sum(step_grad, axis=0, keepdims=True),
                jnp.zeros((6, 128), F32),
            ],
            axis=0,
        )
        skip_sum = skip_sum + jnp.sum(inner * out_grad, axis=0, keepdims=True)

        shared_low = shared_grad.astype(BF16)
        out_map_grad = dot(shared_low, in_map) + dot_right(reached, state_low)
        in_map_grad = dot_left(shared_low, out_map) + dot_right(
            (stepped * end_wide).astype(BF16), state_grad_low
        )
        conv_grad = jnp.concatenate([in_map_grad, out_map_grad, inner_grad], axis=1)
        pre_grad = conv_grad * (sig * (1.0 + pre * (1.0 - sig)))
        taps_sum = taps_sum + jnp.concatenate(
            [jnp.sum(pre_grad * lagged[lag], axis=0, keepdims=True) for lag in range(4)]
            + [jnp.zeros((4, CONV_WIDTH), F32)],
            axis=0,
        )
        both = jnp.concatenate([pre_grad, later], axis=0)
        masks = aux_ref[pl.ds(start, BLOCK + 8), :]
        u_grad = pre_grad * par_ref[0:1, :]
        for lag in range(1, 4):
            shifted = (both * masks[:, lag : lag + 1])[lag : lag + BLOCK]
            u_grad = u_grad + shifted * par_ref[lag : lag + 1, :]
        dproj_ref[rows, 0:256] = u_grad[:, 0:256].astype(BF16)
        inner = jnp.concatenate([u_grad[:, 256 : 256 + INNER], gate_grad[:, 0:INNER]], axis=1)
        dproj_ref[rows, 512:SENT] = inner.astype(BF16)
        state_grad = state_grad * reach_wide[BLOCK - 1 : BLOCK, :] + dot_left(out_map, reached)
        return (state_grad, pre_grad[0:8], taps_sum, head_sum, skip_sum)

    carried = (
        jnp.zeros((BLOCK, 256), F32),
        jnp.zeros((8, CONV_WIDTH), F32),
        jnp.zeros((8, CONV_WIDTH), F32),
        jnp.zeros((8, 128), F32),
        jnp.zeros((1, 256), F32),
    )
    finish(*come[4:6])
    _, _, taps_sum, head_sum, skip_sum = lax.fori_loop(
        0, BLOCKS, block_step, carried, unroll=UNROLL
    )
    gone += begin([(dproj_ref, dproj_hbm)], out_sems, 0)
    finish(come[6])
    gain = jnp.zeros((1, WIDTH), F32)
    w1 = columns(w_ref, 0, SENT)
    for chunk in range(4):
        rows = slice(256 * chunk, 256 * chunk + 256)
        grad = dot_right(dproj_ref[rows, :], w1)
        mix_ref[rows, :] = grad.astype(BF16)
        gone += begin([(mix_ref.at[rows, :], ngrad_hbm.at[rows, :])], out_sems, 1 + chunk)
        normed = normed_ref[2 * chunk : 2 * chunk + 2].reshape(256, WIDTH)
        gain = gain + jnp.sum(grad * normed.astype(F32), axis=0, keepdims=True)
    upper_rows = jnp.concatenate([taps_sum[0:4, 0:256], taps_sum[0:4, 256:512]], axis=0)
    upper_rows = jnp.concatenate([upper_rows, fold(gain)], axis=1)
    skip_rows = jnp.concatenate([skip_sum, jnp.zeros((7, 256), F32)], axis=0)
    lower_rows = jnp.concatenate([fold(second_ref[0:1, :]), head_sum[:, 64:128], skip_rows[:, 0:INNER]], axis=1)
    small = jnp.concatenate([upper_rows, lower_rows], axis=0)
    small_ref[...] = small
    finish(*gone)


def feed_kernel(
    core_ref, n0, n1, n2, n3, c0, c1, c2, c3, own_hbm, mate_hbm,
    o0, o1, o2, o3, g0, g1, g2, g3, act_ref, grads_ref, gain_ref, w_ref, sems,
):
    finish(*join_cores(core_ref[0], own_hbm, mate_hbm, w_ref, sems, 0))
    inputs = ((n0, n1, c0, c1), (n2, n3, c2, c3))
    outs = (((o0, g0), (o1, g1)), ((o2, g2), (o3, g3)))
    gain = jnp.zeros((1, WIDTH), F32)
    for j in range(2):
        rows = slice(256 * j, 256 * j + 256)
        normed = jnp.concatenate([inputs[j][0][...], inputs[j][1][...]], axis=0)
        cot = jnp.concatenate([inputs[j][2][...], inputs[j][3][...]], axis=0)
        out_sum, grad_sum = (0.0, 0.0)
        for h in range(2):
            up_weights = columns(w_ref.at[h], 0, 512)
            down = columns(w_ref.at[h], 512, 768)
            both = dot(normed, up_weights)
            gate, up = (both[:, 0:FEED], both[:, FEED:])
            sig = sigmoid(gate)
            silu = gate * sig
            act = (silu * up).astype(BF16)
            act_ref[rows, h * FEED : (h + 1) * FEED] = act
            out_sum = out_sum + dot_right(act, down)
            act_grad = dot(cot, down)
            gate_grad = (act_grad * up * (sig + silu * (1.0 - sig))).astype(BF16)
            up_grad = (act_grad * silu).astype(BF16)
            grads = jnp.concatenate([gate_grad, up_grad], axis=1)
            grads_ref[rows, h * 512 : (h + 1) * 512] = grads
            grad_sum = grad_sum + dot_right(grads, up_weights)
        gain = gain + jnp.sum(grad_sum * normed.astype(F32), axis=0, keepdims=True)
        out_low, grad_low = (out_sum.astype(BF16), grad_sum.astype(BF16))
        for half in range(2):
            part = slice(half * BLOCK, (half + 1) * BLOCK)
            outs[j][half][0][...] = out_low[part]
            outs[j][half][1][...] = grad_low[part]
    gain_ref[...] = jnp.broadcast_to(gain, (8, WIDTH))


def feed_weights_kernel(
    core_ref, n0, n1, n2, n3, c0, c1, c2, c3, act_ref, grads_ref, keep_hbm, send_hbm, out_ref, sems
):
    normed = jnp.concatenate([r[...] for r in (n0, n1, n2, n3)], axis=0)
    cot = jnp.concatenate([r[...] for r in (c0, c1, c2, c3)], axis=0)
    up = dot_left(normed, grads_ref[...]).astype(BF16)
    down = dot_left(cot, act_ref[...]).astype(BF16)
    for h in range(2):
        up_here = up[:, h * 512 : (h + 1) * 512].reshape(8, 2, 64, 512)
        down_here = down[:, h * FEED : (h + 1) * FEED].reshape(8, 2, 64, FEED)
        out_ref[h, :, :, :, 0:512] = up_here
        out_ref[h, :, :, :, 512:768] = down_here
    finish(*split_cores(core_ref[0], out_ref, keep_hbm, send_hbm, sems, 0))


def mixer_weights_kernel(
    core_ref, normed_ref, dproj_ref, mixgrad_ref, heads_ref, keep_hbm, send_hbm, out_ref, sems
):
    normed = normed_ref[...].reshape(TOKENS, WIDTH)
    for first, last in ((0, 512), (512, SENT)):
        grad = dot_left(normed, dproj_ref[:, first:last]).astype(BF16)
        out_ref[:, :, :, first:last] = grad.reshape(8, 2, 64, last - first)
    grad = dot_left(mixgrad_ref[...], heads_ref[...]).astype(BF16)
    out_ref[:, :, :, SENT:WIDE] = grad.reshape(8, 2, 64, WIDE - SENT)
    finish(*split_cores(core_ref[0], out_ref, keep_hbm, send_hbm, sems, 0))


def mixer_pair_kernel(keep_ref, come_ref, small_ref, small_come_ref, out_ref):
    total = keep_ref[...].astype(F32) + come_ref[...].astype(F32)
    small = small_ref[...] + small_come_ref[...]
    high = small.astype(BF16)
    low = (small - high.astype(F32)).astype(BF16)
    tail = jnp.concatenate([high, low, jnp.zeros_like(high)], axis=1)
    for i in range(8):
        out_ref[i, 0:64, :] = total[i].astype(BF16)
        out_ref[i, 64:, :] = tail


def feed_pair_kernel(keep_ref, come_ref, out_ref):
    out_ref[...] = (keep_ref[...].astype(F32) + come_ref[...].astype(F32)).astype(BF16)


def collect_kernel(
    core_ref, blocks_ref, lines_ref, gate_ref, input_ref, step_ref, query_ref, mamba_ref, attend_ref,
    own_ref,
):
    total = total_rows(blocks_ref)
    own = total[64:, 0:EARLY] + total[64:, EARLY : 2 * EARLY]
    total = total[0:64]
    keyval = total[:, 256:384]
    turned = pltpu.roll(keyval, AHDIM, 1)
    low = iota(keyval.shape, 1) < AHDIM
    first = core_ref[1] == 0
    keys = jnp.where(first, jnp.where(low, keyval, 0.0), jnp.where(low, 0.0, turned))
    values = jnp.where(first, jnp.where(low, turned, 0.0), jnp.where(low, 0.0, keyval))
    shared = jnp.concatenate([total[:, 0:256], keys, values], axis=1)
    for t in range(8):
        lines_ref[t, 0:8, :] = shared[8 * t : 8 * t + 8]
        lines_ref[t, 8:24, 0:EARLY] = own
        lines_ref[t, 8:24, EARLY:] = jnp.zeros((16, 512 - EARLY), F32)
    own_ref[...] = own
    query_ref[...] = total[:, EARLY : EARLY + AHDIM]
    step_ref[...] = total[:, EARLY + STEP_LANE : EARLY + STEP_LANE + HEADS]
    input_ref[...] = total[:, 512 : 512 + INNER]
    gate_ref[...] = total[:, 512 + INNER : SENT]
    turned = jnp.transpose(total[:, SENT:WIDE])
    mamba_ref[...] = turned[0:INNER]
    attend_ref[...] = turned[INNER:]


def last_kernel(
    lines_ref, gain_one_ref, gain_two_ref, state_ref, keyval_ref, taps_ref, first_ref, second_ref
):
    pairs = [lines_ref[2 * t] + lines_ref[2 * t + 1] for t in range(4)]
    total = (pairs[0] + pairs[1]) + (pairs[2] + pairs[3])
    state_ref[...] = total[0:8, 0:256]
    keyval_ref[...] = total[0:8, 256:512]
    taps_ref[...] = total[8:12, 0:256]
    first_ref[...] = total[8:16, 256:384] / gain_one_ref[...]
    second_ref[...] = total[16:24, 0:128] / gain_two_ref[...]


def total_of(pieces):
    return sum(piece[...].astype(F32) for piece in pieces)


def total_rows(blocks_ref):
    return sum(blocks_ref[i].astype(F32) for i in range(8))


def row_norm(values):
    return lax.rsqrt(jnp.mean(values * values, axis=-1, keepdims=True) + NORM_EPS)


def norm_back(values, gain, grad):
    scale = row_norm(values)
    scaled = grad * gain
    return scale * scaled - values * (
        scale**3 * jnp.mean(scaled * values, axis=-1, keepdims=True)
    )


def first_norm_kernel(x_ref, gain_ref, normed_ref):
    x = x_ref[...].astype(F32)
    normed_ref[...] = (x * row_norm(x) * gain_ref[...]).astype(BF16)


def second_norm_kernel(x_ref, gain_ref, blocks_ref, hidden_ref, normed_ref):
    hidden = x_ref[...].astype(F32) + total_rows(blocks_ref)
    hidden_ref[...] = hidden
    normed_ref[...] = (hidden * row_norm(hidden) * gain_ref[...]).astype(BF16)


def hidden_grad_kernel(hidden_ref, gain_ref, cot_ref, s0, s1, s2, s3, grad_ref, low_ref):
    back = norm_back(hidden_ref[...], gain_ref[...], total_of((s0, s1, s2, s3)))
    grad = cot_ref[...].astype(F32) + back
    grad_ref[...] = grad
    low = grad.astype(BF16)
    for i in range(8):
        low_ref[i] = low


def input_grad_kernel(x_ref, gain_ref, hidden_grad_ref, blocks_ref, grad_ref):
    x = x_ref[...].astype(F32)
    back = norm_back(x, gain_ref[...], total_rows(blocks_ref))
    grad_ref[...] = hidden_grad_ref[...] + back


def output_kernel(hidden_ref, s0, s1, s2, s3, out_ref):
    out_ref[...] = (hidden_ref[...] + total_of((s0, s1, s2, s3))).astype(BF16)


def like(dtype, *shape):
    return jax.ShapeDtypeStruct(shape, dtype)


VMEM = pl.BlockSpec(memory_space=pltpu.VMEM)
SMEM = pl.BlockSpec(memory_space=pltpu.SMEM)
ANY = pl.BlockSpec(memory_space=pl.ANY)


def run(kernel, name, outs, args, specs=None, scratch=(), us=0.05, out_specs=None):
    return pl.pallas_call(
        kernel,
        in_specs=specs or [VMEM] * len(args),
        out_specs=out_specs or [VMEM] * len(outs),
        out_shape=list(outs),
        scratch_shapes=list(scratch),
        compiler_params=pltpu.CompilerParams(vmem_limit_bytes=VMEM_BYTES),
        cost_estimate=pl.CostEstimate(
            flops=int(us * 1e9), transcendentals=0, bytes_accessed=int(us * 2e6)
        ),
        name=name,
    )(*args)


def held(array):
    return pltpu.VMEM(array.shape, array.dtype)


HERE = (BLOCK, WIDTH)
UNROLL = 2
FORWARD_US = 20
BACKWARD_US = 33
ROW = (8, BLOCK, WIDTH)


def mixer_forward(core, pieces, own, mate, aux, segrow, pack, rope):
    outs = (
        like(BF16, *ROW),
        like(BF16, TOKENS, WIDTH),
        like(F32, TOKENS, PACKED),
        like(F32, TOKENS, 256),
        like(BF16, TOKENS, 384),
        like(F32, TOKENS, 128),
        like(BF16, TOKENS, 256),
    )
    return run(
        mixer_forward_kernel,
        "mixer_forward",
        outs,
        (core, *pieces, own, mate, rope, aux, segrow, pack),
        [SMEM] + [ANY] * 12 + [VMEM] * 2,
        [pltpu.VMEM(ROW, BF16), pltpu.VMEM((8, 2, 64, WIDE), BF16), held(rope), held(aux)]
        + [held(a) for a in outs[1:]]
        + [pltpu.SemaphoreType.DMA((n,)) for n in (12, 11)],
        FORWARD_US,
        [ANY] * 7,
    )


def mixer_backward(
    core, mix_grad, own, mate, normed, aux, segrow, pack, rope, proj, states, qkv, lse, second
):
    outs = (like(BF16, TOKENS, WIDTH), like(BF16, TOKENS, SENT), like(F32, 16, EARLY))
    moved = (qkv, lse, aux, rope, proj, states)
    return run(
        mixer_backward_kernel,
        "mixer_backward",
        outs,
        (core, mix_grad, own, mate, *moved, normed, segrow, pack, second),
        [SMEM] + [ANY] * 10 + [VMEM] * 3,
        [held(mix_grad), pltpu.VMEM((8, 2, 64, WIDE), BF16)]
        + [held(a) for a in moved]
        + [pltpu.VMEM(ROW, BF16)]
        + [held(a) for a in outs[0:2]]
        + [pltpu.VMEM((TOKENS, 256), F32), pltpu.VMEM((TOKENS, 256), F32)]
        + [pltpu.SemaphoreType.DMA((n,)) for n in (10, 5)],
        BACKWARD_US,
        [ANY] * 2 + [VMEM],
    )


def feed_forward_backward(core, normed, cot, weights):
    return run(
        feed_kernel,
        "feed",
        [like(BF16, *HERE)] * 8
        + [like(BF16, 512, 2 * FEED), like(BF16, 512, 4 * FEED), like(F32, 8, WIDTH)],
        (core, *normed, *cot, *weights),
        [SMEM] + [VMEM] * 8 + [ANY] * 2,
        [pltpu.VMEM((2, 8, 2, 64, 768), BF16), pltpu.SemaphoreType.DMA((2,))],
    )


def aux_arrays(seg):
    columns = [seg]
    for lag in range(1, 4):
        earlier = jnp.concatenate([jnp.full((lag,), -1.0, F32), seg[: TOKENS - lag]])
        columns.append((earlier == seg).astype(F32))
    ends = seg.reshape(BLOCKS, BLOCK)[:, -1]
    before = jnp.concatenate([jnp.full((1,), -1.0, F32), ends[:-1]])
    columns.append((seg == jnp.repeat(before, BLOCK)).astype(F32))
    columns.append((seg == jnp.repeat(ends, BLOCK)).astype(F32))
    aux = jnp.pad(jnp.stack(columns, axis=1), ((0, 8), (0, 128 - len(columns))))
    return (aux, jnp.broadcast_to(seg, (8, TOKENS)))


def rope_arrays():
    half = AHDIM // 2
    freq = (ROPE_BASE ** (-2.0 * np.arange(half) / AHDIM)).astype(np.float32)
    angles = np.arange(TOKENS, dtype=np.float32)[:, None] * freq[None, :]
    cosine, sine = (np.cos(angles.astype(np.float64)), np.sin(angles.astype(np.float64)))
    none = np.zeros_like(sine)
    parts = [cosine, cosine, none, none, -sine, none, none, none, none, sine, none, none]
    return jnp.asarray(np.concatenate(parts, axis=1).astype(np.float32))


def pad_columns(values, width, before=0):
    return jnp.pad(values, ((0, 0), (before, width - before - values.shape[1])))


def index_of(axes):
    return lax.axis_index(axes)


def exchange(values, axes, turn):
    size = 2 ** len(axes)
    return lax.ppermute(values, axes, [(i, turn(i)) for i in range(size)])


def other_core(values):
    return exchange(values, ("c",), lambda i: i ^ 1)


def near_gather(shard):
    return [shard] + near_return([shard] * 4)


def near_return(pieces):
    return [exchange(pieces[j], NEAR, lambda i, j=j: i ^ j) for j in range(1, 4)]


def spread_blocks(shard, axes):
    copies = jnp.broadcast_to(shard, (2 ** len(axes), *shard.shape))
    return turn_blocks(copies, axes)


def turn_blocks(blocks, axes):
    return lax.all_to_all(blocks, axes, split_axis=0, concat_axis=0, tiled=True)


def sum_blocks(blocks):
    return jnp.sum(blocks.astype(F32), axis=0)


def body(
    block_input,
    segments,
    first_gain,
    mamba_gate,
    mamba_input,
    step_weight,
    state_weight,
    conv_inner,
    conv_state,
    decay_log,
    step_bias,
    skip_scale,
    query_weight,
    keyval_weight,
    mamba_out,
    attention_out,
    second_gain,
    feed_gate,
    feed_up,
    feed_down,
    cotangent,
):
    kv_head = lax.axis_index("yh")
    core = jnp.stack([lax.axis_index("c"), kv_head, lax.axis_index(TENSOR)]).astype(jnp.int32)
    x, cot = (block_input[0], cotangent[0])
    gain_one, gain_two = (first_gain[None], second_gain[None])
    shared = spread_blocks(jnp.concatenate([state_weight, keyval_weight], axis=1), TENSOR)
    shared = shared.reshape(-1, 512)
    (normed_here,) = run(first_norm_kernel, "first_norm", [like(BF16, *HERE)], (x, gain_one))
    normed_pieces = [normed_here] + [
        exchange(normed_here, TENSOR, lambda i, k=k: i ^ k) for k in range(1, 8)
    ]
    shared, _ = lax.optimization_barrier((shared, normed_here))
    pack = jnp.concatenate(
        [
            jnp.concatenate([conv_state, pad_columns(conv_inner, 256)], axis=1),
            jnp.zeros((4, 512), F32),
            pad_columns(step_bias[None], 512, STEP_LANE),
            pad_columns(decay_log[None], 512, STEP_LANE),
            pad_columns(jnp.repeat(skip_scale, HDIM)[None], 512),
            jnp.zeros((5, 512), F32),
        ],
        axis=0,
    )
    aux, segrow = aux_arrays(segments.reshape(TOKENS).astype(F32))
    rope = rope_arrays()

    feed_here = jnp.concatenate([feed_gate, feed_up, feed_down.T], axis=1)
    feed_copies = jnp.broadcast_to(feed_here, (16, *feed_here.shape))
    share_rows = shared.shape[0]
    key_part = lax.dynamic_slice(shared, (0, 256 + kv_head * AHDIM), (share_rows, AHDIM))
    value_part = lax.dynamic_slice(
        shared, (0, 256 + (KVHEADS + kv_head) * AHDIM), (share_rows, AHDIM)
    )
    main_here = jnp.concatenate(
        [
            shared[:, 0:256],
            key_part,
            value_part,
            query_weight,
            pad_columns(step_weight, 64),
            mamba_input,
            mamba_gate,
            mamba_out.T,
            attention_out.T,
        ],
        axis=1,
    )
    own = spread_blocks(main_here, CHIPS)
    mate = other_core(own)

    own, feed_copies, aux, segrow, pack = lax.optimization_barrier(
        (own, feed_copies, aux, segrow, pack)
    )
    feed_own = turn_blocks(feed_copies, FEED16).reshape(2, 8, share_rows, 768)

    normed, mix, proj, states, qkv, lse, heads = mixer_forward(
        core, normed_pieces, own, mate, aux, segrow, pack, rope
    )
    mix, feed_own, cot_here = lax.optimization_barrier((mix, feed_own, cot))
    feed_weights = (feed_own, other_core(feed_own))
    mix_blocks, *cot_pieces = lax.optimization_barrier(
        (turn_blocks(mix.reshape(ROW), TENSOR), *near_gather(cot_here))
    )
    hidden, normed_two_here = run(
        second_norm_kernel,
        "second_norm",
        [like(F32, *HERE), like(BF16, *HERE)],
        (x, gain_two, mix_blocks),
    )
    normed_two = near_gather(normed_two_here)
    *parts, act, feed_grads, second_part = feed_forward_backward(
        core, normed_two, cot_pieces, feed_weights
    )
    feed_keep, feed_send = run(
        feed_weights_kernel,
        "feed_weights",
        [like(BF16, 2, 8, share_rows, 768)] * 2,
        (core, *normed_two, *cot_pieces, act, feed_grads),
        [SMEM] + [VMEM] * 10,
        [pltpu.VMEM((2, 8, 2, 64, 768), BF16), pltpu.SemaphoreType.DMA((2,))],
        out_specs=[ANY] * 2,
    )
    sums = near_return(parts[4:8])
    hidden, feed_keep, feed_send, *sums = lax.optimization_barrier(
        (hidden, feed_keep, feed_send, *sums)
    )
    hidden_grad, mix_grad_copies = run(
        hidden_grad_kernel,
        "hidden_grad",
        [like(F32, *HERE), like(BF16, *ROW)],
        (hidden, gain_two, cot, parts[4], *sums),
    )
    (feed_pair,) = run(
        feed_pair_kernel,
        "feed_pair",
        [like(BF16, 2, 8, share_rows, 768)],
        (feed_keep, other_core(feed_send)),
    )
    mix_grad = turn_blocks(mix_grad_copies, TENSOR).reshape(TOKENS, WIDTH)
    feed_pair, mix_grad = lax.optimization_barrier((feed_pair, mix_grad))
    feed_blocks = turn_blocks(feed_pair.reshape(16, share_rows, 768), FEED16)

    normed_grad, dproj, small = mixer_backward(
        core, mix_grad, own, mate, normed, aux, segrow, pack, rope, proj, states, qkv, lse,
        second_part,
    )
    normed_grad, feed_blocks, *out_sums = lax.optimization_barrier(
        (normed_grad, feed_blocks, *near_return(parts[0:4]))
    )
    input_blocks = turn_blocks(normed_grad.reshape(ROW), TENSOR)
    keep, send = run(
        mixer_weights_kernel,
        "mixer_weights",
        [like(BF16, 8, share_rows, WIDE)] * 2,
        (core, normed, dproj, mix_grad, heads),
        [SMEM] + [VMEM] * 4,
        [pltpu.VMEM((8, 2, 64, WIDE), BF16), pltpu.SemaphoreType.DMA((2,))],
        out_specs=[ANY] * 2,
    )
    (pair,) = run(
        mixer_pair_kernel,
        "mixer_pair",
        [like(BF16, 8, share_rows + 16, WIDE)],
        (keep, other_core(send), small, other_core(small)),
    )
    pair, input_blocks = lax.optimization_barrier((pair, input_blocks))
    (block_out,) = run(
        output_kernel, "output", [like(BF16, *HERE)], (hidden, parts[0], *out_sums)
    )
    blocks = turn_blocks(pair, CHIPS)
    (input_grad,) = run(
        input_grad_kernel,
        "input_grad",
        [like(F32, *HERE)],
        (x, gain_one, hidden_grad, input_blocks),
    )
    feed_total = sum_blocks(feed_blocks)
    feed_outs = (feed_total[:, 0:256], feed_total[:, 256:512], feed_total[:, 512:768].T)
    blocks, input_grad, block_out, *feed_outs = lax.optimization_barrier(
        (blocks, input_grad, block_out, *feed_outs)
    )
    lines, gate_sum, input_sum, step_sum, query_sum, mamba_sum, attend_sum, own = run(
        collect_kernel,
        "collect",
        [
            like(F32, 8, 24, 512),
            like(F32, share_rows, INNER),
            like(F32, share_rows, INNER),
            like(F32, share_rows, HEADS),
            like(F32, share_rows, AHDIM),
            like(F32, INNER, share_rows),
            like(F32, AHDIM, share_rows),
            like(F32, 16, EARLY),
        ],
        (core, blocks),
        [SMEM, VMEM],
    )
    state_sum, keyval_sum, state_taps, first_sum, second_sum = run(
        last_kernel,
        "last",
        [
            like(F32, 8, 256),
            like(F32, 8, 256),
            like(F32, 4, 256),
            like(F32, 8, 128),
            like(F32, 8, 128),
        ],
        (turn_blocks(lines, TENSOR), first_gain.reshape(8, 128), second_gain.reshape(8, 128)),
    )
    return (
        block_out[None],
        input_grad[None],
        first_sum.reshape(-1),
        gate_sum,
        input_sum,
        step_sum,
        state_sum,
        own[4:8, 0:INNER],
        state_taps,
        own[8, 128 : 128 + HEADS],
        own[9, 128 : 128 + HEADS],
        jnp.sum(own[8, INNER : 2 * INNER].reshape(HEADS, HDIM), axis=1),
        query_sum,
        keyval_sum,
        mamba_sum,
        attend_sum,
        second_sum.reshape(-1),
        *feed_outs,
    )


def solution(mesh):
    DP, TP = (("zlo", "xh", "xl", "c"), ("yh", "yl", "zhi"))
    fine = jax.sharding.Mesh(mesh.devices.reshape(FINE_SIZES), (*DP, *TP))
    in_specs = (
        P(DP, TP, None),
        P(DP, None),
        P(),
        P(DP, TP),
        P(DP, TP),
        P(DP, TP),
        P((*DP, *TP), None),
        P(None, TP),
        P(),
        P(TP),
        P(TP),
        P(TP),
        P(DP, TP),
        P((*DP, *TP), None),
        P(TP, DP),
        P(TP, DP),
        P(),
        P(DP, TP),
        P(DP, TP),
        P(TP, DP),
        P(DP, TP, None),
    )
    out_specs = (
        P(DP, TP, None),
        P(DP, TP, None),
        P(),
        P(DP, TP),
        P(DP, TP),
        P(DP, TP),
        P((*DP, *TP), None),
        P(None, TP),
        P(),
        P(TP),
        P(TP),
        P(TP),
        P(DP, TP),
        P((*DP, *TP), None),
        P(TP, DP),
        P(TP, DP),
        P(),
        P(DP, TP),
        P(DP, TP),
        P(TP, DP),
    )
    return jax.shard_map(body, mesh=fine, in_specs=in_specs, out_specs=out_specs, check_vma=False)
```

```python
import jax
import jax.numpy as jnp
import numpy as np
from jax import lax
from jax.experimental import pallas as pl
from jax.experimental.pallas import tpu as pltpu
from jax.sharding import PartitionSpec as P

QHEADS = 8
KVHEADS = 2
AHDIM = 64
TOKENS = 1024
WIDTH = 1024
BLOCK = 128
BLOCKS = TOKENS // BLOCK
HEADS = 3
HDIM = 64
INNER = HEADS * HDIM
FEED = 256
QUERY_BLOCK = 256
NORM_EPS = 1e-05
ROPE_BASE = 10000.0
MASKED = -1e30
VMEM_BYTES = 60 * 1024 * 1024

KV_AT = 0
CONV_AT = 128
GATE_AT = 640
QS_AT = 896
PACKED = 1024
EARLY = 384
SENT = 896
PAYLOAD = 32
CONV_WIDTH = 512
STEP_LANE = 64

CHIPS = ("zlo", "xh", "xl")
FEED16 = ("yh", *CHIPS)
TENSOR = ("yh", "yl", "zhi")
NEAR = ("yl", "zhi")
PIECE = BLOCK + 16
WIDE = 1152
FINE_SIZES = (2,) * 7

F32 = jnp.float32
BF16 = jnp.bfloat16


def dot(a, b):
    return lax.dot_general(a, b, (((1,), (0,)), ((), ())), preferred_element_type=F32)


def dot_right(a, b):
    return lax.dot_general(a, b, (((1,), (1,)), ((), ())), preferred_element_type=F32)


def dot_left(a, b):
    return lax.dot_general(a, b, (((0,), (0,)), ((), ())), preferred_element_type=F32)


def parts_of(values, terms):
    parts = []
    for _ in range(terms - 1):
        part = values.astype(BF16)
        parts.append(part)
        values = values - part.astype(F32)
    parts.append(values.astype(BF16))
    return parts


def times_ones(values, ones, terms=2):
    return sum(dot(part, ones) for part in parts_of(values, terms))


def ones_times(ones, values, terms=2):
    return sum(dot(ones, part) for part in parts_of(values, terms))


def iota(shape, dim):
    return lax.broadcasted_iota(jnp.int32, shape, dim)


def softplus(v):
    return jnp.maximum(v, 0.0) + jnp.log1p(jnp.exp(-jnp.abs(v)))


def sigmoid(v):
    return 1.0 / (1.0 + jnp.exp(-v))


def head_matrices():
    lane, channel = (iota((BLOCK, 256), 0), iota((BLOCK, 256), 1))
    spread = ((channel >> 6) + STEP_LANE == lane) & (channel < INNER)
    lane, channel = (iota((256, BLOCK), 1), iota((256, BLOCK), 0))
    gather = ((channel >> 6) + STEP_LANE == lane) & (channel < INNER)
    return (spread.astype(BF16), gather.astype(BF16))


def per_head(values):
    of_head = iota(values.shape, 1) >> 6
    return jnp.concatenate(
        [jnp.where(of_head == h, values, jnp.zeros_like(values)) for h in range(HEADS)], axis=0
    )


def conv_parts(proj_ref, par_ref, aux, start):
    here = proj_ref[pl.ds(start, BLOCK), CONV_AT:GATE_AT]
    before = proj_ref[pl.ds(pl.multiple_of(jnp.maximum(start - 8, 0), 8), 8), CONV_AT:GATE_AT]
    both = jnp.concatenate([before, here], axis=0)
    lagged = [here]
    for lag in range(1, 4):
        lagged.append(both[8 - lag : 8 - lag + BLOCK] * aux[:, lag : lag + 1])
    pre = sum(lagged[lag] * par_ref[lag : lag + 1, :] for lag in range(4))
    return (lagged, pre)


def step_parts(proj_ref, par_ref, aux, lower, start):
    raw = proj_ref[pl.ds(start, BLOCK), QS_AT:PACKED] + par_ref[8:9, 0:128]
    lane = iota((BLOCK, 128), 1)
    is_head = (lane >= STEP_LANE) & (lane < STEP_LANE + HEADS)
    step = jnp.where(is_head, softplus(raw), 0.0)
    rate = -step * jnp.exp(par_ref[9:10, 0:128])
    total = ones_times(lower, rate, 3)
    reach = aux[:, 4:5] * jnp.exp(total)
    to_end = aux[:, 5:6] * jnp.exp(total[BLOCK - 1 : BLOCK, :] - total)
    return (raw, is_head, step, rate, total, reach, to_end)


def decay_of(total, total_rows, keep, h):
    at = STEP_LANE + h
    gap = total[:, at : at + 1] - total_rows[at : at + 1, :]
    return jnp.exp(jnp.where(keep, gap, MASKED))


def turn_halves(values, rope, back):
    up = pltpu.roll(values, 96, 1) * rope[:, 128:256]
    down = pltpu.roll(values, 32, 1) * rope[:, 256:384]
    here = values * rope[:, 0:128]
    return here - up - down if back else here + up + down


def allowed_keys(aux_ref, segrow_ref, first, count):
    query_seg = aux_ref[first : first + QUERY_BLOCK, 0:1]
    key_seg = segrow_ref[0:1, 0:count]
    shape = (QUERY_BLOCK, count)
    return (query_seg == key_seg) & (iota(shape, 1) <= iota(shape, 0) + first)


def fold(line):
    return jnp.concatenate([line[:, 128 * i : 128 * i + 128] for i in range(8)], axis=0)


def begin(pairs, sems, first=0):
    copies = [
        pltpu.make_async_copy(source, target, sems.at[first + at])
        for at, (source, target) in enumerate(pairs)
    ]
    for copy in copies:
        copy.start()
    return copies


def finish(*copies):
    for copy in copies:
        copy.wait()


def join_cores(core, own, mate, whole, sems, first):
    lead = (slice(None),) * (len(whole.shape) - 3)
    pairs = [(own, whole.at[(*lead, core)]), (mate, whole.at[(*lead, 1 - core)])]
    return begin(pairs, sems, first)


def split_cores(core, whole, keep, send, sems, first):
    lead = (slice(None),) * (len(whole.shape) - 3)
    pairs = [(whole.at[(*lead, core)], keep), (whole.at[(*lead, 1 - core)], send)]
    return begin(pairs, sems, first)


def columns(ref, first, last):
    return ref[:, :, :, first:last].reshape(WIDTH, last - first)


def mixer_forward_kernel(
    core_ref,
    p0,
    p1,
    p2,
    p3,
    p4,
    p5,
    p6,
    p7,
    own_hbm,
    mate_hbm,
    rope_hbm,
    aux_hbm,
    segrow_ref,
    par_ref,
    normed_hbm,
    mix_hbm,
    proj_hbm,
    states_hbm,
    qkv_hbm,
    lse_hbm,
    heads_hbm,
    normed_ref,
    w_ref,
    rope_ref,
    aux_ref,
    mix_ref,
    proj_ref,
    states_ref,
    qkv_ref,
    lse_ref,
    heads_ref,
    in_sems,
    out_sems,
):
    pieces = [
        (piece, normed_ref.at[core_ref[2] ^ k])
        for k, piece in enumerate((p0, p1, p2, p3, p4, p5, p6, p7))
    ]
    first_come = begin(pieces, in_sems, 0)
    first_come += join_cores(core_ref[0], own_hbm, mate_hbm, w_ref, in_sems, 8)
    come = begin([(rope_hbm, rope_ref), (aux_hbm, aux_ref)], in_sems, 10)
    finish(*first_come)
    gone = begin([(normed_ref, normed_hbm)], out_sems, 10)
    for chunk in range(4):
        rows = slice(256 * chunk, 256 * chunk + 256)
        normed = normed_ref[2 * chunk : 2 * chunk + 2].reshape(256, WIDTH)
        state = dot(normed, columns(w_ref, 0, 512))
        proj_ref[rows, CONV_AT : CONV_AT + 256] = state[:, 0:256]
        proj_ref[rows, KV_AT:CONV_AT] = state[:, 256:384]
        proj_ref[rows, QS_AT:PACKED] = state[:, 384:512]
        inner = dot(normed, columns(w_ref, 512, SENT))
        real = iota((256, 256), 1) < INNER
        gate = jnp.concatenate([inner[:, INNER:], inner[:, 0:64]], axis=1)
        proj_ref[rows, CONV_AT + 256 : GATE_AT] = jnp.where(real, inner[:, 0:256], 0.0)
        proj_ref[rows, GATE_AT:QS_AT] = jnp.where(real, gate, 0.0)
    gone += begin([(proj_ref, proj_hbm)], out_sems, 1)
    finish(*come)
    lane = iota((256, 128), 1)
    for first in range(0, TOKENS, 256):
        rows = slice(first, first + 256)
        rope = rope_ref[rows, :]
        keyval = proj_ref[rows, KV_AT:CONV_AT]
        turned = turn_halves(proj_ref[rows, QS_AT:PACKED], rope, False)
        qkv_ref[rows, 0:128] = (turned * AHDIM**-0.5).astype(BF16)
        qkv_ref[rows, 128:256] = turn_halves(keyval, rope, False).astype(BF16)
        ones = jnp.where(lane == 0, 1.0, 0.0)
        qkv_ref[rows, 256:384] = jnp.where(lane >= 64, keyval, ones).astype(BF16)
    gone += begin([(qkv_ref, qkv_hbm)], out_sems, 2)
    for first in range(0, TOKENS, QUERY_BLOCK):
        rows = slice(first, first + QUERY_BLOCK)
        count = first + QUERY_BLOCK
        scores = dot_right(qkv_ref[rows, 0:128], qkv_ref[0:count, 128:256])
        scores = jnp.where(allowed_keys(aux_ref, segrow_ref, first, count), scores, MASKED)
        top = jnp.max(scores, axis=1, keepdims=True)
        raised = jnp.exp(scores - top)
        summed = dot(raised.astype(BF16), qkv_ref[0:count, 256:384])
        total = summed[:, 0:1]
        heads_ref[rows, 128:256] = jnp.where(lane >= 64, summed / total, 0.0).astype(BF16)
        lse_ref[rows, :] = jnp.broadcast_to(top + jnp.log(total), (QUERY_BLOCK, 128))

    gone += begin([(lse_ref, lse_hbm)], out_sems, 3)

    spread, _ = head_matrices()
    causal = iota((BLOCK, BLOCK), 0) >= iota((BLOCK, BLOCK), 1)
    lower = causal.astype(BF16)

    def block_step(index, state):
        start = pl.multiple_of(index * BLOCK, BLOCK)
        rows = pl.ds(start, BLOCK)
        aux = aux_ref[rows, :]
        _, pre = conv_parts(proj_ref, par_ref, aux, start)
        conv = (pre * sigmoid(pre)).astype(BF16)
        in_map, out_map, inner = (conv[:, 0:128], conv[:, 128:256], conv[:, 256:512].astype(F32))
        _, _, step, _, total, reach, to_end = step_parts(proj_ref, par_ref, aux, lower, start)
        wide = times_ones(jnp.concatenate([step, reach, to_end], axis=0), spread)
        step_wide, reach_wide, end_wide = (wide[0:128], wide[128:256], wide[256:384])
        stepped = inner * step_wide
        keep = causal & (aux[:, 0:1] == segrow_ref[0:1, pl.ds(start, BLOCK)])
        total_rows = jnp.transpose(total)
        shared = dot_right(out_map, in_map)
        mixing = jnp.concatenate(
            [(decay_of(total, total_rows, keep, h) * shared).astype(BF16) for h in range(HEADS)],
            axis=1,
        )
        states_ref[rows, :] = state
        result = dot(mixing, per_head(stepped).astype(BF16))
        result = result + dot(out_map, state.astype(BF16)) * reach_wide
        result = result + inner * par_ref[10:11, 0:256]
        gate = proj_ref[rows, GATE_AT:QS_AT]
        gated = (result * (gate * sigmoid(gate))).astype(BF16)
        heads_ref[rows, 0:128] = gated[:, 0:128]
        heads_ref[rows, 128:256] = heads_ref[rows, 128:256] + gated[:, 128:256]
        added = dot_left(in_map, (stepped * end_wide).astype(BF16))
        return state * reach_wide[BLOCK - 1 : BLOCK, :] + added

    lax.fori_loop(0, BLOCKS, block_step, jnp.zeros((BLOCK, 256), F32), unroll=UNROLL)
    gone += begin([(states_ref, states_hbm), (heads_ref, heads_hbm)], out_sems, 4)
    w2 = columns(w_ref, SENT, WIDE)
    for chunk in range(4):
        rows = slice(256 * chunk, 256 * chunk + 256)
        mix_ref[rows, :] = dot_right(heads_ref[rows, :], w2).astype(BF16)
        gone += begin([(mix_ref.at[rows, :], mix_hbm.at[rows, :])], out_sems, 6 + chunk)
    finish(*gone)


def mixer_backward_kernel(
    core_ref,
    mixgrad_hbm,
    own_hbm,
    mate_hbm,
    qkv_hbm,
    lse_hbm,
    aux_hbm,
    rope_hbm,
    proj_hbm,
    states_hbm,
    normed_hbm,
    segrow_ref,
    par_ref,
    second_ref,
    ngrad_hbm,
    dproj_hbm,
    small_ref,
    mixgrad_ref,
    w_ref,
    qkv_ref,
    lse_ref,
    aux_ref,
    rope_ref,
    proj_ref,
    states_ref,
    normed_ref,
    mix_ref,
    dproj_ref,
    d_ref,
    dkv_ref,
    in_sems,
    out_sems,
):
    first_come = begin([(mixgrad_hbm, mixgrad_ref)], in_sems, 0)
    first_come += join_cores(core_ref[0], own_hbm, mate_hbm, w_ref, in_sems, 1)
    come = begin(
        [
            (qkv_hbm, qkv_ref),
            (lse_hbm, lse_ref),
            (aux_hbm, aux_ref),
            (rope_hbm, rope_ref),
            (proj_hbm, proj_ref),
            (states_hbm, states_ref),
            (normed_hbm, normed_ref),
        ],
        in_sems,
        3,
    )
    finish(*first_come)
    gone = []
    w2 = columns(w_ref, SENT, WIDE)
    for first in range(0, TOKENS, 256):
        rows = slice(first, first + 256)
        d_ref[rows, :] = dot(mixgrad_ref[rows, :], w2)
    lane = iota((QUERY_BLOCK, 128), 1)
    dkv_ref[...] = jnp.zeros_like(dkv_ref)
    finish(*come[0:3])
    for first in range(0, TOKENS, QUERY_BLOCK):
        rows = slice(first, first + QUERY_BLOCK)
        count = first + QUERY_BLOCK
        queries, keys = (qkv_ref[rows, 0:128], qkv_ref[0:count, 128:256])
        out_grad = jnp.where(lane >= 64, d_ref[rows, 128:256], 0.0).astype(BF16)
        scores = dot_right(queries, keys) - lse_ref[rows, 0:1]
        weights = jnp.exp(
            jnp.where(allowed_keys(aux_ref, segrow_ref, first, count), scores, MASKED)
        )
        weight_grad = dot_right(out_grad, qkv_ref[0:count, 256:384])
        mean = jnp.sum(weights * weight_grad, axis=1, keepdims=True)
        score_grad = (weights * (weight_grad - mean)).astype(BF16)
        query_grad = dot(score_grad, keys) * AHDIM**-0.5
        d_ref[rows, 128:256] = jnp.where(
            lane < 64, d_ref[rows, 128:256], pltpu.roll(query_grad, 64, 1)
        )
        dkv_ref[0:count, 0:128] += dot_left(score_grad, queries)
        dkv_ref[0:count, 128:256] += dot_left(weights.astype(BF16), out_grad)
    finish(come[3])
    for first in range(0, TOKENS, 256):
        rows = slice(first, first + 256)
        rope = rope_ref[rows, :]
        query_grad = turn_halves(pltpu.roll(d_ref[rows, 128:256], 64, 1), rope, True)
        dproj_ref[rows, 384:512] = query_grad.astype(BF16)
        key_grad = turn_halves(dkv_ref[rows, 0:128], rope, True)
        keyval_grad = jnp.where(lane < 64, key_grad, dkv_ref[rows, 128:256])
        dproj_ref[rows, 256:384] = keyval_grad.astype(BF16)

    spread, gather = head_matrices()
    row, column = (iota((BLOCK, BLOCK), 0), iota((BLOCK, BLOCK), 1))
    causal = row >= column
    lower = causal.astype(BF16)
    upper = (row <= column).astype(BF16)
    strict = (row > column).astype(BF16)
    real = iota((BLOCK, 256), 1) < INNER
    head_lane = iota((BLOCK, 128), 1)

    def block_step(turn, carried):
        state_grad, later, taps_sum, head_sum, skip_sum = carried
        start = pl.multiple_of((BLOCKS - 1 - turn) * BLOCK, BLOCK)
        rows = pl.ds(start, BLOCK)
        aux = aux_ref[rows, :]
        lagged, pre = conv_parts(proj_ref, par_ref, aux, start)
        sig = sigmoid(pre)
        conv = (pre * sig).astype(BF16)
        in_map, out_map, inner = (conv[:, 0:128], conv[:, 128:256], conv[:, 256:512].astype(F32))
        raw, is_head, step, rate, total, reach, to_end = step_parts(
            proj_ref, par_ref, aux, lower, start
        )
        wide = times_ones(jnp.concatenate([step, reach, to_end], axis=0), spread)
        step_wide, reach_wide, end_wide = (wide[0:128], wide[128:256], wide[256:384])
        stepped = inner * step_wide
        stepped_low = stepped.astype(BF16)
        keep = causal & (aux[:, 0:1] == segrow_ref[0:1, pl.ds(start, BLOCK)])
        total_rows = jnp.transpose(total)
        shared = dot_right(out_map, in_map)
        decays = [decay_of(total, total_rows, keep, h) for h in range(HEADS)]
        mixing = [(decay * shared).astype(BF16) for decay in decays]
        state = states_ref[rows, :]
        state_low = state.astype(BF16)
        incoming = dot(out_map, state_low) * reach_wide
        result = dot(jnp.concatenate(mixing, axis=1), per_head(stepped).astype(BF16)) + incoming
        result = result + inner * par_ref[10:11, 0:256]

        gate = proj_ref[rows, GATE_AT:QS_AT]
        gate_sig = sigmoid(gate)
        gated_grad = jnp.where(real, d_ref[rows, :], 0.0)
        gate_grad = gated_grad * result * (gate_sig * (1.0 + gate * (1.0 - gate_sig)))
        out_grad = gated_grad * (gate * gate_sig)
        by_head = per_head(out_grad).astype(BF16)

        mixing_grad = dot_right(by_head, stepped_low)
        shared_grad = jnp.zeros((BLOCK, BLOCK), F32)
        edges = []
        for h in range(HEADS):
            decayed = mixing_grad[h * BLOCK : (h + 1) * BLOCK] * decays[h]
            shared_grad = shared_grad + decayed
            edges.append((decayed * shared).astype(BF16))
        crossing = dot(upper, jnp.concatenate(edges, axis=1))
        rate_grad = jnp.zeros((BLOCK, 128), F32)
        for h in range(HEADS):
            part = jnp.where(row > column, crossing[:, h * BLOCK : (h + 1) * BLOCK], 0.0)
            part = jnp.sum(part, axis=1, keepdims=True)
            rate_grad = rate_grad + jnp.where(head_lane == STEP_LANE + h, part, 0.0)

        reached = (out_grad * reach_wide).astype(BF16)
        state_grad_low = state_grad.astype(BF16)
        ended = dot(in_map, state_grad_low) * end_wide
        mapped = dot_left(jnp.concatenate(mixing, axis=0), by_head) + ended
        inner_grad = mapped * step_wide + out_grad * par_ref[10:11, 0:256]
        kept = jnp.sum(state_grad * state, axis=0, keepdims=True)
        kept = jnp.broadcast_to(kept * reach_wide[BLOCK - 1 : BLOCK, :], (8, 256))
        sums = times_ones(
            jnp.concatenate([inner * mapped, out_grad * incoming, stepped * ended, kept], axis=0),
            gather,
        )
        flows = ones_times(
            jnp.concatenate([upper, strict], axis=1), sums[128:384]
        )
        rate_grad = rate_grad + flows + sums[384:385]
        step_grad = sums[0:128] - jnp.exp(par_ref[9:10, 0:128]) * rate_grad
        step_grad = jnp.where(is_head, step_grad * sigmoid(raw), 0.0)
        dproj_ref[rows, 384:512] = dproj_ref[rows, 384:512] + step_grad.astype(BF16)
        head_sum = head_sum + jnp.concatenate(
            [
                jnp.sum(jnp.where(is_head, rate_grad * rate, 0.0), axis=0, keepdims=True),
                jnp.sum(step_grad, axis=0, keepdims=True),
                jnp.zeros((6, 128), F32),
            ],
            axis=0,
        )
        skip_sum = skip_sum + jnp.sum(inner * out_grad, axis=0, keepdims=True)

        shared_low = shared_grad.astype(BF16)
        out_map_grad = dot(shared_low, in_map) + dot_right(reached, state_low)
        in_map_grad = dot_left(shared_low, out_map) + dot_right(
            (stepped * end_wide).astype(BF16), state_grad_low
        )
        conv_grad = jnp.concatenate([in_map_grad, out_map_grad, inner_grad], axis=1)
        pre_grad = conv_grad * (sig * (1.0 + pre * (1.0 - sig)))
        taps_sum = taps_sum + jnp.concatenate(
            [jnp.sum(pre_grad * lagged[lag], axis=0, keepdims=True) for lag in range(4)]
            + [jnp.zeros((4, CONV_WIDTH), F32)],
            axis=0,
        )
        both = jnp.concatenate([pre_grad, later], axis=0)
        masks = aux_ref[pl.ds(start, BLOCK + 8), :]
        u_grad = pre_grad * par_ref[0:1, :]
        for lag in range(1, 4):
            shifted = (both * masks[:, lag : lag + 1])[lag : lag + BLOCK]
            u_grad = u_grad + shifted * par_ref[lag : lag + 1, :]
        dproj_ref[rows, 0:256] = u_grad[:, 0:256].astype(BF16)
        inner = jnp.concatenate([u_grad[:, 256 : 256 + INNER], gate_grad[:, 0:INNER]], axis=1)
        dproj_ref[rows, 512:SENT] = inner.astype(BF16)
        state_grad = state_grad * reach_wide[BLOCK - 1 : BLOCK, :] + dot_left(out_map, reached)
        return (state_grad, pre_grad[0:8], taps_sum, head_sum, skip_sum)

    carried = (
        jnp.zeros((BLOCK, 256), F32),
        jnp.zeros((8, CONV_WIDTH), F32),
        jnp.zeros((8, CONV_WIDTH), F32),
        jnp.zeros((8, 128), F32),
        jnp.zeros((1, 256), F32),
    )
    finish(*come[4:6])
    _, _, taps_sum, head_sum, skip_sum = lax.fori_loop(
        0, BLOCKS, block_step, carried, unroll=UNROLL
    )
    gone += begin([(dproj_ref, dproj_hbm)], out_sems, 0)
    finish(come[6])
    gain = jnp.zeros((1, WIDTH), F32)
    w1 = columns(w_ref, 0, SENT)
    for chunk in range(4):
        rows = slice(256 * chunk, 256 * chunk + 256)
        grad = dot_right(dproj_ref[rows, :], w1)
        mix_ref[rows, :] = grad.astype(BF16)
        gone += begin([(mix_ref.at[rows, :], ngrad_hbm.at[rows, :])], out_sems, 1 + chunk)
        normed = normed_ref[2 * chunk : 2 * chunk + 2].reshape(256, WIDTH)
        gain = gain + jnp.sum(grad * normed.astype(F32), axis=0, keepdims=True)
    upper_rows = jnp.concatenate([taps_sum[0:4, 0:256], taps_sum[0:4, 256:512]], axis=0)
    upper_rows = jnp.concatenate([upper_rows, fold(gain)], axis=1)
    skip_rows = jnp.concatenate([skip_sum, jnp.zeros((7, 256), F32)], axis=0)
    lower_rows = jnp.concatenate([fold(second_ref[0:1, :]), head_sum[:, 64:128], skip_rows[:, 0:INNER]], axis=1)
    small = jnp.concatenate([upper_rows, lower_rows], axis=0)
    small_ref[...] = small
    finish(*gone)


def feed_kernel(
    core_ref, n0, n1, n2, n3, c0, c1, c2, c3, own_hbm, mate_hbm,
    o0, o1, o2, o3, g0, g1, g2, g3, act_ref, grads_ref, gain_ref, w_ref, sems,
):
    finish(*join_cores(core_ref[0], own_hbm, mate_hbm, w_ref, sems, 0))
    inputs = ((n0, n1, c0, c1), (n2, n3, c2, c3))
    outs = (((o0, g0), (o1, g1)), ((o2, g2), (o3, g3)))
    gain = jnp.zeros((1, WIDTH), F32)
    for j in range(2):
        rows = slice(256 * j, 256 * j + 256)
        normed = jnp.concatenate([inputs[j][0][...], inputs[j][1][...]], axis=0)
        cot = jnp.concatenate([inputs[j][2][...], inputs[j][3][...]], axis=0)
        out_sum, grad_sum = (0.0, 0.0)
        for h in range(2):
            up_weights = columns(w_ref.at[h], 0, 512)
            down = columns(w_ref.at[h], 512, 768)
            both = dot(normed, up_weights)
            gate, up = (both[:, 0:FEED], both[:, FEED:])
            sig = sigmoid(gate)
            silu = gate * sig
            act = (silu * up).astype(BF16)
            act_ref[rows, h * FEED : (h + 1) * FEED] = act
            out_sum = out_sum + dot_right(act, down)
            act_grad = dot(cot, down)
            gate_grad = (act_grad * up * (sig + silu * (1.0 - sig))).astype(BF16)
            up_grad = (act_grad * silu).astype(BF16)
            grads = jnp.concatenate([gate_grad, up_grad], axis=1)
            grads_ref[rows, h * 512 : (h + 1) * 512] = grads
            grad_sum = grad_sum + dot_right(grads, up_weights)
        gain = gain + jnp.sum(grad_sum * normed.astype(F32), axis=0, keepdims=True)
        out_low, grad_low = (out_sum.astype(BF16), grad_sum.astype(BF16))
        for half in range(2):
            part = slice(half * BLOCK, (half + 1) * BLOCK)
            outs[j][half][0][...] = out_low[part]
            outs[j][half][1][...] = grad_low[part]
    gain_ref[...] = jnp.broadcast_to(gain, (8, WIDTH))


def feed_weights_kernel(
    core_ref, n0, n1, n2, n3, c0, c1, c2, c3, act_ref, grads_ref, keep_hbm, send_hbm, out_ref, sems
):
    normed = jnp.concatenate([r[...] for r in (n0, n1, n2, n3)], axis=0)
    cot = jnp.concatenate([r[...] for r in (c0, c1, c2, c3)], axis=0)
    up = dot_left(normed, grads_ref[...]).astype(BF16)
    down = dot_left(cot, act_ref[...]).astype(BF16)
    for h in range(2):
        up_here = up[:, h * 512 : (h + 1) * 512].reshape(8, 2, 64, 512)
        down_here = down[:, h * FEED : (h + 1) * FEED].reshape(8, 2, 64, FEED)
        out_ref[h, :, :, :, 0:512] = up_here
        out_ref[h, :, :, :, 512:768] = down_here
    finish(*split_cores(core_ref[0], out_ref, keep_hbm, send_hbm, sems, 0))


def mixer_weights_kernel(
    core_ref, normed_ref, dproj_ref, mixgrad_ref, heads_ref, keep_hbm, send_hbm, out_ref, sems
):
    normed = normed_ref[...].reshape(TOKENS, WIDTH)
    for first, last in ((0, 512), (512, SENT)):
        grad = dot_left(normed, dproj_ref[:, first:last]).astype(BF16)
        out_ref[:, :, :, first:last] = grad.reshape(8, 2, 64, last - first)
    grad = dot_left(mixgrad_ref[...], heads_ref[...]).astype(BF16)
    out_ref[:, :, :, SENT:WIDE] = grad.reshape(8, 2, 64, WIDE - SENT)
    finish(*split_cores(core_ref[0], out_ref, keep_hbm, send_hbm, sems, 0))


def mixer_pair_kernel(keep_ref, come_ref, small_ref, small_come_ref, out_ref):
    total = keep_ref[...].astype(F32) + come_ref[...].astype(F32)
    small = small_ref[...] + small_come_ref[...]
    high = small.astype(BF16)
    low = (small - high.astype(F32)).astype(BF16)
    tail = jnp.concatenate([high, low, jnp.zeros_like(high)], axis=1)
    for i in range(8):
        out_ref[i, 0:64, :] = total[i].astype(BF16)
        out_ref[i, 64:, :] = tail


def feed_pair_kernel(keep_ref, come_ref, out_ref):
    out_ref[...] = (keep_ref[...].astype(F32) + come_ref[...].astype(F32)).astype(BF16)


def collect_kernel(
    core_ref, blocks_ref, lines_ref, gate_ref, input_ref, step_ref, query_ref, mamba_ref, attend_ref,
    own_ref,
):
    total = total_rows(blocks_ref)
    own = total[64:, 0:EARLY] + total[64:, EARLY : 2 * EARLY]
    total = total[0:64]
    keyval = total[:, 256:384]
    turned = pltpu.roll(keyval, AHDIM, 1)
    low = iota(keyval.shape, 1) < AHDIM
    first = core_ref[1] == 0
    keys = jnp.where(first, jnp.where(low, keyval, 0.0), jnp.where(low, 0.0, turned))
    values = jnp.where(first, jnp.where(low, turned, 0.0), jnp.where(low, 0.0, keyval))
    shared = jnp.concatenate([total[:, 0:256], keys, values], axis=1)
    for t in range(8):
        lines_ref[t, 0:8, :] = shared[8 * t : 8 * t + 8]
        lines_ref[t, 8:24, 0:EARLY] = own
        lines_ref[t, 8:24, EARLY:] = jnp.zeros((16, 512 - EARLY), F32)
    own_ref[...] = own
    query_ref[...] = total[:, EARLY : EARLY + AHDIM]
    step_ref[...] = total[:, EARLY + STEP_LANE : EARLY + STEP_LANE + HEADS]
    input_ref[...] = total[:, 512 : 512 + INNER]
    gate_ref[...] = total[:, 512 + INNER : SENT]
    turned = jnp.transpose(total[:, SENT:WIDE])
    mamba_ref[...] = turned[0:INNER]
    attend_ref[...] = turned[INNER:]


def last_kernel(
    lines_ref, gain_one_ref, gain_two_ref, state_ref, keyval_ref, taps_ref, first_ref, second_ref
):
    pairs = [lines_ref[2 * t] + lines_ref[2 * t + 1] for t in range(4)]
    total = (pairs[0] + pairs[1]) + (pairs[2] + pairs[3])
    state_ref[...] = total[0:8, 0:256]
    keyval_ref[...] = total[0:8, 256:512]
    taps_ref[...] = total[8:12, 0:256]
    first_ref[...] = total[8:16, 256:384] / gain_one_ref[...]
    second_ref[...] = total[16:24, 0:128] / gain_two_ref[...]


def total_of(pieces):
    return sum(piece[...].astype(F32) for piece in pieces)


def total_rows(blocks_ref):
    return sum(blocks_ref[i].astype(F32) for i in range(8))


def row_norm(values):
    return lax.rsqrt(jnp.mean(values * values, axis=-1, keepdims=True) + NORM_EPS)


def norm_back(values, gain, grad):
    scale = row_norm(values)
    scaled = grad * gain
    return scale * scaled - values * (
        scale**3 * jnp.mean(scaled * values, axis=-1, keepdims=True)
    )


def first_norm_kernel(x_ref, gain_ref, feed_ref, normed_ref, copies_ref):
    x = x_ref[...].astype(F32)
    normed_ref[...] = (x * row_norm(x) * gain_ref[...]).astype(BF16)
    for i in range(16):
        copies_ref[i] = feed_ref[...]


def second_norm_kernel(x_ref, gain_ref, blocks_ref, hidden_ref, normed_ref):
    hidden = x_ref[...].astype(F32) + total_rows(blocks_ref)
    hidden_ref[...] = hidden
    normed_ref[...] = (hidden * row_norm(hidden) * gain_ref[...]).astype(BF16)


def hidden_grad_kernel(hidden_ref, gain_ref, cot_ref, s0, s1, s2, s3, grad_ref, low_ref):
    back = norm_back(hidden_ref[...], gain_ref[...], total_of((s0, s1, s2, s3)))
    grad = cot_ref[...].astype(F32) + back
    grad_ref[...] = grad
    low = grad.astype(BF16)
    for i in range(8):
        low_ref[i] = low


def input_grad_kernel(x_ref, gain_ref, hidden_grad_ref, blocks_ref, grad_ref):
    x = x_ref[...].astype(F32)
    back = norm_back(x, gain_ref[...], total_rows(blocks_ref))
    grad_ref[...] = hidden_grad_ref[...] + back


def output_kernel(hidden_ref, s0, s1, s2, s3, out_ref):
    out_ref[...] = (hidden_ref[...] + total_of((s0, s1, s2, s3))).astype(BF16)


def like(dtype, *shape):
    return jax.ShapeDtypeStruct(shape, dtype)


VMEM = pl.BlockSpec(memory_space=pltpu.VMEM)
SMEM = pl.BlockSpec(memory_space=pltpu.SMEM)
ANY = pl.BlockSpec(memory_space=pl.ANY)


def run(kernel, name, outs, args, specs=None, scratch=(), us=0.05, out_specs=None):
    return pl.pallas_call(
        kernel,
        in_specs=specs or [VMEM] * len(args),
        out_specs=out_specs or [VMEM] * len(outs),
        out_shape=list(outs),
        scratch_shapes=list(scratch),
        compiler_params=pltpu.CompilerParams(vmem_limit_bytes=VMEM_BYTES),
        cost_estimate=pl.CostEstimate(
            flops=int(us * 1e9), transcendentals=0, bytes_accessed=int(us * 2e6)
        ),
        name=name,
    )(*args)


def held(array):
    return pltpu.VMEM(array.shape, array.dtype)


HERE = (BLOCK, WIDTH)
UNROLL = 4
FORWARD_US = 20
BACKWARD_US = 33
ROW = (8, BLOCK, WIDTH)


def mixer_forward(core, pieces, own, mate, aux, segrow, pack, rope):
    outs = (
        like(BF16, *ROW),
        like(BF16, TOKENS, WIDTH),
        like(F32, TOKENS, PACKED),
        like(F32, TOKENS, 256),
        like(BF16, TOKENS, 384),
        like(F32, TOKENS, 128),
        like(BF16, TOKENS, 256),
    )
    return run(
        mixer_forward_kernel,
        "mixer_forward",
        outs,
        (core, *pieces, own, mate, rope, aux, segrow, pack),
        [SMEM] + [ANY] * 12 + [VMEM] * 2,
        [pltpu.VMEM(ROW, BF16), pltpu.VMEM((8, 2, 64, WIDE), BF16), held(rope), held(aux)]
        + [held(a) for a in outs[1:]]
        + [pltpu.SemaphoreType.DMA((n,)) for n in (12, 11)],
        FORWARD_US,
        [ANY] * 7,
    )


def mixer_backward(
    core, mix_grad, own, mate, normed, aux, segrow, pack, rope, proj, states, qkv, lse, second
):
    outs = (like(BF16, TOKENS, WIDTH), like(BF16, TOKENS, SENT), like(F32, 16, EARLY))
    moved = (qkv, lse, aux, rope, proj, states)
    return run(
        mixer_backward_kernel,
        "mixer_backward",
        outs,
        (core, mix_grad, own, mate, *moved, normed, segrow, pack, second),
        [SMEM] + [ANY] * 10 + [VMEM] * 3,
        [held(mix_grad), pltpu.VMEM((8, 2, 64, WIDE), BF16)]
        + [held(a) for a in moved]
        + [pltpu.VMEM(ROW, BF16)]
        + [held(a) for a in outs[0:2]]
        + [pltpu.VMEM((TOKENS, 256), F32), pltpu.VMEM((TOKENS, 256), F32)]
        + [pltpu.SemaphoreType.DMA((n,)) for n in (10, 5)],
        BACKWARD_US,
        [ANY] * 2 + [VMEM],
    )


def feed_forward_backward(core, normed, cot, weights):
    return run(
        feed_kernel,
        "feed",
        [like(BF16, *HERE)] * 8
        + [like(BF16, 512, 2 * FEED), like(BF16, 512, 4 * FEED), like(F32, 8, WIDTH)],
        (core, *normed, *cot, *weights),
        [SMEM] + [VMEM] * 8 + [ANY] * 2,
        [pltpu.VMEM((2, 8, 2, 64, 768), BF16), pltpu.SemaphoreType.DMA((2,))],
    )


def aux_arrays(seg):
    columns = [seg]
    for lag in range(1, 4):
        earlier = jnp.concatenate([jnp.full((lag,), -1.0, F32), seg[: TOKENS - lag]])
        columns.append((earlier == seg).astype(F32))
    ends = seg.reshape(BLOCKS, BLOCK)[:, -1]
    before = jnp.concatenate([jnp.full((1,), -1.0, F32), ends[:-1]])
    columns.append((seg == jnp.repeat(before, BLOCK)).astype(F32))
    columns.append((seg == jnp.repeat(ends, BLOCK)).astype(F32))
    aux = jnp.pad(jnp.stack(columns, axis=1), ((0, 8), (0, 128 - len(columns))))
    return (aux, jnp.broadcast_to(seg, (8, TOKENS)))


def rope_arrays():
    half = AHDIM // 2
    freq = (ROPE_BASE ** (-2.0 * np.arange(half) / AHDIM)).astype(np.float32)
    angles = np.arange(TOKENS, dtype=np.float32)[:, None] * freq[None, :]
    cosine, sine = (np.cos(angles.astype(np.float64)), np.sin(angles.astype(np.float64)))
    none = np.zeros_like(sine)
    parts = [cosine, cosine, none, none, -sine, none, none, none, none, sine, none, none]
    return jnp.asarray(np.concatenate(parts, axis=1).astype(np.float32))


def pad_columns(values, width, before=0):
    return jnp.pad(values, ((0, 0), (before, width - before - values.shape[1])))


def index_of(axes):
    return lax.axis_index(axes)


def exchange(values, axes, turn):
    size = 2 ** len(axes)
    return lax.ppermute(values, axes, [(i, turn(i)) for i in range(size)])


def other_core(values):
    return exchange(values, ("c",), lambda i: i ^ 1)


def near_gather(shard):
    return [shard] + near_return([shard] * 4)


def near_return(pieces):
    return [exchange(pieces[j], NEAR, lambda i, j=j: i ^ j) for j in range(1, 4)]


def spread_blocks(shard, axes):
    copies = jnp.broadcast_to(shard, (2 ** len(axes), *shard.shape))
    return turn_blocks(copies, axes)


def turn_blocks(blocks, axes):
    return lax.all_to_all(blocks, axes, split_axis=0, concat_axis=0, tiled=True)


def sum_blocks(blocks):
    return jnp.sum(blocks.astype(F32), axis=0)


def body(
    block_input,
    segments,
    first_gain,
    mamba_gate,
    mamba_input,
    step_weight,
    state_weight,
    conv_inner,
    conv_state,
    decay_log,
    step_bias,
    skip_scale,
    query_weight,
    keyval_weight,
    mamba_out,
    attention_out,
    second_gain,
    feed_gate,
    feed_up,
    feed_down,
    cotangent,
):
    kv_head = lax.axis_index("yh")
    core = jnp.stack([lax.axis_index("c"), kv_head, lax.axis_index(TENSOR)]).astype(jnp.int32)
    x, cot = (block_input[0], cotangent[0])
    gain_one, gain_two = (first_gain[None], second_gain[None])
    shared = spread_blocks(jnp.concatenate([state_weight, keyval_weight], axis=1), TENSOR)
    shared = shared.reshape(-1, 512)
    feed_here = jnp.concatenate([feed_gate, feed_up, feed_down.T], axis=1)
    normed_here, feed_copies = run(
        first_norm_kernel,
        "first_norm",
        [like(BF16, *HERE), like(BF16, 16, *feed_here.shape)],
        (x, gain_one, feed_here),
    )
    normed_pieces = [normed_here] + [
        exchange(normed_here, TENSOR, lambda i, k=k: i ^ k) for k in range(1, 8)
    ]
    shared, _ = lax.optimization_barrier((shared, normed_here))
    pack = jnp.concatenate(
        [
            jnp.concatenate([conv_state, pad_columns(conv_inner, 256)], axis=1),
            jnp.zeros((4, 512), F32),
            pad_columns(step_bias[None], 512, STEP_LANE),
            pad_columns(decay_log[None], 512, STEP_LANE),
            pad_columns(jnp.repeat(skip_scale, HDIM)[None], 512),
            jnp.zeros((5, 512), F32),
        ],
        axis=0,
    )
    aux, segrow = aux_arrays(segments.reshape(TOKENS).astype(F32))
    rope = rope_arrays()

    share_rows = shared.shape[0]
    key_part = lax.dynamic_slice(shared, (0, 256 + kv_head * AHDIM), (share_rows, AHDIM))
    value_part = lax.dynamic_slice(
        shared, (0, 256 + (KVHEADS + kv_head) * AHDIM), (share_rows, AHDIM)
    )
    main_here = jnp.concatenate(
        [
            shared[:, 0:256],
            key_part,
            value_part,
            query_weight,
            pad_columns(step_weight, 64),
            mamba_input,
            mamba_gate,
            mamba_out.T,
            attention_out.T,
        ],
        axis=1,
    )
    own = spread_blocks(main_here, CHIPS)
    mate = other_core(own)

    own, feed_copies, aux, segrow, pack = lax.optimization_barrier(
        (own, feed_copies, aux, segrow, pack)
    )
    feed_own = turn_blocks(feed_copies, FEED16).reshape(2, 8, share_rows, 768)

    normed, mix, proj, states, qkv, lse, heads = mixer_forward(
        core, normed_pieces, own, mate, aux, segrow, pack, rope
    )
    mix, feed_own, cot_here = lax.optimization_barrier((mix, feed_own, cot))
    feed_weights = (feed_own, other_core(feed_own))
    mix_blocks, *cot_pieces = lax.optimization_barrier(
        (turn_blocks(mix.reshape(ROW), TENSOR), *near_gather(cot_here))
    )
    hidden, normed_two_here = run(
        second_norm_kernel,
        "second_norm",
        [like(F32, *HERE), like(BF16, *HERE)],
        (x, gain_two, mix_blocks),
    )
    normed_two = near_gather(normed_two_here)
    *parts, act, feed_grads, second_part = feed_forward_backward(
        core, normed_two, cot_pieces, feed_weights
    )
    feed_keep, feed_send = run(
        feed_weights_kernel,
        "feed_weights",
        [like(BF16, 2, 8, share_rows, 768)] * 2,
        (core, *normed_two, *cot_pieces, act, feed_grads),
        [SMEM] + [VMEM] * 10,
        [pltpu.VMEM((2, 8, 2, 64, 768), BF16), pltpu.SemaphoreType.DMA((2,))],
        out_specs=[ANY] * 2,
    )
    sums = near_return(parts[4:8])
    hidden, feed_keep, feed_send, *sums = lax.optimization_barrier(
        (hidden, feed_keep, feed_send, *sums)
    )
    hidden_grad, mix_grad_copies = run(
        hidden_grad_kernel,
        "hidden_grad",
        [like(F32, *HERE), like(BF16, *ROW)],
        (hidden, gain_two, cot, parts[4], *sums),
    )
    (feed_pair,) = run(
        feed_pair_kernel,
        "feed_pair",
        [like(BF16, 2, 8, share_rows, 768)],
        (feed_keep, other_core(feed_send)),
    )
    mix_grad = turn_blocks(mix_grad_copies, TENSOR).reshape(TOKENS, WIDTH)
    feed_pair, mix_grad = lax.optimization_barrier((feed_pair, mix_grad))
    feed_blocks = turn_blocks(feed_pair.reshape(16, share_rows, 768), FEED16)

    normed_grad, dproj, small = mixer_backward(
        core, mix_grad, own, mate, normed, aux, segrow, pack, rope, proj, states, qkv, lse,
        second_part,
    )
    normed_grad, feed_blocks, *out_sums = lax.optimization_barrier(
        (normed_grad, feed_blocks, *near_return(parts[0:4]))
    )
    input_blocks = turn_blocks(normed_grad.reshape(ROW), TENSOR)
    keep, send = run(
        mixer_weights_kernel,
        "mixer_weights",
        [like(BF16, 8, share_rows, WIDE)] * 2,
        (core, normed, dproj, mix_grad, heads),
        [SMEM] + [VMEM] * 4,
        [pltpu.VMEM((8, 2, 64, WIDE), BF16), pltpu.SemaphoreType.DMA((2,))],
        out_specs=[ANY] * 2,
    )
    (pair,) = run(
        mixer_pair_kernel,
        "mixer_pair",
        [like(BF16, 8, share_rows + 16, WIDE)],
        (keep, other_core(send), small, other_core(small)),
    )
    pair, input_blocks = lax.optimization_barrier((pair, input_blocks))
    (block_out,) = run(
        output_kernel, "output", [like(BF16, *HERE)], (hidden, parts[0], *out_sums)
    )
    blocks = turn_blocks(pair, CHIPS)
    (input_grad,) = run(
        input_grad_kernel,
        "input_grad",
        [like(F32, *HERE)],
        (x, gain_one, hidden_grad, input_blocks),
    )
    feed_total = sum_blocks(feed_blocks)
    feed_outs = (feed_total[:, 0:256], feed_total[:, 256:512], feed_total[:, 512:768].T)
    blocks, input_grad, block_out, *feed_outs = lax.optimization_barrier(
        (blocks, input_grad, block_out, *feed_outs)
    )
    lines, gate_sum, input_sum, step_sum, query_sum, mamba_sum, attend_sum, own = run(
        collect_kernel,
        "collect",
        [
            like(F32, 8, 24, 512),
            like(F32, share_rows, INNER),
            like(F32, share_rows, INNER),
            like(F32, share_rows, HEADS),
            like(F32, share_rows, AHDIM),
            like(F32, INNER, share_rows),
            like(F32, AHDIM, share_rows),
            like(F32, 16, EARLY),
        ],
        (core, blocks),
        [SMEM, VMEM],
    )
    state_sum, keyval_sum, state_taps, first_sum, second_sum = run(
        last_kernel,
        "last",
        [
            like(F32, 8, 256),
            like(F32, 8, 256),
            like(F32, 4, 256),
            like(F32, 8, 128),
            like(F32, 8, 128),
        ],
        (turn_blocks(lines, TENSOR), first_gain.reshape(8, 128), second_gain.reshape(8, 128)),
    )
    return (
        block_out[None],
        input_grad[None],
        first_sum.reshape(-1),
        gate_sum,
        input_sum,
        step_sum,
        state_sum,
        own[4:8, 0:INNER],
        state_taps,
        own[8, 128 : 128 + HEADS],
        own[9, 128 : 128 + HEADS],
        jnp.sum(own[8, INNER : 2 * INNER].reshape(HEADS, HDIM), axis=1),
        query_sum,
        keyval_sum,
        mamba_sum,
        attend_sum,
        second_sum.reshape(-1),
        *feed_outs,
    )


def solution(mesh):
    DP, TP = (("zlo", "xh", "xl", "c"), ("yh", "yl", "zhi"))
    fine = jax.sharding.Mesh(mesh.devices.reshape(FINE_SIZES), (*DP, *TP))
    in_specs = (
        P(DP, TP, None),
        P(DP, None),
        P(),
        P(DP, TP),
        P(DP, TP),
        P(DP, TP),
        P((*DP, *TP), None),
        P(None, TP),
        P(),
        P(TP),
        P(TP),
        P(TP),
        P(DP, TP),
        P((*DP, *TP), None),
        P(TP, DP),
        P(TP, DP),
        P(),
        P(DP, TP),
        P(DP, TP),
        P(TP, DP),
        P(DP, TP, None),
    )
    out_specs = (
        P(DP, TP, None),
        P(DP, TP, None),
        P(),
        P(DP, TP),
        P(DP, TP),
        P(DP, TP),
        P((*DP, *TP), None),
        P(None, TP),
        P(),
        P(TP),
        P(TP),
        P(TP),
        P(DP, TP),
        P((*DP, *TP), None),
        P(TP, DP),
        P(TP, DP),
        P(),
        P(DP, TP),
        P(DP, TP),
        P(TP, DP),
    )
    return jax.shard_map(body, mesh=fine, in_specs=in_specs, out_specs=out_specs, check_vma=False)
```
